128 devices in a mesh: rows: 16 (over z, y), seq: 8 (over x, core).
Axes of the slice: x: 4, y: 4, z: 4, core: 2. Of those that a mesh axis runs over, the one named last changes fastest.
Arguments:
- inputs: bfloat16 [16, 8192, 512], P('rows', 'seq'), may hold values from -6 to 6
- qkv_weight: bfloat16 [512, 1536], replicated, may hold values from -0.25 to 0.25
- out_weight: bfloat16 [512, 512], replicated, may hold values from -2 to 2
- up_weight: bfloat16 [512, 2048], replicated, may hold values from -0.25 to 0.25
- down_weight: bfloat16 [2048, 512], replicated, may hold values from -0.125 to 0.125
- norm1_gain: float32 [512], replicated, may hold values from 0.1 to 1.9
- norm1_shift: float32 [512], replicated, may hold values from -3 to 3
- norm2_gain: float32 [512], replicated, may hold values from 0.1 to 1.9
- norm2_shift: float32 [512], replicated, may hold values from -3 to 3
- segment_ids: int32 [16, 8192], P('rows'), may hold values from 0 to 64, never falling along the last dimension, each value on 1 to 250 neighbouring positions
- item_steps: int32 [16, 65], P('rows'), may hold values from 0 to 249
- gen_rank: int32 [16, 8192], P('rows', 'seq'), may hold values from 0 to 249
- out_grad: bfloat16 [16, 8192, 512], P('rows', 'seq'), may hold values from -6 to 6
Outputs:
- output: bfloat16 [16, 8192, 512], P('rows', 'seq')
- input_grad: float32 [16, 8192, 512], P('rows', 'seq')
- grad_qkv_weight: float32 [512, 1536], replicated
- grad_out_weight: float32 [512, 512], replicated
- grad_up_weight: float32 [512, 2048], replicated
- grad_down_weight: float32 [2048, 512], replicated
- grad_norm1_gain: float32 [512], replicated
- grad_norm1_shift: float32 [512], replicated
- grad_norm2_gain: float32 [512], replicated
- grad_norm2_shift: float32 [512], replicated
The draws below stay inside these ranges and needn't reach their ends.
All inputs are finite; a program needn't handle non-finite values.
Results may differ from the reference program's by a relative error of at most 0.011.
Values may be sent and summed in bfloat16 or wider, within the bound.
No kernel may reach another device: no remote copies, remote signals or barrier semaphores. Data moves between devices by JAX's collectives and lax.ppermute only.
A program may use at most 128 MiB of HBM per device.

```python
import math
import jax
import jax.numpy as jnp
import numpy as np
from jax import lax

D = 512
HEADS = 8
FF = 2048
HEAD_DIM = 64
ITEM = 250
LEN = 8192
ROWS = 16
SEGS = 65


def with_ends(drawn, key, least, largest):
    spot = [jax.random.randint(jax.random.fold_in(key, axis), (), 0, length) for axis, length in enumerate(drawn.shape)]
    longest = drawn.shape.index(max(drawn.shape))
    neighbour = spot[:longest] + [(spot[longest] + 1) % drawn.shape[longest]] + spot[longest + 1:]
    return drawn.at[tuple(spot)].set(least).at[tuple(neighbour)].set(largest)


def steps_of(key, extent, cuts, smallest, largest):
    level, own = 1.0, jax.random.fold_in(key, 6)
    for axis_at, blocks in cuts:
        steps = jnp.exp(jax.random.uniform(jax.random.fold_in(own, axis_at), (blocks,), jnp.float32, smallest / len(cuts), largest / len(cuts)))
        level = level * jnp.repeat(steps, extent[axis_at] // blocks).reshape([-1 if axis == axis_at else 1 for axis in range(len(extent))])
    return level


def rank_table(count, skew):
    loads = [(1 << 20) // math.isqrt(grade ** skew) + 1 for grade in range(1, count + 1)]
    scale = 1 + sum(loads) // (1 << 30)
    return np.cumsum(np.array([max(1, weight // scale) for weight in loads]))


def ranked_ids(own_key, shape, amount, skew):
    table = rank_table(amount, skew)
    lot = jax.random.randint(jax.random.fold_in(own_key, 1), shape, 0, int(table[amount - 1]))
    grade = jnp.searchsorted(jnp.asarray(table, jnp.int32), lot, side="right")
    return jax.random.permutation(jax.random.fold_in(own_key, 2), amount)[grade].astype(jnp.int32)


def profile(number_of, total, reach, lean):
    portions = [(1 << 20) // math.isqrt(grade ** lean) + 1 for grade in range(2, number_of + 1)]
    rest, given = total - reach - (number_of - 1), [1] * (number_of - 1)
    while rest > 0:
        movable = [i for i in range(number_of - 1) if given[i] < reach]
        pool, budget = sum([portions[i] for i in movable]), rest
        for i in movable:
            more = min(reach - given[i], max(1, budget * portions[i] // pool), rest)
            given[i] = given[i] + more
            rest = rest - more
    return np.array([reach] + given)


def uneven_parts(key, number_of, total, most, slope):
    if number_of == 2:
        one = jax.random.randint(key, (), max(1, total - most), min(most, total - 1) + 1)
        return jnp.stack([one, total - one])
    tallies = jnp.asarray(profile(number_of, total, most, slope), jnp.int32)
    pairs = (number_of - 1) // 2
    giver, receiver = tallies[1:1 + 2 * pairs:2], tallies[2:2 + 2 * pairs:2]
    margin = jnp.minimum(giver - 1, most - receiver)
    shifted = jax.random.randint(jax.random.fold_in(key, 1), (pairs,), 0, 1 << 20) % (margin + 1)
    tallies = tallies.at[1:1 + 2 * pairs:2].set(giver - shifted).at[2:2 + 2 * pairs:2].set(receiver + shifted)
    return tallies[jax.random.permutation(jax.random.fold_in(key, 2), number_of)]


def gaussian(stream_key, dims, scale, most, shards=(), kind=jnp.bfloat16):
    level = steps_of(stream_key, dims, shards, -0.22, 0.18) if shards else 1.0
    array = jax.random.normal(stream_key, dims, jnp.float32) * scale * level
    return jnp.minimum(jnp.maximum(array, -most), most).astype(kind)


def setup_inputs(seed: int = 0) -> dict:
    arg_keys = jax.random.split(jax.random.key(seed), 14)
    return {
        "inputs": gaussian(arg_keys[0], (ROWS, LEN, D), 1.0, 6.0, ((0, 16), (1, 8))),
        "qkv_weight": gaussian(arg_keys[1], (D, 3 * D), D ** -0.5, 0.25),
        "out_weight": gaussian(arg_keys[2], (D, D), (D // 64) ** -0.5, 2.0),
        "up_weight": gaussian(arg_keys[3], (D, FF), D ** -0.5, 0.25),
        "down_weight": gaussian(arg_keys[4], (FF, D), FF ** -0.5, 0.125),
        "norm1_gain": jnp.clip(1.0 + 0.18 * jax.random.normal(arg_keys[5], (D,), jnp.float32), 0.1, 1.9),
        "norm1_shift": gaussian(arg_keys[6], (D,), 0.5, 3.0, (), jnp.float32),
        "norm2_gain": jnp.clip(1.0 + 0.18 * jax.random.normal(arg_keys[7], (D,), jnp.float32), 0.1, 1.9),
        "norm2_shift": gaussian(arg_keys[8], (D,), 0.5, 3.0, (), jnp.float32),
        "segment_ids": jax.vmap(lambda own: jnp.searchsorted(jnp.cumsum(uneven_parts(own, SEGS, LEN, ITEM, 2)), jnp.arange(LEN), side="right"))(jax.random.split(arg_keys[9], ROWS)).reshape((ROWS, LEN)).astype(jnp.int32),
        "item_steps": with_ends(ranked_ids(arg_keys[10], (ROWS, SEGS), ITEM, 2), jax.random.fold_in(arg_keys[10], 3), 0, ITEM - 1).astype(jnp.int32),
        "gen_rank": with_ends(jax.random.randint(arg_keys[11], (ROWS, LEN), 0, ITEM), jax.random.fold_in(arg_keys[11], 1), 0, ITEM - 1).astype(jnp.int32),
        "out_grad": gaussian(arg_keys[12], (ROWS, LEN, D), 1.0, 6.0, ((0, 16), (1, 8))),
    }


@jax.custom_vjp
def low(v):
    return lax.optimization_barrier(v.astype(jnp.bfloat16)).astype(jnp.float32)

@jax.custom_vjp
def low_back(v):
    return v

def low_keep(v):
    return (low(v), None)

def low_pass(kept, grad):
    return (grad,)

def back_keep(v):
    return (v, None)

def back_low(kept, grad):
    return (low(grad),)
low.defvjp(low_keep, low_pass)
low_back.defvjp(back_keep, back_low)
EPS = 1e-05
HIGH = lax.Precision.HIGHEST

def layer_norm(value, gain, shift):
    center = lax.optimization_barrier(jnp.mean(value, axis=-1, keepdims=True))
    centred = value - center
    spread = lax.optimization_barrier(jnp.mean(centred * centred, axis=-1, keepdims=True))
    return centred * lax.rsqrt(spread + EPS) * gain + shift

def attend(queries, key_rows, value_rows, segment_row):
    length = queries.shape[0]
    block = math.gcd(512, length)
    block_count = length // block
    query_blocks = queries.reshape(block_count, block, HEADS, HEAD_DIM)
    segment_blocks = segment_row.reshape(block_count, block)
    factor = 1.0 / math.sqrt(HEAD_DIM)

    def one_block(pair):
        query_block, segment_block = pair
        raw = jnp.einsum('qhd,khd->hqk', query_block, key_rows, precision=HIGH) * factor
        scores = low_back(raw)
        same_item = segment_block[:, None] == segment_row[None, :]
        scores = jnp.where(same_item[None], scores, -1e+30)
        highest = lax.optimization_barrier(jnp.max(scores, axis=-1, keepdims=True))
        weights = jnp.exp(scores - highest)
        probs = weights / lax.optimization_barrier(jnp.sum(weights, axis=-1, keepdims=True))
        return jnp.einsum('hqk,khd->qhd', low(probs), value_rows, precision=HIGH)
    attended = lax.map(jax.checkpoint(one_block), (query_blocks, segment_blocks))
    return attended.reshape(length, HEADS * HEAD_DIM)

def forward_row(row_input, qkv_weight, out_weight, up_weight, down_weight, norm1_gain, norm1_shift, norm2_gain, norm2_shift, segment_row):
    length = row_input.shape[0]
    normed1 = low(layer_norm(row_input, norm1_gain, norm1_shift))
    qkv = low(low_back(jnp.dot(normed1, qkv_weight, precision=HIGH)))
    queries = qkv[:, :D].reshape(length, HEADS, HEAD_DIM)
    key_rows = qkv[:, D:2 * D].reshape(length, HEADS, HEAD_DIM)
    value_rows = qkv[:, 2 * D:].reshape(length, HEADS, HEAD_DIM)
    attended = low(low_back(attend(queries, key_rows, value_rows, segment_row)))
    mid = row_input + low_back(jnp.dot(attended, out_weight, precision=HIGH))
    normed2 = low(layer_norm(mid, norm2_gain, norm2_shift))
    pre = low_back(jnp.dot(normed2, up_weight, precision=HIGH))
    act = low(jax.nn.gelu(pre))
    return mid + jnp.dot(act, down_weight, precision=HIGH)

def reference(inputs, qkv_weight, out_weight, up_weight, down_weight, norm1_gain, norm1_shift, norm2_gain, norm2_shift, segment_ids, item_steps, gen_rank, out_grad):
    params = (qkv_weight.astype(jnp.float32), out_weight.astype(jnp.float32), up_weight.astype(jnp.float32), down_weight.astype(jnp.float32), norm1_gain.astype(jnp.float32), norm1_shift.astype(jnp.float32), norm2_gain.astype(jnp.float32), norm2_shift.astype(jnp.float32))

    def one_row(totals, row_items):
        row_input, segment_row, step_row, rank_row, cot_row = row_items

        def forward(value, *weights):
            return forward_row(value, *weights, segment_row)
        row_output, pullback = jax.vjp(forward, row_input.astype(jnp.float32), *params)
        slots = jnp.arange(step_row.shape[0], dtype=jnp.int32)
        picked = segment_row[:, None] == slots[None, :]
        step_token = lax.optimization_barrier(jnp.sum(jnp.where(picked, step_row[None, :], 0), axis=1)).astype(jnp.int32)
        keep_mask = (rank_row >= step_token).astype(jnp.float32)
        cotangent = cot_row.astype(jnp.float32) * keep_mask[:, None]
        grads = pullback(cotangent)
        new_totals = tuple((total + grad for total, grad in zip(totals, grads[1:])))
        return (new_totals, (row_output.astype(jnp.bfloat16), grads[0]))
    start_totals = tuple((jnp.zeros_like(param) for param in params))
    totals, (outputs, in_grads) = lax.scan(one_row, start_totals, (inputs, segment_ids, item_steps, gen_rank, out_grad))
    return (outputs, in_grads, totals[0], totals[1], totals[2], totals[3], totals[4], totals[5], totals[6], totals[7])
```

```python
import functools

import jax
import jax.numpy as jnp
from jax import lax
from jax.experimental import pallas as pl
from jax.experimental.pallas import tpu as pltpu
from jax.sharding import Mesh
from jax.sharding import PartitionSpec as P

D = 512
HEADS = 8
PAIRS = HEADS // 2
FF = 2048
EPS = 1e-05
HALO = 128
BLOCK = 128
BF16 = jnp.bfloat16
F32 = jnp.float32
VMEM_LIMIT = 58 * 1024 * 1024


def dot(a, b):
    return lax.dot_general(a, b, (((1,), (0,)), ((), ())), preferred_element_type=F32)


def dot_t(a, b):
    return lax.dot_general(a, b, (((1,), (1,)), ((), ())), preferred_element_type=F32)


def t_dot(a, b):
    return lax.dot_general(a, b, (((0,), (0,)), ((), ())), preferred_element_type=F32)


def normalize(value):
    center = jnp.mean(value, axis=-1, keepdims=True)
    centred = value - center
    spread = jnp.mean(centred * centred, axis=-1, keepdims=True)
    inverse = lax.rsqrt(spread + EPS)
    return centred * inverse, inverse


def window_rows(left, middle, right, block):
    last = 2 + middle.shape[0] // BLOCK - 1
    if block == 0:
        return left[...]
    if block == last:
        return right[...]
    return middle[(block - 1) * BLOCK : block * BLOCK, :]


def two_blocks(left, middle, right, tile):
    return jnp.concatenate(
        [window_rows(left, middle, right, 2 * tile), window_rows(left, middle, right, 2 * tile + 1)],
        axis=0,
    )


def split_pairs(keys, values, kc, vx, block):
    lane = lax.broadcasted_iota(jnp.int32, (BLOCK, BLOCK), 1)
    even = lane < 64
    zero = jnp.zeros((BLOCK, BLOCK), BF16)
    ones_even = even.astype(F32).astype(BF16)
    ones_odd = (~even).astype(F32).astype(BF16)
    for p in range(PAIRS):
        k = keys[:, p * 128 : (p + 1) * 128]
        v = values[:, p * 128 : (p + 1) * 128]
        base = block * 256
        kc[p, pl.ds(base, 128), :] = jnp.where(even, k, zero)
        kc[p, pl.ds(base + 128, 128), :] = jnp.where(even, zero, k)
        vx[p, pl.ds(base, 128), 0:128] = jnp.where(even, v, zero)
        vx[p, pl.ds(base + 128, 128), 0:128] = jnp.where(even, zero, v)
        vx[p, pl.ds(base, 128), 128:256] = ones_even
        vx[p, pl.ds(base + 128, 128), 128:256] = ones_odd


def attend_kernel(blocks, scal, xl, x, xr, seg, gain, shift, weight,
                  normed_o, qkv_o, att_o, probs_o, inv_o, normed_s, qkv_s, kc, vx):
    step = pl.program_id(0)
    tiles = blocks // 2

    @pl.when(step == 0)
    def _():
        for r in range(tiles):
            base, _ = normalize(two_blocks(xl, x, xr, r).astype(F32))
            normed_s[r * 256 : (r + 1) * 256, :] = (base * gain[...] + shift[...]).astype(BF16)

        def project(r, carry):
            rows = pl.ds(pl.multiple_of(r * 256, 256), 256)
            qkv = dot(normed_s[rows, :], weight[...]).astype(BF16)
            qkv_s[rows, :] = qkv
            for half in range(2):
                part = qkv[half * 128 : (half + 1) * 128]
                split_pairs(part[:, 512:1024], part[:, 1024:1536], kc, vx, 2 * r + half)
            return carry

        lax.fori_loop(0, tiles, project, 0)

    @pl.when(step > 0)
    def _():
        i = step - 1
        rows = pl.ds(pl.multiple_of(i * BLOCK, BLOCK), BLOCK)
        normed_o[...] = normed_s[rows, :]
        qkv_o[...] = qkv_s[rows, :]
        low = scal[i]
        count = scal[blocks + i]
        seg_q = jnp.transpose(jnp.broadcast_to(seg[i].astype(F32), (BLOCK, BLOCK)))
        first = pl.multiple_of(low * 256, 256)

        def attend(n):
            bias = [
                jnp.where(seg_q == jnp.broadcast_to(seg[low + t].astype(F32), (BLOCK, BLOCK)), 0.0, -1e30)
                for t in range(n)
            ]
            for p in range(PAIRS):
                q = qkv_s[rows, p * 128 : (p + 1) * 128] * jnp.asarray(0.125, BF16)
                scores = dot_t(q, kc[p, pl.ds(first, n * 256), :])
                tiles_s = [
                    [scores[:, t * 256 + h * 128 : t * 256 + h * 128 + 128] + bias[t] for t in range(n)]
                    for h in range(2)
                ]
                highest = [
                    jnp.max(functools.reduce(jnp.maximum, tiles_s[h]), axis=-1, keepdims=True)
                    for h in range(2)
                ]
                parts = []
                for t in range(n):
                    for h in range(2):
                        parts.append(jnp.exp(tiles_s[h][t] - highest[h]).astype(BF16))
                probs = jnp.concatenate(parts, axis=1)
                probs_o[0, p, :, 0 : n * 256] = probs
                mixed = dot(probs, vx[p, pl.ds(first, n * 256), :])
                inverse = 1.0 / mixed[:, 128:256]
                inv_o[:, p * 128 : (p + 1) * 128] = inverse
                att_o[:, p * 128 : (p + 1) * 128] = (mixed[:, 0:128] * inverse).astype(BF16)

        for n in range(1, 6):
            pl.when(count == n)(functools.partial(attend, n))


def gelu_both(v):
    c = 0.7978845608028654
    square = v * v
    t = jnp.tanh(c * v * (1.0 + 0.044715 * square))
    half = 0.5 * (1.0 + t)
    slope = half + 0.5 * v * (1.0 - t * t) * (c * (1.0 + 3.0 * 0.044715 * square))
    return v * half, slope


def feed_kernel(blocks, scal, att, inv, xl, x, xr, cl, cot, cr, out_w, up_w, down_w, gain, shift,
                out_o, dmid_o, a_o, mine_o, sent_o, ln_o,
                cot_s, mid_s, n2_s, act_s, dpre_s, sum_s, dn2_s, dbr_s):
    f = pl.program_id(0)
    steps = pl.num_programs(0)
    tiles = blocks // 2
    core = scal[2 * blocks]

    @pl.when(f == 0)
    def _():
        for r in range(tiles):
            rows = slice(r * 256, (r + 1) * 256)
            cot_s[rows, :] = two_blocks(cl, cot, cr, r)
            mid = two_blocks(xl, x, xr, r).astype(F32) + dot(att[rows, :], out_w[...])
            mid_s[rows, :] = mid
            sum_s[rows, :] = mid
            base, _ = normalize(mid)
            n2_s[rows, :] = (base * gain[...] + shift[...]).astype(BF16)
            dn2_s[rows, :] = jnp.zeros((256, D), F32)

    def tile(r, carry):
        rows = pl.ds(pl.multiple_of(r * 256, 256), 256)
        pre = dot(n2_s[rows, :], up_w[...])
        d_act = dot_t(cot_s[rows, :], down_w[...])
        act, slope = gelu_both(pre)
        act = act.astype(BF16)
        d_pre = (slope * d_act).astype(BF16)
        act_s[rows, :] = act
        dpre_s[rows, :] = d_pre
        sum_s[rows, :] += dot(act, down_w[...])
        dn2_s[rows, :] += dot_t(d_pre, up_w[...])
        return carry

    lax.fori_loop(0, tiles, tile, 0)
    grad_down = t_dot(act_s[...], cot_s[...]).astype(BF16).reshape(32, 16, 512)
    grad_up = t_dot(n2_s[...], dpre_s[...]).astype(BF16).reshape(2, 16, 16, 512)

    spot = lax.rem(f, 2) * 8
    for half in range(2):

        @pl.when((f // 2 == half) & (core == half))
        def _():
            mine_o[pl.ds(spot, 8), :, :, 0:512] = grad_down.reshape(8, 4, 16, 512)

        @pl.when((f // 2 == half) & (core != half))
        def _():
            sent_o[pl.ds(spot, 8), :, :, 0:512] = grad_down.reshape(8, 4, 16, 512)

        @pl.when(core == half)
        def _():
            mine_o[:, pl.ds(f, 1), :, 512:1024] = grad_up[half].reshape(16, 1, 16, 512)

        @pl.when(core != half)
        def _():
            sent_o[:, pl.ds(f, 1), :, 512:1024] = grad_up[half].reshape(16, 1, 16, 512)

    @pl.when(f == steps - 1)
    def _():
        def finish(r, carry):
            rows = pl.ds(pl.multiple_of(r * 256, 256), 256)
            out_o[rows, :] = sum_s[rows, :].astype(BF16)
            n2, inverse = normalize(mid_s[rows, :])
            d_n2 = dn2_s[rows, :]
            e = d_n2 * gain[...]
            mean_e = jnp.mean(e, axis=-1, keepdims=True)
            mean_en = jnp.mean(e * n2, axis=-1, keepdims=True)
            d_mid = cot_s[rows, :].astype(F32) + (e - mean_e - n2 * mean_en) * inverse
            dmid_o[rows, :] = d_mid
            branch = d_mid.astype(BF16)
            dbr_s[rows, :] = branch
            d_att = dot_t(branch, out_w[...]) * inv[rows, :]
            minus = -(d_att * att[rows, :].astype(F32))
            for p in range(PAIRS):
                cols = slice(p * 128, (p + 1) * 128)
                a_o[rows, p * 256 : p * 256 + 128] = d_att[:, cols].astype(BF16)
                a_o[rows, p * 256 + 128 : p * 256 + 256] = minus[:, cols].astype(BF16)
            g, s = carry
            return (
                g + jnp.sum(d_n2 * n2, axis=0, keepdims=True),
                s + jnp.sum(d_n2, axis=0, keepdims=True),
            )

        zero = jnp.zeros((1, D), F32)
        grad_gain, grad_shift = lax.fori_loop(0, tiles, finish, (zero, zero))
        ln_o[0:1, :] = grad_gain
        ln_o[1:2, :] = grad_shift
        grad_out = t_dot(att[...], dbr_s[...]).astype(BF16)
        for half in range(2):
            part = grad_out[half * 256 : (half + 1) * 256].reshape(16, 16, 512)

            @pl.when(core == half)
            def _():
                for c in range(4):
                    mine_o[:, c, :, 1024:1152] = part[:, :, c * 128 : (c + 1) * 128]

            @pl.when(core != half)
            def _():
                for c in range(4):
                    sent_o[:, c, :, 1024:1152] = part[:, :, c * 128 : (c + 1) * 128]


def back_kernel(blocks, scal, probs, a, qkv, normed, weight, xl, x, xr, dmid, gain, ln2,
                grad_o, mine_o, sent_o, kc, vx, dk_s, dv_s, dqkv_s):
    step = pl.program_id(0)
    tiles = blocks // 2
    core = scal[2 * blocks]

    @pl.when(step == 0)
    def _():
        def build(b, carry):
            rows = pl.ds(pl.multiple_of(b * BLOCK, BLOCK), BLOCK)
            split_pairs(qkv[rows, 512:1024], qkv[rows, 1024:1536], kc, vx, b)
            return carry

        lax.fori_loop(0, blocks, build, 0)
        dk_s[...] = jnp.zeros(dk_s.shape, F32)
        dv_s[...] = jnp.zeros(dv_s.shape, F32)

    @pl.when(step < blocks)
    def _():
        low = scal[step]
        count = scal[blocks + step]
        rows = pl.ds(pl.multiple_of(step * BLOCK, BLOCK), BLOCK)
        first = pl.multiple_of(low * 256, 256)

        def back(n):
            keys = pl.ds(first, n * 256)
            for p in range(PAIRS):
                d_out = a[:, p * 256 : p * 256 + 128]
                d_probs = dot_t(a[:, p * 256 : p * 256 + 256], vx[p, keys, :])
                weights = probs[0, p, :, 0 : n * 256]
                d_scores = (weights.astype(F32) * d_probs).astype(BF16)
                q = qkv[rows, p * 128 : (p + 1) * 128] * jnp.asarray(0.125, BF16)
                d_q = dot(d_scores, kc[p, keys, :]) * 0.125
                dqkv_s[rows, p * 128 : (p + 1) * 128] = d_q.astype(BF16)
                dk_s[p, keys, :] += t_dot(d_scores, q)
                dv_s[p, keys, :] += t_dot(weights, d_out)

        for n in range(1, 6):
            pl.when(count == n)(functools.partial(back, n))

    @pl.when(step == blocks)
    def _():
        even = lax.broadcasted_iota(jnp.int32, (BLOCK, BLOCK), 1) < 64

        def fold(b, carry):
            rows = pl.ds(pl.multiple_of(b * BLOCK, BLOCK), BLOCK)
            up = pl.ds(pl.multiple_of(b * 256, 256), 128)
            down = pl.ds(pl.multiple_of(b * 256 + 128, 128), 128)
            for p in range(PAIRS):
                for source, spot in ((dk_s, 512), (dv_s, 1024)):
                    both = jnp.where(even, source[p, up, :], source[p, down, :])
                    dqkv_s[rows, spot + p * 128 : spot + (p + 1) * 128] = both.astype(BF16)
            return carry

        lax.fori_loop(0, blocks, fold, 0)
        for c in range(4):
            part = t_dot(normed[...], dqkv_s[:, c * 384 : (c + 1) * 384]).astype(BF16)
            for half in range(2):
                piece = part[half * 256 : (half + 1) * 256].reshape(16, 16, 384)

                @pl.when(core == half)
                def _():
                    mine_o[:, c, :, 0:384] = piece

                @pl.when(core != half)
                def _():
                    sent_o[:, c, :, 0:384] = piece

        grad_gain = jnp.zeros((1, D), F32)
        grad_shift = jnp.zeros((1, D), F32)
        for r in range(tiles):
            rows = slice(r * 256, (r + 1) * 256)
            d_n1 = dot_t(dqkv_s[rows, :], weight[...])
            n1, inverse = normalize(two_blocks(xl, x, xr, r).astype(F32))
            e = d_n1 * gain[...]
            mean_e = jnp.mean(e, axis=-1, keepdims=True)
            mean_en = jnp.mean(e * n1, axis=-1, keepdims=True)
            grad_o[rows, :] = dmid[rows, :] + (e - mean_e - n1 * mean_en) * inverse
            grad_gain += jnp.sum(d_n1 * n1, axis=0, keepdims=True)
            grad_shift += jnp.sum(d_n1, axis=0, keepdims=True)
        vectors = [grad_gain, grad_shift, ln2[0:1, :], ln2[1:2, :]]
        small = jnp.concatenate(
            [v[:, c * 128 : (c + 1) * 128] for v in vectors for c in range(4)], axis=0
        ).astype(BF16)
        spread = jnp.broadcast_to(small[None, None], (16, 4, 16, 128))
        mine_o[:, :, :, 384:512] = spread
        sent_o[:, :, :, 384:512] = spread


def whole(shape):
    return pl.BlockSpec(shape, lambda s, scal: (0,) * len(shape))


def shape_of(shape, dtype):
    return jax.ShapeDtypeStruct(shape, dtype)


def params():
    return pltpu.CompilerParams(
        dimension_semantics=("arbitrary",), vmem_limit_bytes=VMEM_LIMIT
    )


def attend_call(scal, xl, x, xr, seg, gain, shift, weight):
    rows = x.shape[0] + 2 * HALO
    blocks = rows // BLOCK
    at = lambda s, scal: (jnp.maximum(s - 1, 0), 0)
    at4 = lambda s, scal: (jnp.maximum(s - 1, 0), 0, 0, 0)
    return pl.pallas_call(
        functools.partial(attend_kernel, blocks),
        grid_spec=pltpu.PrefetchScalarGridSpec(
            num_scalar_prefetch=1,
            grid=(blocks + 1,),
            in_specs=[
                whole((HALO, D)), whole(x.shape), whole((HALO, D)), whole(seg.shape),
                whole((1, D)), whole((1, D)), whole(weight.shape),
            ],
            out_specs=[
                pl.BlockSpec((BLOCK, D), at),
                pl.BlockSpec((BLOCK, 3 * D), at),
                pl.BlockSpec((BLOCK, D), at),
                pl.BlockSpec((1, PAIRS, BLOCK, 1280), at4),
                pl.BlockSpec((BLOCK, D), at),
            ],
            scratch_shapes=[
                pltpu.VMEM((rows, D), BF16),
                pltpu.VMEM((rows, 3 * D), BF16),
                pltpu.VMEM((PAIRS, blocks * 256, 128), BF16),
                pltpu.VMEM((PAIRS, blocks * 256, 256), BF16),
            ],
        ),
        out_shape=[
            shape_of((rows, D), BF16),
            shape_of((rows, 3 * D), BF16),
            shape_of((rows, D), BF16),
            shape_of((blocks, PAIRS, BLOCK, 1280), BF16),
            shape_of((rows, D), F32),
        ],
        compiler_params=params(),
        cost_estimate=pl.CostEstimate(flops=8 * 10**9, bytes_accessed=25 * 10**6, transcendentals=4 * 10**6),
        name="attend",
    )(scal, xl, x, xr, seg, gain, shift, weight)


def feed_call(scal, att, inv, xl, x, xr, cl, cot, cr, out_w, up_w, down_w, gain, shift):
    rows = att.shape[0]
    blocks = rows // BLOCK
    half = (16, 4, 16, 1152)
    return pl.pallas_call(
        functools.partial(feed_kernel, blocks),
        grid_spec=pltpu.PrefetchScalarGridSpec(
            num_scalar_prefetch=1,
            grid=(FF // 512,),
            in_specs=[
                whole((rows, D)), whole((rows, D)),
                whole((HALO, D)), whole(x.shape), whole((HALO, D)),
                whole((HALO, D)), whole(x.shape), whole((HALO, D)),
                whole((D, D)),
                pl.BlockSpec((D, 512), lambda s, scal: (0, s)),
                pl.BlockSpec((512, D), lambda s, scal: (s, 0)),
                whole((1, D)), whole((1, D)),
            ],
            out_specs=[
                whole((rows, D)), whole((rows, D)), whole((rows, 2 * D)),
                whole(half), whole(half), whole((2, D)),
            ],
            scratch_shapes=[
                pltpu.VMEM((rows, D), BF16),
                pltpu.VMEM((rows, D), F32),
                pltpu.VMEM((rows, D), BF16),
                pltpu.VMEM((rows, 512), BF16),
                pltpu.VMEM((rows, 512), BF16),
                pltpu.VMEM((rows, D), F32),
                pltpu.VMEM((rows, D), F32),
                pltpu.VMEM((rows, D), BF16),
            ],
        ),
        out_shape=[
            shape_of((rows, D), BF16),
            shape_of((rows, D), F32),
            shape_of((rows, 2 * D), BF16),
            shape_of(half, BF16),
            shape_of(half, BF16),
            shape_of((2, D), F32),
        ],
        compiler_params=params(),
        cost_estimate=pl.CostEstimate(flops=20 * 10**9, bytes_accessed=25 * 10**6, transcendentals=3 * 10**6),
        name="feed",
    )(scal, att, inv, xl, x, xr, cl, cot, cr, out_w, up_w, down_w, gain, shift)


def back_call(scal, probs, a, qkv, normed, weight, xl, x, xr, dmid, gain, ln2):
    rows = qkv.shape[0]
    blocks = rows // BLOCK
    half = (16, 4, 16, 512)
    last = blocks - 1
    return pl.pallas_call(
        functools.partial(back_kernel, blocks),
        grid_spec=pltpu.PrefetchScalarGridSpec(
            num_scalar_prefetch=1,
            grid=(blocks + 1,),
            in_specs=[
                pl.BlockSpec((1, PAIRS, BLOCK, 1280), lambda s, scal: (jnp.minimum(s, last), 0, 0, 0)),
                pl.BlockSpec((BLOCK, 2 * D), lambda s, scal: (jnp.minimum(s, last), 0)),
                whole((rows, 3 * D)), whole((rows, D)), whole((D, 3 * D)),
                whole((HALO, D)), whole(x.shape), whole((HALO, D)),
                whole((rows, D)), whole((1, D)), whole((2, D)),
            ],
            out_specs=[whole((rows, D)), whole(half), whole(half)],
            scratch_shapes=[
                pltpu.VMEM((PAIRS, blocks * 256, 128), BF16),
                pltpu.VMEM((PAIRS, blocks * 256, 256), BF16),
                pltpu.VMEM((PAIRS, blocks * 256, 128), F32),
                pltpu.VMEM((PAIRS, blocks * 256, 128), F32),
                pltpu.VMEM((rows, 3 * D), BF16),
            ],
        ),
        out_shape=[shape_of((rows, D), F32), shape_of(half, BF16), shape_of(half, BF16)],
        compiler_params=params(),
        cost_estimate=pl.CostEstimate(flops=15 * 10**9, bytes_accessed=30 * 10**6, transcendentals=0),
        name="back",
    )(scal, probs, a, qkv, normed, weight, xl, x, xr, dmid, gain, ln2)


def other_core(value):
    return lax.ppermute(value, "core", [(0, 1), (1, 0)])


def all_shares(value, groups):
    parts = lax.all_to_all(value, ("rows", "x"), 0, 0, tiled=True)
    return jnp.sum(parts.astype(F32), axis=0).astype(BF16)


def gather_shares(share, groups):
    copies = jnp.broadcast_to(share[None], (groups, *share.shape))
    return lax.all_to_all(copies, ("rows", "x"), 0, 0, tiled=True)


def per_device(
    inputs, qkv_weight, out_weight, up_weight, down_weight, norm1_gain, norm1_shift,
    norm2_gain, norm2_shift, segment_ids, item_steps, gen_rank, out_grad,
):
    x = inputs[0]
    positions = x.shape[0]
    blocks = (positions + 2 * HALO) // BLOCK
    chips = lax.axis_size("rows") * lax.axis_size("x")
    seq_parts = lax.axis_size("x") * lax.axis_size("core")
    seq = ("x", "core")
    to_right = [(i, i + 1) for i in range(seq_parts - 1)]
    to_left = [(i + 1, i) for i in range(seq_parts - 1)]
    core = lax.axis_index("core")

    xl = lax.ppermute(x[positions - HALO :], seq, to_right)
    xr = lax.ppermute(x[:HALO], seq, to_left)

    ends = jnp.full((HALO,), -1, jnp.int32), jnp.full((HALO,), 1000, jnp.int32)
    padded = jnp.concatenate([ends[0], segment_ids[0], ends[1]])
    window = lax.dynamic_slice_in_dim(
        padded, lax.axis_index(seq) * positions, positions + 2 * HALO, 0
    )
    by_block = window.reshape(blocks, BLOCK)
    low = jnp.sum(window[None, :] < by_block[:, :1], axis=1, dtype=jnp.int32) // BLOCK
    high = (jnp.sum(window[None, :] <= by_block[:, -1:], axis=1, dtype=jnp.int32) - 1) // BLOCK

    local = window[HALO : HALO + positions]

    def border(before, after):
        value = before[-1]
        across = value == after[0]
        left_count = jnp.sum(before == value, dtype=jnp.int32)
        right_count = jnp.sum(after == value, dtype=jnp.int32)
        return value, across, left_count >= right_count

    value_l, across_l, to_left_l = border(window[:HALO], local)
    value_r, across_r, to_left_r = border(local, window[HALO + positions :])
    drop_l = jnp.where(across_l & to_left_l, value_l, -2)
    drop_r = jnp.where(across_r & ~to_left_r, value_r, -2)
    own = (local != drop_l) & (local != drop_r)
    scal = jnp.concatenate([low, high - low + 1, core[None].astype(jnp.int32)])
    seg_rows = by_block.reshape(blocks, 1, BLOCK)

    slots = jnp.arange(item_steps.shape[1], dtype=jnp.int32)
    picked = local[None, :] == slots[:, None]
    step_token = jnp.sum(jnp.where(picked, item_steps[0][:, None], 0), axis=0)
    keep = gen_rank[0] >= step_token
    zero = jnp.zeros((), BF16)
    cot = jnp.where((keep & own)[:, None], out_grad[0], zero)
    send_l = jnp.where((keep & (local == drop_l))[:HALO, None], out_grad[0, :HALO], zero)
    send_r = jnp.where(
        (keep & (local == drop_r))[positions - HALO :, None], out_grad[0, positions - HALO :], zero
    )
    cl = lax.ppermute(send_r, seq, to_right)
    cr = lax.ppermute(send_l, seq, to_left)

    gain1, shift1 = norm1_gain.reshape(1, D), norm1_shift.reshape(1, D)
    gain2, shift2 = norm2_gain.reshape(1, D), norm2_shift.reshape(1, D)
    normed1, qkv, att, probs, inv = attend_call(
        scal, xl, x, xr, seg_rows, gain1, shift1, qkv_weight
    )
    out_w, d_mid, a, mine_a, sent_a, ln2 = feed_call(
        scal, att, inv, xl, x, xr, cl, cot, cr, out_weight, up_weight, down_weight, gain2, shift2
    )
    out_from_r = lax.ppermute(out_w[:HALO], seq, to_left)
    out_from_l = lax.ppermute(out_w[HALO + positions :], seq, to_right)

    half_a = (mine_a.astype(F32) + other_core(sent_a).astype(F32)).astype(BF16)
    share_a = all_shares(half_a.reshape(chips, -1, 1152), chips)
    in_w, mine_b, sent_b = back_call(
        scal, probs, a, qkv, normed1, qkv_weight, xl, x, xr, d_mid, gain1, ln2
    )
    in_from_r = lax.ppermute(in_w[:HALO].astype(BF16), seq, to_left)
    in_from_l = lax.ppermute(in_w[HALO + positions :].astype(BF16), seq, to_right)
    half_b = (mine_b.astype(F32) + other_core(sent_b).astype(F32)).astype(BF16)
    share_b = all_shares(half_b.reshape(chips, -1, 512), chips)
    small = share_b[:16, 384:]
    full_a = gather_shares(share_a, chips)
    full_b = gather_shares(share_b[:, :384], chips)
    far_a = other_core(full_a)
    far_b = other_core(full_b)

    def both(near, far):
        first = jnp.where(core == 0, near, far)
        second = jnp.where(core == 0, far, near)
        return jnp.stack([first, second])

    all_a = both(full_a, far_a).reshape(2, 16, 4, 16, 1152)
    all_b = both(full_b, far_b).reshape(2, 16, 4, 16, 384)
    grad_down = all_a[..., :512].reshape(FF, D).astype(F32)
    grad_up = all_a[..., 512:1024].transpose(0, 1, 3, 2, 4).reshape(D, FF).astype(F32)
    grad_out = all_a[..., 1024:].transpose(0, 1, 3, 2, 4).reshape(D, D).astype(F32)
    grad_qkv = all_b.transpose(0, 1, 3, 2, 4).reshape(D, 3 * D).astype(F32)
    vectors = small.astype(F32).reshape(4, D)

    def merge(own_rows, from_l, from_r):
        mine = own_rows[HALO : HALO + positions]
        head = jnp.where(own[:HALO, None], mine[:HALO], from_l.astype(mine.dtype))
        tail = jnp.where(
            own[positions - HALO :, None], mine[positions - HALO :], from_r.astype(mine.dtype)
        )
        return jnp.concatenate([head, mine[HALO : positions - HALO], tail])

    output = merge(out_w, out_from_l, out_from_r)
    input_grad = merge(in_w, in_from_l, in_from_r)
    return (
        output[None], input_grad[None], grad_qkv, grad_out, grad_up, grad_down,
        vectors[0], vectors[1], vectors[2], vectors[3],
    )


def solution(mesh):
    rows = mesh.devices.shape[0]
    parts = mesh.devices.shape[1]
    split = Mesh(mesh.devices.reshape(rows, parts // 2, 2), ("rows", "x", "core"))
    seq = ("x", "core")
    return jax.shard_map(
        per_device,
        mesh=split,
        in_specs=(
            P("rows", seq, None), P(), P(), P(), P(), P(), P(), P(), P(),
            P("rows", None), P("rows", None), P("rows", seq), P("rows", seq, None),
        ),
        out_specs=(
            P("rows", seq, None), P("rows", seq, None),
            P(), P(), P(), P(), P(), P(), P(), P(),
        ),
        check_vma=False,
    )
```

```python
import functools

import jax
import jax.numpy as jnp
from jax import lax
from jax.experimental import pallas as pl
from jax.experimental.pallas import tpu as pltpu
from jax.sharding import Mesh
from jax.sharding import PartitionSpec as P

D = 512
HEADS = 8
PAIRS = HEADS // 2
FF = 2048
EPS = 1e-05
HALO = 128
BLOCK = 128
BF16 = jnp.bfloat16
F32 = jnp.float32
VMEM_LIMIT = 58 * 1024 * 1024


def dot(a, b):
    return lax.dot_general(a, b, (((1,), (0,)), ((), ())), preferred_element_type=F32)


def dot_t(a, b):
    return lax.dot_general(a, b, (((1,), (1,)), ((), ())), preferred_element_type=F32)


def t_dot(a, b):
    return lax.dot_general(a, b, (((0,), (0,)), ((), ())), preferred_element_type=F32)


def normalize(value):
    center = jnp.mean(value, axis=-1, keepdims=True)
    centred = value - center
    spread = jnp.mean(centred * centred, axis=-1, keepdims=True)
    inverse = lax.rsqrt(spread + EPS)
    return centred * inverse, inverse


def two_blocks(left, middle, right, tile, start=0):
    last = 1 + middle.shape[0] // BLOCK
    parts = []
    for block in (2 * tile, 2 * tile + 1):
        if block == 0:
            parts.append(left[start : start + HALO, :])
        elif block == last:
            parts.append(right[start : start + HALO, :])
        else:
            parts.append(middle[(block - 1) * BLOCK : block * BLOCK, :])
    return jnp.concatenate(parts, axis=0)


def split_pairs(keys, values, kc, vx, block):
    lane = lax.broadcasted_iota(jnp.int32, (BLOCK, BLOCK), 1)
    even = lane < 64
    zero = jnp.zeros((BLOCK, BLOCK), BF16)
    ones_even = even.astype(F32).astype(BF16)
    ones_odd = (~even).astype(F32).astype(BF16)
    for p in range(kc.shape[0]):
        k = keys[:, p * 128 : (p + 1) * 128]
        v = values[:, p * 128 : (p + 1) * 128]
        base = block * 256
        kc[p, pl.ds(base, 128), :] = jnp.where(even, k, zero)
        kc[p, pl.ds(base + 128, 128), :] = jnp.where(even, zero, k)
        vx[p, pl.ds(base, 128), 0:128] = jnp.where(even, v, zero)
        vx[p, pl.ds(base + 128, 128), 0:128] = jnp.where(even, zero, v)
        vx[p, pl.ds(base, 128), 128:256] = ones_even
        vx[p, pl.ds(base + 128, 128), 128:256] = ones_odd


def column(row):
    return jnp.transpose(jnp.broadcast_to(row, (BLOCK, BLOCK)))


def keep_rows(values, mask):
    return jnp.concatenate(
        [
            jnp.where(mask, values[:, c * 128 : (c + 1) * 128].astype(F32), 0.0).astype(BF16)
            for c in range(D // 128)
        ],
        axis=1,
    )


def count(mask):
    return jnp.sum(mask.astype(F32)).astype(jnp.int32)


def prepare_kernel(inner, place, segments, steps, rank, x, out_grad, scal_o, seg_o, cot_o, left_o, right_o):
    seq = place[0]
    row_blocks = segments.shape[1] // BLOCK
    rows = []
    for b in range(inner + 2):
        at = seq * inner + b - 1
        if b == 0:
            at = jnp.maximum(at, 0)
        if b == inner + 1:
            at = jnp.minimum(at, row_blocks - 1)
        row = segments[0:1, pl.ds(pl.multiple_of(at * BLOCK, BLOCK), BLOCK)]
        if b == 0:
            row = jnp.where(seq > 0, row, -1)
        if b == inner + 1:
            row = jnp.where(seq * inner + inner < row_blocks, row, 1000)
        rows.append(row)
        seg_o[b] = row
    window = jnp.concatenate(rows, axis=0)
    local = window[1 : inner + 1]
    for b in range(inner + 2):
        first, last = rows[b][0, 0], rows[b][0, BLOCK - 1]
        low = count(window < first) // BLOCK
        high = (count(window <= last) - 1) // BLOCK
        scal_o[b] = low
        scal_o[inner + 2 + b] = high - low + 1
    scal_o[2 * inner + 4] = place[1]

    def border(before, after, first):
        value = before[-1:][0, BLOCK - 1]
        across = value == first
        return value, across, count(before == value) >= count(after == value)

    value_l, across_l, to_left_l = border(rows[0], local, rows[1][0, 0])
    value_r, across_r, to_left_r = border(local, rows[-1], rows[-1][0, 0])
    drop_l = jnp.where(across_l & to_left_l, value_l, -2)
    drop_r = jnp.where(across_r & jnp.logical_not(to_left_r), value_r, -2)
    scal_o[2 * inner + 5] = drop_l
    scal_o[2 * inner + 6] = drop_r

    token = jnp.zeros(local.shape, jnp.int32)
    for slot in range(steps.shape[1]):
        token = jnp.where(local == slot, steps[0, slot], token)
    for b in range(inner):
        part = slice(b * BLOCK, (b + 1) * BLOCK)
        keep = rank[0:1, part] >= token[b : b + 1]
        seg = rows[b + 1]
        own = (seg != drop_l) & (seg != drop_r)
        values = out_grad[part, :]
        cot_o[part, :] = keep_rows(values, column((keep & own).astype(F32)) > 0.5)
        if b == 0:
            left_o[0:HALO, :] = x[part, :]
            left_o[HALO : 2 * HALO, :] = keep_rows(values, column((keep & (seg == drop_l)).astype(F32)) > 0.5)
        if b == inner - 1:
            right_o[0:HALO, :] = x[part, :]
            right_o[HALO : 2 * HALO, :] = keep_rows(values, column((keep & (seg == drop_r)).astype(F32)) > 0.5)


def prepare_call(place, segments, steps, rank, x, out_grad):
    inner = x.shape[0] // BLOCK
    vmem = pl.BlockSpec(memory_space=pltpu.VMEM)
    smem = pl.BlockSpec(memory_space=pltpu.SMEM)
    return pl.pallas_call(
        functools.partial(prepare_kernel, inner),
        in_specs=[smem, vmem, smem, vmem, vmem, vmem],
        out_specs=[smem, vmem, vmem, vmem, vmem],
        out_shape=[
            shape_of((2 * inner + 7,), jnp.int32),
            shape_of((inner + 2, 1, BLOCK), jnp.int32),
            shape_of(x.shape, BF16),
            shape_of((2 * HALO, D), BF16),
            shape_of((2 * HALO, D), BF16),
        ],
        compiler_params=pltpu.CompilerParams(vmem_limit_bytes=VMEM_LIMIT),
        name="prepare",
    )(place, segments, steps, rank, x, out_grad)


def patch_kernel(blocks, scal, out, grad, seg, left, right, out_o, grad_o):
    step = pl.program_id(0)
    drop_l, drop_r = scal[2 * blocks + 1], scal[2 * blocks + 2]
    row = seg[0]
    drop = jnp.where(step == 0, drop_l, drop_r)
    lost = column((row == drop).astype(F32)) > 0.5
    for c in range(D // 128):
        cols = slice(c * 128, (c + 1) * 128)
        for mine, start, result in ((out, 0, out_o), (grad, HALO, grad_o)):
            part = slice(start, start + HALO)
            other = jnp.where(step == 0, left[part, cols].astype(F32), right[part, cols].astype(F32))
            value = jnp.where(lost, other, mine[:, cols].astype(F32))
            result[:, cols] = value.astype(result.dtype)


def patch_call(scal, out, grad, seg, left, right):
    inner = out.shape[0] // BLOCK
    block = lambda s, scal: (s * (inner - 1), 0)
    return pl.pallas_call(
        functools.partial(patch_kernel, inner + 2),
        grid_spec=pltpu.PrefetchScalarGridSpec(
            num_scalar_prefetch=1,
            grid=(2,),
            in_specs=[
                pl.BlockSpec((BLOCK, D), block),
                pl.BlockSpec((BLOCK, D), block),
                pl.BlockSpec((1, 1, BLOCK), lambda s, scal: (1 + s * (inner - 1), 0, 0)),
                whole((2 * HALO, D)), whole((2 * HALO, D)),
            ],
            out_specs=[pl.BlockSpec((BLOCK, D), block), pl.BlockSpec((BLOCK, D), block)],
        ),
        out_shape=[shape_of(out.shape, out.dtype), shape_of(grad.shape, grad.dtype)],
        input_output_aliases={1: 0, 2: 1},
        compiler_params=params(),
        name="patch",
    )(scal, out, grad, seg, left, right)


def unpack_kernel(core_at, scal, near, far, down_o, up_o, out_o, qkv_o):
    step = pl.program_id(0)
    core = scal[core_at]

    def unpack(a):
        down_o[...] = a[:, :, :, 0:512].astype(F32).reshape(256, 512)
        for c in range(4):
            cols = slice(c * 128, (c + 1) * 128)
            up_o[:, c * 512 : (c + 1) * 512] = a[:, c, :, 512:1024].astype(F32).reshape(64, 512)
            for part in range(3):
                spot = part * 512 + c * 128
                value = a[:, c, :, 1024 + part * 128 : 1152 + part * 128]
                qkv_o[:, spot : spot + 128] = value.astype(F32).reshape(64, 128)
            out_o[:, cols] = a[:, c, :, 1408:1536].astype(F32).reshape(64, 128)

    pl.when(step // 4 == core)(lambda: unpack(near))
    pl.when(step // 4 != core)(lambda: unpack(far))


def unpack_call(scal, core_at, near, far):
    def near_at(s, scal):
        return (jnp.where(s // 4 == scal[core_at], s % 4, jnp.where(s < 4, 0, 3)), 0, 0, 0)

    def far_at(s, scal):
        return (jnp.where(s // 4 != scal[core_at], s % 4, jnp.where(s < 4, 0, 3)), 0, 0, 0)

    out = lambda s, scal: (s, 0)
    block = (4, *near.shape[1:])
    return pl.pallas_call(
        functools.partial(unpack_kernel, core_at),
        grid_spec=pltpu.PrefetchScalarGridSpec(
            num_scalar_prefetch=1,
            grid=(8,),
            in_specs=[
                pl.BlockSpec(block, near_at), pl.BlockSpec(block, far_at),
            ],
            out_specs=[
                pl.BlockSpec((256, D), out), pl.BlockSpec((64, FF), out),
                pl.BlockSpec((64, D), out), pl.BlockSpec((64, 3 * D), out),
            ],
        ),
        out_shape=[
            shape_of((FF, D), F32), shape_of((D, FF), F32), shape_of((D, D), F32), shape_of((D, 3 * D), F32),
        ],
        compiler_params=params(),
        name="unpack",
    )(scal, near, far)


def attend_kernel(blocks, scal, left, x, right, seg, gain, shift, weight,
                  normed_o, qkv_o, att_o, probs_o, inv_o, normed_s, qkv_s, kc, vx):
    step = pl.program_id(0)
    tiles = blocks // 2

    @pl.when(step == 0)
    def _():
        for r in range(tiles):
            base, _ = normalize(two_blocks(left, x, right, r).astype(F32))
            normed_s[r * 256 : (r + 1) * 256, :] = (base * gain[...] + shift[...]).astype(BF16)

        def project(r, carry):
            rows = pl.ds(pl.multiple_of(r * 256, 256), 256)
            qkv = dot(normed_s[rows, :], weight[...]).astype(BF16)
            qkv_s[rows, :] = qkv
            for half in range(2):
                part = qkv[half * 128 : (half + 1) * 128]
                split_pairs(part[:, 512:1024], part[:, 1024:1536], kc, vx, 2 * r + half)
            return carry

        lax.fori_loop(0, tiles, project, 0)

    @pl.when(step > 0)
    def _():
        i = step - 1
        rows = pl.ds(pl.multiple_of(i * BLOCK, BLOCK), BLOCK)
        normed_o[...] = normed_s[rows, :]
        qkv_o[...] = qkv_s[rows, :]
        low = scal[i]
        count = scal[blocks + i]
        seg_q = jnp.transpose(jnp.broadcast_to(seg[i].astype(F32), (BLOCK, BLOCK)))
        first = pl.multiple_of(low * 256, 256)

        def attend(n):
            bias = [
                jnp.where(seg_q == jnp.broadcast_to(seg[low + t].astype(F32), (BLOCK, BLOCK)), 0.0, -1e30)
                for t in range(n)
            ]
            for p in range(PAIRS):
                q = qkv_s[rows, p * 128 : (p + 1) * 128] * jnp.asarray(0.125, BF16)
                scores = dot_t(q, kc[p, pl.ds(first, n * 256), :])
                tiles_s = [
                    [scores[:, t * 256 + h * 128 : t * 256 + h * 128 + 128] + bias[t] for t in range(n)]
                    for h in range(2)
                ]
                highest = [
                    jnp.max(functools.reduce(jnp.maximum, tiles_s[h]), axis=-1, keepdims=True)
                    for h in range(2)
                ]
                parts = []
                for t in range(n):
                    for h in range(2):
                        parts.append(jnp.exp(tiles_s[h][t] - highest[h]).astype(BF16))
                probs = jnp.concatenate(parts, axis=1)
                probs_o[0, p, :, 0 : n * 256] = probs
                mixed = dot(probs, vx[p, pl.ds(first, n * 256), :])
                inverse = 1.0 / mixed[:, 128:256]
                inv_o[:, p * 128 : (p + 1) * 128] = inverse.astype(BF16)
                att_o[:, p * 128 : (p + 1) * 128] = (mixed[:, 0:128] * inverse).astype(BF16)

        for n in range(1, 6):
            pl.when(count == n)(functools.partial(attend, n))


def gelu_both(v):
    c = 0.7978845608028654
    square = v * v
    inner = c + (0.044715 * c) * square
    gate = 0.5 + 0.5 * jnp.tanh(v * inner)
    act = v * gate
    slope = gate + act * ((1.0 - gate) * (6.0 * inner - 4.0 * c))
    return act, slope


def feed_kernel(blocks, scal, att, left, x, right, cot, out_w, up_w, down_w, gain, shift,
                base_o, rstd_o, cot_o, dn2_o, act_o, mine_o, sent_o,
                n2_s, act_s, dpre_s, up_s, *stage_s):
    f = pl.program_id(0)
    steps = pl.num_programs(0)
    tiles = blocks // 2
    core = scal[2 * blocks]

    @pl.when(f == 0)
    def _():
        for r in range(tiles):
            rows = slice(r * 256, (r + 1) * 256)
            cot_o[rows, :] = two_blocks(left, cot, right, r, HALO)
            mid = two_blocks(left, x, right, r).astype(F32) + dot(att[rows, :], out_w[...])
            base, inverse = normalize(mid)
            base_o[rows, :] = base.astype(BF16)
            rstd_o[rows, :] = jnp.broadcast_to(inverse, (256, 128))
            n2_s[rows, :] = (base * gain[...] + shift[...]).astype(BF16)

    up_s[f] = up_w[...]
    for r in range(tiles + 1):
        if r < tiles:
            rows = slice(r * 256, (r + 1) * 256)
            stage_s[r % 2][...] = dot(n2_s[rows, :], up_w[...])
            stage_s[2 + r % 2][...] = dot_t(cot_o[rows, :], down_w[...])
        if r > 0:
            rows = slice((r - 1) * 256, r * 256)
            act, slope = gelu_both(stage_s[(r - 1) % 2][...])
            act_s[rows, :] = act.astype(BF16)
            dpre_s[f, rows, :] = (slope * stage_s[2 + (r - 1) % 2][...]).astype(BF16)
    act_o[...] = act_s[...]
    grad_down = t_dot(act_s[...], cot_o[...]).astype(BF16).reshape(8, 4, 16, 512)
    grad_up = t_dot(n2_s[...], dpre_s[f]).astype(BF16).reshape(2, 16, 1, 16, 512)

    spot = lax.rem(f, 2) * 8
    for half in range(2):

        @pl.when((f // 2 == half) & (core == half))
        def _():
            mine_o[pl.ds(spot, 8), :, :, 0:512] = grad_down

        @pl.when((f // 2 == half) & (core != half))
        def _():
            sent_o[pl.ds(spot, 8), :, :, 0:512] = grad_down

        @pl.when(core == half)
        def _():
            mine_o[:, pl.ds(f, 1), :, 512:1024] = grad_up[half]

        @pl.when(core != half)
        def _():
            sent_o[:, pl.ds(f, 1), :, 512:1024] = grad_up[half]

    @pl.when(f == steps - 1)
    def _():
        def turn(r, carry):
            rows = pl.ds(pl.multiple_of(r * 256, 256), 256)
            d_pre = jnp.concatenate([dpre_s[k, rows, :] for k in range(FF // 512)], axis=1)
            up = jnp.concatenate([up_s[k] for k in range(FF // 512)], axis=1)
            dn2_o[rows, :] = dot_t(d_pre, up).astype(BF16)
            return carry

        lax.fori_loop(0, tiles, turn, 0)


def finish_kernel(blocks, att, left, x, right, act, out_w, down_w, out_o, left_o, right_o):
    tiles = blocks // 2
    for r in range(tiles):
        rows = slice(r * 256, (r + 1) * 256)
        mid = two_blocks(left, x, right, r).astype(F32) + dot(att[rows, :], out_w[...])
        total = (mid + dot(act[rows, :], down_w[...])).astype(BF16)
        for h in range(2):
            block = 2 * r + h
            part = total[h * BLOCK : (h + 1) * BLOCK]
            if block == 0:
                left_o[...] = part
            elif block == blocks - 1:
                right_o[...] = part
            else:
                out_o[(block - 1) * BLOCK : block * BLOCK, :] = part


def finish_call(att, left, x, right, act, out_w, down_w):
    rows = att.shape[0]
    vmem = pl.BlockSpec(memory_space=pltpu.VMEM)
    edge = shape_of((HALO, D), BF16)
    return pl.pallas_call(
        functools.partial(finish_kernel, rows // BLOCK),
        in_specs=[vmem] * 7,
        out_specs=[vmem] * 3,
        out_shape=[shape_of(x.shape, BF16), edge, edge],
        compiler_params=pltpu.CompilerParams(vmem_limit_bytes=VMEM_LIMIT),
        cost_estimate=pl.CostEstimate(flops=4 * 10**9, bytes_accessed=12 * 10**6, transcendentals=0),
        name="finish",
    )(att, left, x, right, act, out_w, down_w)


def middle_kernel(core_at, scal, base, rstd, dn2, cot, att, inv, out_w, gain,
                  dbr_o, a_o, mine_o, sent_o, ln_o, sum_s):
    r = pl.program_id(0)
    core = scal[core_at]

    @pl.when(r == 0)
    def _():
        sum_s[...] = jnp.zeros(sum_s.shape, F32)
        ln_o[...] = jnp.zeros(ln_o.shape, F32)

    n2 = base[...].astype(F32)
    inverse = jnp.concatenate([rstd[...]] * 4, axis=1)
    d_n2 = dn2[...].astype(F32)
    e = d_n2 * gain[...]
    scaled = d_n2 * n2
    mean_e = jnp.mean(e, axis=-1, keepdims=True)
    mean_en = jnp.mean(e * n2, axis=-1, keepdims=True)
    d_mid = cot[...].astype(F32) + (e - mean_e - n2 * mean_en) * inverse
    branch = d_mid.astype(BF16)
    dbr_o[...] = branch
    d_att = dot_t(branch, out_w[...]) * inv[...].astype(F32)
    minus = -(d_att * att[...].astype(F32))
    for p in range(PAIRS):
        cols = slice(p * 128, (p + 1) * 128)
        a_o[:, p * 256 : p * 256 + 128] = d_att[:, cols].astype(BF16)
        a_o[:, p * 256 + 128 : p * 256 + 256] = minus[:, cols].astype(BF16)
    ln_o[0:1, :] += jnp.sum(scaled, axis=0, keepdims=True)
    ln_o[1:2, :] += jnp.sum(d_n2, axis=0, keepdims=True)
    sum_s[...] += t_dot(att[...], branch)

    @pl.when(r == pl.num_programs(0) - 1)
    def _():
        for half in range(2):
            part = sum_s[half * 256 : (half + 1) * 256, :].astype(BF16).reshape(16, 16, 512)

            @pl.when(core == half)
            def _():
                for c in range(4):
                    mine_o[:, c] = part[:, :, c * 128 : (c + 1) * 128]

            @pl.when(core != half)
            def _():
                for c in range(4):
                    sent_o[:, c] = part[:, :, c * 128 : (c + 1) * 128]


def back_kernel(blocks, pairs, scal, probs, a, q_ref, k_ref, v_ref, normed,
                dqkv_o, mine_o, sent_o, kc, vx, dk_s, dv_s):
    step = pl.program_id(0)
    core = scal[2 * blocks]

    @pl.when(step == 0)
    def _():
        def build(b, carry):
            rows = pl.ds(pl.multiple_of(b * BLOCK, BLOCK), BLOCK)
            split_pairs(k_ref[rows, :], v_ref[rows, :], kc, vx, b)
            return carry

        lax.fori_loop(0, blocks, build, 0)
        dk_s[...] = jnp.zeros(dk_s.shape, F32)
        dv_s[...] = jnp.zeros(dv_s.shape, F32)

    @pl.when(step < blocks)
    def _():
        low = scal[step]
        n_keys = scal[blocks + step]
        rows = pl.ds(pl.multiple_of(step * BLOCK, BLOCK), BLOCK)
        first = pl.multiple_of(low * 256, 256)

        def back(n):
            keys = pl.ds(first, n * 256)
            for p in range(pairs):
                d_out = a[:, p * 256 : p * 256 + 128]
                d_probs = dot_t(a[:, p * 256 : p * 256 + 256], vx[p, keys, :])
                weights = probs[0, p, :, 0 : n * 256]
                d_scores = (weights.astype(F32) * d_probs).astype(BF16)
                q = q_ref[rows, p * 128 : (p + 1) * 128] * jnp.asarray(0.125, BF16)
                d_q = dot(d_scores, kc[p, keys, :]) * 0.125
                dqkv_o[rows, p * 384 : p * 384 + 128] = d_q.astype(BF16)
                dk_s[p, keys, :] += t_dot(d_scores, q)
                dv_s[p, keys, :] += t_dot(weights, d_out)

        for n in range(1, 6):
            pl.when(n_keys == n)(functools.partial(back, n))

    @pl.when(step == blocks)
    def _():
        even = lax.broadcasted_iota(jnp.int32, (BLOCK, BLOCK), 1) < 64

        def fold(b, carry):
            rows = pl.ds(pl.multiple_of(b * BLOCK, BLOCK), BLOCK)
            up = pl.ds(pl.multiple_of(b * 256, 256), 128)
            down = pl.ds(pl.multiple_of(b * 256 + 128, 128), 128)
            for p in range(pairs):
                for source, spot in ((dk_s, 128), (dv_s, 256)):
                    both = jnp.where(even, source[p, up, :], source[p, down, :])
                    dqkv_o[rows, p * 384 + spot : p * 384 + spot + 128] = both.astype(BF16)
            return carry

        lax.fori_loop(0, blocks, fold, 0)
        for p in range(pairs):
            part = t_dot(normed[...], dqkv_o[:, p * 384 : (p + 1) * 384]).astype(BF16)
            for half in range(2):
                piece = part[half * 256 : (half + 1) * 256].reshape(16, 16, 384)

                @pl.when(core == half)
                def _():
                    mine_o[:, p] = piece

                @pl.when(core != half)
                def _():
                    sent_o[:, p] = piece


def entry_kernel(blocks, left, x, right, dbr, gain, ln2, weight, d_qkv,
                 grad_o, left_o, right_o, small_o, w_s, x_s, ln_s, grad_s):
    r = pl.program_id(0)
    tiles = blocks // 2

    @pl.when(r == 0)
    def _():
        for p in range(PAIRS):
            for part in range(3):
                spot = part * 512 + p * 128
                to = p * 384 + part * 128
                w_s[:, to : to + 128] = weight[:, spot : spot + 128]
        for t in range(tiles):
            x_s[t * 256 : (t + 1) * 256, :] = two_blocks(left, x, right, t)
        ln_s[0:2, :] = jnp.zeros((2, D), F32)

    rows = pl.ds(pl.multiple_of(r * 256, 256), 256)
    d_n1 = dot_t(d_qkv[...], w_s[...])
    n1, inverse = normalize(x_s[rows, :].astype(F32))
    e = d_n1 * gain[...]
    mean_e = jnp.mean(e, axis=-1, keepdims=True)
    mean_en = jnp.mean(e * n1, axis=-1, keepdims=True)
    grad_s[rows, :] = dbr[...].astype(F32) + (e - mean_e - n1 * mean_en) * inverse
    ln_s[0:1, :] += jnp.sum(d_n1 * n1, axis=0, keepdims=True)
    ln_s[1:2, :] += jnp.sum(d_n1, axis=0, keepdims=True)

    @pl.when(r == tiles - 1)
    def _():
        inner = (blocks - 2) * BLOCK
        grad_o[...] = grad_s[HALO : HALO + inner, :]
        left_o[...] = grad_s[0:HALO, :].astype(BF16)
        right_o[...] = grad_s[HALO + inner :, :].astype(BF16)
        vectors = [ln_s[0:1, :], ln_s[1:2, :], ln2[0:1, :], ln2[1:2, :]]
        small_o[...] = jnp.concatenate(
            [v[:, c * 128 : (c + 1) * 128] for v in vectors for c in range(4)], axis=0
        )


def join_kernel(groups, *refs):
    mine, other, (out_m, out_o, result) = refs[:groups], refs[groups : 2 * groups], refs[2 * groups :]
    pairs = PAIRS // groups
    for g in range(groups):
        for p in range(pairs):
            value = mine[g][:, p].astype(F32) + other[g][:, p].astype(F32)
            result[:, g * pairs + p, :, 0:384] = value.astype(BF16)
    result[:, :, :, 384:512] = (out_m[...].astype(F32) + out_o[...].astype(F32)).astype(BF16)


def join_call(mine, other, out_m, out_o):
    vmem = pl.BlockSpec(memory_space=pltpu.VMEM)
    return pl.pallas_call(
        functools.partial(join_kernel, len(mine)),
        in_specs=[vmem] * (2 * len(mine) + 2),
        out_specs=vmem,
        out_shape=shape_of((16, 4, 16, 512), BF16),
        compiler_params=pltpu.CompilerParams(vmem_limit_bytes=VMEM_LIMIT),
        name="join",
    )(*mine, *other, out_m, out_o)


def whole(shape):
    return pl.BlockSpec(shape, lambda s, scal: (0,) * len(shape))


def shape_of(shape, dtype):
    return jax.ShapeDtypeStruct(shape, dtype)


def params():
    return pltpu.CompilerParams(
        dimension_semantics=("arbitrary",), vmem_limit_bytes=VMEM_LIMIT
    )


def attend_call(scal, left, x, right, seg, gain, shift, weight):
    rows = x.shape[0] + 2 * HALO
    blocks = rows // BLOCK
    at = lambda s, scal: (jnp.maximum(s - 1, 0), 0)
    at4 = lambda s, scal: (jnp.maximum(s - 1, 0), 0, 0, 0)
    return pl.pallas_call(
        functools.partial(attend_kernel, blocks),
        grid_spec=pltpu.PrefetchScalarGridSpec(
            num_scalar_prefetch=1,
            grid=(blocks + 1,),
            in_specs=[
                whole((2 * HALO, D)), whole(x.shape), whole((2 * HALO, D)), whole(seg.shape),
                whole((1, D)), whole((1, D)), whole(weight.shape),
            ],
            out_specs=[
                pl.BlockSpec((BLOCK, D), at),
                pl.BlockSpec((BLOCK, 3 * D), at),
                pl.BlockSpec((BLOCK, D), at),
                pl.BlockSpec((1, PAIRS, BLOCK, 1280), at4),
                pl.BlockSpec((BLOCK, D), at),
            ],
            scratch_shapes=[
                pltpu.VMEM((rows, D), BF16),
                pltpu.VMEM((rows, 3 * D), BF16),
                pltpu.VMEM((PAIRS, blocks * 256, 128), BF16),
                pltpu.VMEM((PAIRS, blocks * 256, 256), BF16),
            ],
        ),
        out_shape=[
            shape_of((rows, D), BF16),
            shape_of((rows, 3 * D), BF16),
            shape_of((rows, D), BF16),
            shape_of((blocks, PAIRS, BLOCK, 1280), BF16),
            shape_of((rows, D), BF16),
        ],
        compiler_params=params(),
        cost_estimate=pl.CostEstimate(flops=8 * 10**9, bytes_accessed=25 * 10**6, transcendentals=4 * 10**6),
        name="attend",
    )(scal, left, x, right, seg, gain, shift, weight)


def feed_call(scal, att, left, x, right, cot, out_w, up_w, down_w, gain, shift):
    rows = att.shape[0]
    blocks = rows // BLOCK
    half = (16, 4, 16, 1024)
    return pl.pallas_call(
        functools.partial(feed_kernel, blocks),
        grid_spec=pltpu.PrefetchScalarGridSpec(
            num_scalar_prefetch=1,
            grid=(FF // 512,),
            in_specs=[
                whole((rows, D)),
                whole((2 * HALO, D)), whole(x.shape), whole((2 * HALO, D)), whole(x.shape),
                whole((D, D)),
                pl.BlockSpec((D, 512), lambda s, scal: (0, s)),
                pl.BlockSpec((512, D), lambda s, scal: (s, 0)),
                whole((1, D)), whole((1, D)),
            ],
            out_specs=[
                whole((rows, D)), whole((rows, 128)), whole((rows, D)), whole((rows, D)),
                pl.BlockSpec((rows, 512), lambda s, scal: (0, s)), whole(half), whole(half),
            ],
            scratch_shapes=[
                pltpu.VMEM((rows, D), BF16),
                pltpu.VMEM((rows, 512), BF16),
                pltpu.VMEM((FF // 512, rows, 512), BF16),
                pltpu.VMEM((FF // 512, D, 512), BF16),
            ] + [pltpu.VMEM((256, 512), F32)] * 4,
        ),
        out_shape=[
            shape_of((rows, D), BF16),
            shape_of((rows, 128), F32),
            shape_of((rows, D), BF16),
            shape_of((rows, D), BF16),
            shape_of((rows, FF), BF16),
            shape_of(half, BF16),
            shape_of(half, BF16),
        ],
        compiler_params=params(),
        cost_estimate=pl.CostEstimate(flops=16 * 10**9, bytes_accessed=25 * 10**6, transcendentals=3 * 10**6),
        name="feed",
    )(scal, att, left, x, right, cot, out_w, up_w, down_w, gain, shift)


def middle_call(scal, base, rstd, dn2, cot, att, inv, out_w, gain):
    rows = att.shape[0]
    blocks = rows // BLOCK
    part = (16, 4, 16, 128)
    tile = pl.BlockSpec((256, D), lambda s, scal: (s, 0))
    return pl.pallas_call(
        functools.partial(middle_kernel, 2 * blocks),
        grid_spec=pltpu.PrefetchScalarGridSpec(
            num_scalar_prefetch=1,
            grid=(rows // 256,),
            in_specs=[
                tile, pl.BlockSpec((256, 128), lambda s, scal: (s, 0)), tile, tile, tile, tile,
                whole((D, D)), whole((1, D)),
            ],
            out_specs=[
                tile, pl.BlockSpec((256, 2 * D), lambda s, scal: (s, 0)),
                whole(part), whole(part), whole((2, D)),
            ],
            scratch_shapes=[pltpu.VMEM((D, D), F32)],
        ),
        out_shape=[
            shape_of((rows, D), BF16), shape_of((rows, 2 * D), BF16),
            shape_of(part, BF16), shape_of(part, BF16), shape_of((2, D), F32),
        ],
        compiler_params=params(),
        cost_estimate=pl.CostEstimate(flops=2 * 10**9, bytes_accessed=15 * 10**6, transcendentals=0),
        name="middle",
    )(scal, base, rstd, dn2, cot, att, inv, out_w, gain)


def back_call(scal, probs, a, qkv, normed, group, groups):
    rows = qkv.shape[0]
    blocks = rows // BLOCK
    pairs = PAIRS // groups
    width = pairs * 128
    half = (16, pairs, 16, 384)
    last = blocks - 1
    return pl.pallas_call(
        functools.partial(back_kernel, blocks, pairs),
        grid_spec=pltpu.PrefetchScalarGridSpec(
            num_scalar_prefetch=1,
            grid=(blocks + 1,),
            in_specs=[
                pl.BlockSpec((1, pairs, BLOCK, 1280), lambda s, scal: (jnp.minimum(s, last), group, 0, 0)),
                pl.BlockSpec((BLOCK, pairs * 256), lambda s, scal: (jnp.minimum(s, last), group)),
                pl.BlockSpec((rows, width), lambda s, scal: (0, group)),
                pl.BlockSpec((rows, width), lambda s, scal: (0, groups + group)),
                pl.BlockSpec((rows, width), lambda s, scal: (0, 2 * groups + group)),
                whole((rows, D)),
            ],
            out_specs=[whole((rows, pairs * 384)), whole(half), whole(half)],
            scratch_shapes=[
                pltpu.VMEM((pairs, blocks * 256, 128), BF16),
                pltpu.VMEM((pairs, blocks * 256, 256), BF16),
                pltpu.VMEM((pairs, blocks * 256, 128), F32),
                pltpu.VMEM((pairs, blocks * 256, 128), F32),
            ],
        ),
        out_shape=[shape_of((rows, pairs * 384), BF16), shape_of(half, BF16), shape_of(half, BF16)],
        compiler_params=params(),
        cost_estimate=pl.CostEstimate(flops=12 * 10**9 // groups, bytes_accessed=20 * 10**6 // groups, transcendentals=0),
        name="back",
    )(scal, probs, a, qkv, qkv, qkv, normed)


def entry_call(left, x, right, dbr, gain, ln2, weight, d_qkv):
    rows = dbr.shape[0]
    fixed = lambda v: pl.BlockSpec(v.shape, lambda s: (0,) * len(v.shape))
    at = lambda s: (s, 0)
    edge = shape_of((HALO, D), BF16)
    outs = [shape_of(x.shape, F32), edge, edge, shape_of((16, 128), F32)]
    return pl.pallas_call(
        functools.partial(entry_kernel, rows // BLOCK),
        grid=(rows // 256,),
        in_specs=[
            fixed(left), fixed(x), fixed(right), pl.BlockSpec((256, D), at), fixed(gain), fixed(ln2),
            fixed(weight), pl.BlockSpec((256, 3 * D), at),
        ],
        out_specs=[fixed(v) for v in outs],
        out_shape=outs,
        scratch_shapes=[
            pltpu.VMEM((D, 3 * D), BF16), pltpu.VMEM((rows, D), BF16), pltpu.VMEM((8, D), F32),
            pltpu.VMEM((rows, D), F32),
        ],
        compiler_params=params(),
        cost_estimate=pl.CostEstimate(flops=2 * 10**9, bytes_accessed=15 * 10**6, transcendentals=0),
        name="entry",
    )(left, x, right, dbr, gain, ln2, weight, d_qkv)


def other_core(value):
    return lax.ppermute(value, "core", [(0, 1), (1, 0)])


def all_shares(value, groups):
    parts = lax.all_to_all(value, ("rows", "x"), 0, 0, tiled=True)
    return jnp.sum(parts.astype(F32), axis=0).astype(BF16)


def gather_shares(share, groups):
    copies = jnp.broadcast_to(share[None], (groups, *share.shape))
    return lax.all_to_all(copies, ("rows", "x"), 0, 0, tiled=True)


def per_device(
    inputs, qkv_weight, out_weight, up_weight, down_weight, norm1_gain, norm1_shift,
    norm2_gain, norm2_shift, segment_ids, item_steps, gen_rank, out_grad,
):
    x = inputs[0]
    positions = x.shape[0]
    blocks = (positions + 2 * HALO) // BLOCK
    chips = lax.axis_size("rows") * lax.axis_size("x")
    seq_parts = lax.axis_size("x") * lax.axis_size("core")
    seq = ("x", "core")
    to_right = [(i, (i + 1) % seq_parts) for i in range(seq_parts)]
    to_left = [((i + 1) % seq_parts, i) for i in range(seq_parts)]

    place = jnp.stack([lax.axis_index(seq), lax.axis_index("core")]).astype(jnp.int32)
    scal, seg_rows, cot, send_l, send_r = prepare_call(
        place, segment_ids, item_steps, gen_rank, x, out_grad[0]
    )
    left = lax.ppermute(send_r, seq, to_right)
    right = lax.ppermute(send_l, seq, to_left)

    gain1, shift1 = norm1_gain.reshape(1, D), norm1_shift.reshape(1, D)
    gain2, shift2 = norm2_gain.reshape(1, D), norm2_shift.reshape(1, D)
    normed1, qkv, att, probs, inv = attend_call(
        scal, left, x, right, seg_rows, gain1, shift1, qkv_weight
    )
    base2, rstd2, cot_w, dn2, act, mine_a, sent_a = feed_call(
        scal, att, left, x, right, cot, out_weight, up_weight, down_weight, gain2, shift2
    )
    got_a = other_core(sent_a)
    d_branch, a, mine_o, sent_o, ln2 = middle_call(
        scal, base2, rstd2, dn2, cot_w, att, inv, out_weight, gain2
    )
    tie = lax.optimization_barrier
    half_a = (mine_a.astype(F32) + got_a.astype(F32)).astype(BF16)
    a, half_a = tie((a, half_a))
    share_a = all_shares(half_a.reshape(chips, -1, 1024), chips)
    d_qkv, mine_b, sent_b = back_call(scal, probs, a, qkv, normed1, 0, 1)
    share_a, sent_b, sent_o = tie((share_a, sent_b, sent_o))
    half_b = join_call((mine_b,), (other_core(sent_b),), mine_o, other_core(sent_o))
    d_branch, half_b = tie((d_branch, half_b))
    share_b = all_shares(half_b.reshape(chips, -1, 512), chips)
    grad, grad_l, grad_r, small = entry_call(
        left, x, right, d_branch, gain1, ln2, qkv_weight, d_qkv
    )
    small = small + other_core(small)
    share = jnp.concatenate([share_a, share_b, small.astype(BF16)], axis=1)
    att, share = tie((att, share))
    near = gather_shares(share, chips)
    out, out_l, out_r = finish_call(att, left, x, right, act, out_weight, down_weight)
    edge_l = jnp.concatenate([out_l, grad_l], axis=0)
    edge_r = jnp.concatenate([out_r, grad_r], axis=0)
    edge_l, edge_r, near = tie((edge_l, edge_r, near))
    far = other_core(near)
    from_r = lax.ppermute(edge_l, seq, to_left)
    from_l = lax.ppermute(edge_r, seq, to_right)
    output, input_grad = patch_call(scal, out, grad, seg_rows, from_l, from_r)
    vectors = jnp.sum(near[:, :, 1536:].astype(F32), axis=0).reshape(4, D)
    grad_down, grad_up, grad_out, grad_qkv = unpack_call(
        scal, 2 * blocks, near.reshape(16, 4, 16, 1664), far.reshape(16, 4, 16, 1664)
    )
    return (
        output[None], input_grad[None], grad_qkv, grad_out, grad_up, grad_down,
        vectors[0], vectors[1], vectors[2], vectors[3],
    )


def solution(mesh):
    rows = mesh.devices.shape[0]
    parts = mesh.devices.shape[1]
    split = Mesh(mesh.devices.reshape(rows, parts // 2, 2), ("rows", "x", "core"))
    seq = ("x", "core")
    return jax.shard_map(
        per_device,
        mesh=split,
        in_specs=(
            P("rows", seq, None), P(), P(), P(), P(), P(), P(), P(), P(),
            P("rows", None), P("rows", None), P("rows", seq), P("rows", seq, None),
        ),
        out_specs=(
            P("rows", seq, None), P("rows", seq, None),
            P(), P(), P(), P(), P(), P(), P(), P(),
        ),
        check_vma=False,
    )
```

```python
import functools

import jax
import jax.numpy as jnp
from jax import lax
from jax.experimental import pallas as pl
from jax.experimental.pallas import tpu as pltpu
from jax.sharding import Mesh
from jax.sharding import PartitionSpec as P

D = 512
HEADS = 8
PAIRS = HEADS // 2
FF = 2048
EPS = 1e-05
HALO = 128
BLOCK = 128
BF16 = jnp.bfloat16
F32 = jnp.float32
VMEM_LIMIT = 58 * 1024 * 1024
HIGH, CORE, DROP_L, DROP_R = 16, 32, 33, 34


def dot(a, b):
    return lax.dot_general(a, b, (((1,), (0,)), ((), ())), preferred_element_type=F32)


def dot_t(a, b):
    return lax.dot_general(a, b, (((1,), (1,)), ((), ())), preferred_element_type=F32)


def t_dot(a, b):
    return lax.dot_general(a, b, (((0,), (0,)), ((), ())), preferred_element_type=F32)


def normalize(value):
    center = jnp.mean(value, axis=-1, keepdims=True)
    centred = value - center
    spread = jnp.mean(centred * centred, axis=-1, keepdims=True)
    inverse = lax.rsqrt(spread + EPS)
    return centred * inverse, inverse


def two_blocks(left, middle, right, tile):
    last = 1 + middle.shape[0] // BLOCK
    parts = []
    for block in (2 * tile, 2 * tile + 1):
        if block == 0:
            parts.append(left[...])
        elif block == last:
            parts.append(right[...])
        else:
            parts.append(middle[(block - 1) * BLOCK : block * BLOCK, :])
    return jnp.concatenate(parts, axis=0)


def split_pairs(keys, values, kc, vx, block):
    lane = lax.broadcasted_iota(jnp.int32, (BLOCK, BLOCK), 1)
    even = lane < 64
    zero = jnp.zeros((BLOCK, BLOCK), BF16)
    ones_even = even.astype(F32).astype(BF16)
    ones_odd = (~even).astype(F32).astype(BF16)
    base = block * 256
    for p in range(PAIRS):
        k = keys[:, p * 128 : (p + 1) * 128]
        v = values[:, p * 128 : (p + 1) * 128]
        kc[p, pl.ds(base, 128), 0:128] = jnp.where(even, k, zero)
        kc[p, pl.ds(base + 128, 128), 0:128] = jnp.where(even, zero, k)
        vx[p, pl.ds(base, 128), 0:128] = jnp.where(even, v, zero)
        vx[p, pl.ds(base + 128, 128), 0:128] = jnp.where(even, zero, v)
        vx[p, pl.ds(base, 128), 128:256] = ones_even
        vx[p, pl.ds(base + 128, 128), 128:256] = ones_odd
        if kc.shape[2] == 256:
            minus = jnp.where(lax.rem(lane, 64) < 3, -1.0, 0.0)
            kc[p, pl.ds(base, 128), 128:256] = jnp.where(even, minus, 0.0).astype(BF16)
            kc[p, pl.ds(base + 128, 128), 128:256] = jnp.where(even, 0.0, minus).astype(BF16)


def mask_rows(seg, row, low, n):
    seg_q = column(seg[row].astype(F32))
    return [
        jnp.where(seg_q == jnp.broadcast_to(seg[low + t].astype(F32), (BLOCK, BLOCK)), 0.0, -1e30)
        for t in range(n)
    ]


def column(row):
    return jnp.transpose(jnp.broadcast_to(row, (BLOCK, BLOCK)))


def keep_rows(values, mask):
    return jnp.concatenate(
        [
            jnp.where(mask, values[:, c * 128 : (c + 1) * 128].astype(F32), 0.0).astype(BF16)
            for c in range(D // 128)
        ],
        axis=1,
    )


def prepare_kernel(inner, place, segments, steps, rank, out_grad, scal_o, seg_o, cot_o, left_o, right_o, part_s):
    seq = place[0]
    row_blocks = segments.shape[1] // BLOCK
    blocks = inner + 2
    rows = []
    for b in range(blocks):
        at = seq * inner + b - 1
        if b == 0:
            at = jnp.maximum(at, 0)
        if b == blocks - 1:
            at = jnp.minimum(at, row_blocks - 1)
        row = segments[0:1, pl.ds(pl.multiple_of(at * BLOCK, BLOCK), BLOCK)]
        if b == 0:
            row = jnp.where(seq > 0, row, -1)
        if b == blocks - 1:
            row = jnp.where(seq * inner + inner < row_blocks, row, 1000)
        rows.append(row)
        seg_o[b] = row
    window = jnp.concatenate(rows, axis=0)
    local = window[1 : inner + 1]
    first, last = window[:, 0:1], window[:, BLOCK - 1 : BLOCK]
    below = jnp.zeros(window.shape, F32)
    upto = jnp.zeros(window.shape, F32)
    for row in rows:
        below += (row < first).astype(F32)
        upto += (row <= last).astype(F32)
    part_s[...] = jnp.zeros(part_s.shape, F32)
    part_s[0:blocks, :] = below
    part_s[HIGH : HIGH + blocks, :] = upto
    counts = dot_t(jnp.ones((8, BLOCK), BF16), part_s[...].astype(BF16))[0:1]

    def border(before, after):
        value = before[-1:, BLOCK - 1 : BLOCK]
        across = value == after[0:1, 0:1]
        sizes = [jnp.sum((part == value).astype(F32), axis=(0, 1), keepdims=True) for part in (before, after)]
        return value, across, sizes[0] >= sizes[1]

    value_l, across_l, to_left_l = border(rows[0], local)
    value_r, across_r, to_left_r = border(local, rows[-1])
    drop_l = jnp.where(across_l & to_left_l, value_l, -2)
    drop_r = jnp.where(across_r & jnp.logical_not(to_left_r), value_r, -2)
    lane = lax.broadcasted_iota(jnp.int32, (1, BLOCK), 1)
    at_block = jnp.floor(jnp.where(lane >= HIGH, counts - 1.0, counts) * (1.0 / BLOCK)).astype(jnp.int32)
    at_block = jnp.where(lane == CORE, place[1], at_block)
    at_block = jnp.where(lane == DROP_L, drop_l, at_block)
    scal_o[...] = jnp.where(lane == DROP_R, drop_r, at_block)

    token = jnp.zeros(local.shape, jnp.int32)
    for slot in range(steps.shape[1]):
        token = jnp.where(local == slot, steps[0, slot], token)
    for b in range(inner):
        part = slice(b * BLOCK, (b + 1) * BLOCK)
        keep = rank[0:1, part] >= token[b : b + 1]
        seg = rows[b + 1]
        own = (seg != drop_l) & (seg != drop_r)
        values = out_grad[part, :]
        cot_o[part, :] = keep_rows(values, column((keep & own).astype(F32)) > 0.5)
        if b == 0:
            left_o[...] = keep_rows(values, column((keep & (seg == drop_l)).astype(F32)) > 0.5)
        if b == inner - 1:
            right_o[...] = keep_rows(values, column((keep & (seg == drop_r)).astype(F32)) > 0.5)


def prepare_call(place, segments, steps, rank, out_grad):
    inner = out_grad.shape[0] // BLOCK
    vmem = pl.BlockSpec(memory_space=pltpu.VMEM)
    smem = pl.BlockSpec(memory_space=pltpu.SMEM)
    return pl.pallas_call(
        functools.partial(prepare_kernel, inner),
        in_specs=[smem, vmem, smem, vmem, vmem],
        out_specs=[vmem] * 5,
        out_shape=[
            shape_of((1, BLOCK), jnp.int32),
            shape_of((inner + 2, 1, BLOCK), jnp.int32),
            shape_of(out_grad.shape, BF16),
            shape_of((HALO, D), BF16),
            shape_of((HALO, D), BF16),
        ],
        scratch_shapes=[pltpu.VMEM((BLOCK, BLOCK), F32)],
        compiler_params=pltpu.CompilerParams(vmem_limit_bytes=VMEM_LIMIT),
        cost_estimate=pl.CostEstimate(flops=10**6, bytes_accessed=4 * 10**6, transcendentals=0),
        name="prepare",
    )(place, segments, steps, rank, out_grad)


def patch_kernel(blocks, scal, out, grad, seg, left, right, out_o, grad_o):
    step = pl.program_id(0)
    drop_l, drop_r = scal[0, DROP_L], scal[0, DROP_R]
    row = seg[0]
    drop = jnp.where(step == 0, drop_l, drop_r)
    lost = column((row == drop).astype(F32)) > 0.5
    for c in range(D // 128):
        cols = slice(c * 128, (c + 1) * 128)
        for mine, start, result in ((out, 0, out_o), (grad, HALO, grad_o)):
            part = slice(start, start + HALO)
            other = jnp.where(step == 0, left[part, cols].astype(F32), right[part, cols].astype(F32))
            value = jnp.where(lost, other, mine[:, cols].astype(F32))
            result[:, cols] = value.astype(result.dtype)


def patch_call(scal, out, grad, seg, left, right):
    inner = out.shape[0] // BLOCK
    block = lambda s, scal: (s * (inner - 1), 0)
    return pl.pallas_call(
        functools.partial(patch_kernel, inner + 2),
        grid_spec=pltpu.PrefetchScalarGridSpec(
            num_scalar_prefetch=1,
            grid=(2,),
            in_specs=[
                pl.BlockSpec((BLOCK, D), block),
                pl.BlockSpec((BLOCK, D), block),
                pl.BlockSpec((1, 1, BLOCK), lambda s, scal: (1 + s * (inner - 1), 0, 0)),
                whole((2 * HALO, D)), whole((2 * HALO, D)),
            ],
            out_specs=[pl.BlockSpec((BLOCK, D), block), pl.BlockSpec((BLOCK, D), block)],
        ),
        out_shape=[shape_of(out.shape, out.dtype), shape_of(grad.shape, grad.dtype)],
        input_output_aliases={1: 0, 2: 1},
        compiler_params=params(),
        name="patch",
    )(scal, out, grad, seg, left, right)


def unpack_feed(a, down_o, up_o):
    rows = a.shape[0] * 16
    down_o[...] = a[:, :, :, 0:512].astype(F32).reshape(4 * rows, 512)
    for c in range(4):
        up_o[:, c * 512 : (c + 1) * 512] = a[:, c, :, 512:1024].astype(F32).reshape(rows, 512)


def unpack_rest(a, out_o, qkv_o, small_o=None):
    rows = a.shape[0] * 16
    for c in range(4):
        value = a[:, c, :, 0:512].astype(F32).reshape(rows, 512)
        for part in range(3):
            spot = part * 512 + c * 128
            qkv_o[:, spot : spot + 128] = value[:, part * 128 : (part + 1) * 128]
        out_o[:, c * 128 : (c + 1) * 128] = value[:, 384:512]
    if small_o is not None:
        part = jnp.sum(a[:, :, :, 512:640].astype(F32), axis=(0, 1))

        @pl.when(pl.program_id(0) == 0)
        def _():
            small_o[...] = part

        @pl.when(pl.program_id(0) > 0)
        def _():
            small_o[...] += part


def unpack_call(body, shapes, scal, value, before=(), steps=4, small=None):
    def out(s, scal):
        half = scal[0, CORE] if not before else 1 - scal[0, CORE]
        return (half * steps + s, 0)

    def kernel(scal, a, *refs):
        body(a, *refs[len(before) :])

    extra = [] if small is None else [small]
    return pl.pallas_call(
        kernel,
        grid_spec=pltpu.PrefetchScalarGridSpec(
            num_scalar_prefetch=1,
            grid=(steps,),
            in_specs=[pl.BlockSpec((16 // steps, *value.shape[1:]), lambda s, scal: (s, 0, 0, 0))]
            + [pl.BlockSpec(memory_space=pl.ANY)] * len(before),
            out_specs=[pl.BlockSpec((rows // (2 * steps), cols), out) for rows, cols in shapes]
            + [whole(v) for v in extra],
        ),
        out_shape=[shape_of(shape, F32) for shape in (*shapes, *extra)],
        input_output_aliases={2 + k: k for k in range(len(before))},
        compiler_params=params(),
        cost_estimate=pl.CostEstimate(flops=10**6, bytes_accessed=10 * 10**6, transcendentals=0),
        name="unpack",
    )(scal, value, *before)


def attend_kernel(blocks, scal, left, x, right, seg, gain, shift, weight,
                  normed_o, qkv_o, att_o, lse_o, normed_s, qkv_s, kc, vx):
    step = pl.program_id(0)
    tiles = blocks // 2

    @pl.when(step == 0)
    def _():
        for r in range(tiles + 1):
            if r < tiles:
                base, _ = normalize(two_blocks(left, x, right, r).astype(F32))
                normed_s[r * 256 : (r + 1) * 256, :] = (base * gain[...] + shift[...]).astype(BF16)
            if r > 0:
                rows = slice((r - 1) * 256, r * 256)
                qkv = dot(normed_s[rows, :], weight[...]).astype(BF16)
                qkv_s[rows, :] = qkv
                for half in range(2):
                    part = qkv[half * 128 : (half + 1) * 128]
                    split_pairs(part[:, 512:1024], part[:, 1024:1536], kc, vx, 2 * (r - 1) + half)

    @pl.when(step > 0)
    def _():
        two = pl.ds(pl.multiple_of((step - 1) * 256, 256), 256)
        normed_o[...] = normed_s[two, :]
        qkv_o[...] = qkv_s[two, :]
        lane = lax.broadcasted_iota(jnp.int32, (BLOCK, BLOCK), 1)
        place = lax.rem(lane, 64)
        for h in range(2):
            i = 2 * (step - 1) + h
            rows = pl.ds(pl.multiple_of(i * BLOCK, BLOCK), BLOCK)
            part = slice(h * BLOCK, (h + 1) * BLOCK)
            low = scal[0, i]
            n_keys = scal[0, HIGH + i] - low + 1
            first = pl.multiple_of(low * 256, 256)

            def attend(n):
                bias = mask_rows(seg, i, low, n)
                def pair(p, carry):
                    cols = pl.ds(pl.multiple_of(p * 128, 128), 128)
                    q = qkv_s[rows, cols] * jnp.asarray(0.125, BF16)
                    scores = dot_t(q, kc[p, pl.ds(first, n * 256), :])
                    tiles_s = [
                        [scores[:, t * 256 + o * 128 : t * 256 + o * 128 + 128] + bias[t] for t in range(n)]
                        for o in range(2)
                    ]
                    highest = [
                        jnp.max(functools.reduce(jnp.maximum, tiles_s[o]), axis=-1, keepdims=True)
                        for o in range(2)
                    ]
                    pieces = []
                    for t in range(n):
                        for o in range(2):
                            pieces.append(jnp.exp(tiles_s[o][t] - highest[o]).astype(BF16))
                    mixed = dot(jnp.concatenate(pieces, axis=1), vx[p, pl.ds(first, n * 256), :])
                    total = mixed[:, 128:256]
                    att_o[part, cols] = (mixed[:, 0:128] * (1.0 / total)).astype(BF16)
                    lse = jnp.where(lane < 64, highest[0], highest[1]) + jnp.log(total)
                    top = lse.astype(BF16).astype(F32)
                    rest = lse - top
                    second = rest.astype(BF16).astype(F32)
                    third = jnp.where(place == 2, rest - second, 0.0)
                    lse_o[part, cols] = jnp.where(
                        place == 0, top, jnp.where(place == 1, second, third)
                    ).astype(BF16)
                    return carry

                lax.fori_loop(0, PAIRS, pair, 0, unroll=PAIRS)

            for n in range(1, 6):
                pl.when(n_keys == n)(functools.partial(attend, n))


def gelu_both(v):
    c = 0.7978845608028654
    square = v * v
    inner = c + (0.044715 * c) * square
    gate = 0.5 + 0.5 * jnp.tanh(v * inner)
    act = v * gate
    slope = gate + act * ((1.0 - gate) * (6.0 * inner - 4.0 * c))
    return act, slope


def feed_kernel(blocks, scal, att, left, x, right, cot_l, cot, cot_r, out_w, up_w, down_w, gain, shift,
                base_o, rstd_o, cot_o, dn2_o, act_o, mine_o, sent_o,
                base_s, rstd_s, cot_s, mine_s, sent_s, sems, n2_s, act_s, dpre_s, up_s, *stage_s):
    f = pl.program_id(0)
    steps = FF // 512
    tiles = blocks // 2
    core = scal[0, CORE]

    def early():
        return [
            pltpu.make_async_copy(base_s, base_o, sems.at[0]),
            pltpu.make_async_copy(rstd_s, rstd_o, sems.at[1]),
            pltpu.make_async_copy(cot_s, cot_o, sems.at[2]),
        ]

    def down_copy(k, from_s, to_o):
        spot = (slice((k % 2) * 8, (k % 2) * 8 + 8), slice(None), slice(None), slice(0, 512))
        return pltpu.make_async_copy(from_s.at[spot], to_o.at[spot], sems.at[3 + k])

    def up_copies(k):
        spot = (slice(None), slice(k, k + 1), slice(None), slice(512, 1024))
        return [
            pltpu.make_async_copy(mine_s.at[spot], mine_o.at[spot], sems.at[3 + steps + k]),
            pltpu.make_async_copy(sent_s.at[spot], sent_o.at[spot], sems.at[3 + 2 * steps + k]),
        ]

    @pl.when(f == 0)
    def _():
        for r in range(tiles):
            rows = slice(r * 256, (r + 1) * 256)
            cot_s[rows, :] = two_blocks(cot_l, cot, cot_r, r)
            mid = two_blocks(left, x, right, r).astype(F32) + dot(att[rows, :], out_w[...])
            base, inverse = normalize(mid)
            base_s[rows, :] = base.astype(BF16)
            rstd_s[rows, :] = jnp.broadcast_to(inverse, (256, 128))
            n2_s[rows, :] = (base * gain[...] + shift[...]).astype(BF16)
        for copy in early():
            copy.start()

    up_s[f] = up_w[...]
    for r in range(tiles + 1):
        if r < tiles:
            rows = slice(r * 256, (r + 1) * 256)
            stage_s[r % 2][...] = dot(n2_s[rows, :], up_w[...])
            stage_s[2 + r % 2][...] = dot_t(cot_s[rows, :], down_w[...])
        if r > 0:
            rows = slice((r - 1) * 256, r * 256)
            act, slope = gelu_both(stage_s[(r - 1) % 2][...])
            act_s[rows, :] = act.astype(BF16)
            dpre_s[f, rows, :] = (slope * stage_s[2 + (r - 1) % 2][...]).astype(BF16)
    act_o[...] = act_s[...]
    grad_down = t_dot(act_s[...], cot_s[...]).astype(BF16).reshape(8, 4, 16, 512)
    grad_up = t_dot(n2_s[...], dpre_s[f]).astype(BF16).reshape(2, 16, 1, 16, 512)

    for k in range(steps):

        @pl.when((f == k) & (core == k // 2))
        def _():
            mine_s[(k % 2) * 8 : (k % 2) * 8 + 8, :, :, 0:512] = grad_down
            down_copy(k, mine_s, mine_o).start()

        @pl.when((f == k) & (core != k // 2))
        def _():
            sent_s[(k % 2) * 8 : (k % 2) * 8 + 8, :, :, 0:512] = grad_down
            down_copy(k, sent_s, sent_o).start()

    for half in range(2):

        @pl.when(core == half)
        def _():
            mine_s[:, pl.ds(f, 1), :, 512:1024] = grad_up[half]
            sent_s[:, pl.ds(f, 1), :, 512:1024] = grad_up[1 - half]

    for k in range(steps):

        @pl.when(f == k)
        def _():
            for copy in up_copies(k):
                copy.start()

    @pl.when(f == steps - 1)
    def _():
        def turn(r, carry):
            rows = pl.ds(pl.multiple_of(r * 256, 256), 256)
            d_pre = jnp.concatenate([dpre_s[k, rows, :] for k in range(steps)], axis=1)
            up = jnp.concatenate([up_s[k] for k in range(steps)], axis=1)
            dn2_o[rows, :] = dot_t(d_pre, up).astype(BF16)
            return carry

        lax.fori_loop(0, tiles, turn, 0)
        for copy in early():
            copy.wait()
        for k in range(steps):
            pl.when(core == k // 2)(lambda: down_copy(k, mine_s, mine_o).wait())
            pl.when(core != k // 2)(lambda: down_copy(k, sent_s, sent_o).wait())
            for copy in up_copies(k):
                copy.wait()


def finish_kernel(blocks, att, left, x, right, act, out_w, down_w, out_o, left_o, right_o):
    tiles = blocks // 2
    for r in range(tiles):
        rows = slice(r * 256, (r + 1) * 256)
        mid = two_blocks(left, x, right, r).astype(F32) + dot(att[rows, :], out_w[...])
        total = (mid + dot(act[rows, :], down_w[...])).astype(BF16)
        for h in range(2):
            block = 2 * r + h
            part = total[h * BLOCK : (h + 1) * BLOCK]
            if block == 0:
                left_o[...] = part
            elif block == blocks - 1:
                right_o[...] = part
            else:
                out_o[(block - 1) * BLOCK : block * BLOCK, :] = part


def finish_call(att, left, x, right, act, out_w, down_w):
    rows = att.shape[0]
    vmem = pl.BlockSpec(memory_space=pltpu.VMEM)
    edge = shape_of((HALO, D), BF16)
    return pl.pallas_call(
        functools.partial(finish_kernel, rows // BLOCK),
        in_specs=[vmem] * 7,
        out_specs=[vmem] * 3,
        out_shape=[shape_of(x.shape, BF16), edge, edge],
        compiler_params=pltpu.CompilerParams(vmem_limit_bytes=VMEM_LIMIT),
        cost_estimate=pl.CostEstimate(flops=4 * 10**9, bytes_accessed=12 * 10**6, transcendentals=0),
        name="finish",
    )(att, left, x, right, act, out_w, down_w)


def middle_kernel(scal, base, rstd, dn2, cot, att, out_w, gain,
                  dbr_o, a_o, mine_o, sent_o, ln_o, sum_s):
    r = pl.program_id(0)
    core = scal[0, CORE]

    @pl.when(r == 0)
    def _():
        sum_s[...] = jnp.zeros(sum_s.shape, F32)
        ln_o[...] = jnp.zeros(ln_o.shape, F32)

    n2 = base[...].astype(F32)
    inverse = jnp.concatenate([rstd[...]] * 4, axis=1)
    d_n2 = dn2[...].astype(F32)
    e = d_n2 * gain[...]
    scaled = d_n2 * n2
    mean_e = jnp.mean(e, axis=-1, keepdims=True)
    mean_en = jnp.mean(e * n2, axis=-1, keepdims=True)
    d_mid = cot[...].astype(F32) + (e - mean_e - n2 * mean_en) * inverse
    branch = d_mid.astype(BF16)
    dbr_o[...] = branch
    d_att = dot_t(branch, out_w[...])
    minus = -(d_att * att[...].astype(F32))
    for p in range(PAIRS):
        cols = slice(p * 128, (p + 1) * 128)
        a_o[:, p * 256 : p * 256 + 128] = d_att[:, cols].astype(BF16)
        a_o[:, p * 256 + 128 : p * 256 + 256] = minus[:, cols].astype(BF16)
    ln_o[0:1, :] += jnp.sum(scaled, axis=0, keepdims=True)
    ln_o[1:2, :] += jnp.sum(d_n2, axis=0, keepdims=True)
    sum_s[...] += t_dot(att[...], branch)

    @pl.when(r == pl.num_programs(0) - 1)
    def _():
        for half in range(2):
            part = sum_s[half * 256 : (half + 1) * 256, :].astype(BF16).reshape(16, 16, 512)

            @pl.when(core == half)
            def _():
                for c in range(4):
                    mine_o[:, c] = part[:, :, c * 128 : (c + 1) * 128]

            @pl.when(core != half)
            def _():
                for c in range(4):
                    sent_o[:, c] = part[:, :, c * 128 : (c + 1) * 128]


def back_kernel(blocks, scal, a, lse, seg, qkv, normed, dqkv_o, mine_o, sent_o,
                q_s, kc, vx, dk_s, dv_s, bias_s, dqkv_s, normed_s):
    step = pl.program_id(0)
    core = scal[0, CORE]

    def rows_of(block, count=1):
        return pl.ds(pl.multiple_of(block * BLOCK, BLOCK), count * BLOCK)

    @pl.when(step < blocks // 2)
    def _():
        rows = rows_of(2 * step, 2)
        q_s[rows, :] = qkv[:, 0:512] * jnp.asarray(0.125, BF16)
        normed_s[rows, :] = normed[...]
        for h in range(2):
            part = slice(h * BLOCK, (h + 1) * BLOCK)
            split_pairs(qkv[part, 512:1024], qkv[part, 1024:1536], kc, vx, 2 * step + h)
        both = pl.ds(pl.multiple_of(step * 512, 512), 512)
        for p in range(PAIRS):
            dk_s[p, both, :] = jnp.zeros((512, 128), F32)
            dv_s[p, both, :] = jnp.zeros((512, 128), F32)

    @pl.when((step >= 1) & (step <= blocks // 2))
    def _():
        i = 2 * (step - 1)
        rows = rows_of(i, 2)
        low = scal[0, i]
        n_keys = scal[0, HIGH + i + 1] - low + 1
        keys_at = pl.multiple_of(low * 256, 256)
        seg_q = [jnp.broadcast_to(seg[i + h].astype(F32), (BLOCK, BLOCK)) for h in range(2)]

        def back(n):
            keys = pl.ds(keys_at, n * 256)
            for t in range(n):
                seg_k = column(seg[low + t].astype(F32))
                for h in range(2):
                    cols = slice(h * BLOCK, (h + 1) * BLOCK)
                    bias_s[t * BLOCK : (t + 1) * BLOCK, cols] = jnp.where(seg_k == seg_q[h], 0.0, -1e30)

            def pair(p, carry):
                cols = pl.ds(pl.multiple_of(p * 128, 128), 128)
                q = q_s[rows, cols]
                d_out = a[:, pl.ds(pl.multiple_of(p * 256, 256), 128)]
                scores = dot_t(kc[p, keys, :], jnp.concatenate([q, lse[:, cols]], axis=1))
                d_probs = dot_t(vx[p, keys, :], a[:, pl.ds(pl.multiple_of(p * 256, 256), 256)])
                parts, d_parts = [], []
                for t in range(n):
                    bias = bias_s[t * BLOCK : (t + 1) * BLOCK, :]
                    for h in range(2):
                        part = slice((2 * t + h) * BLOCK, (2 * t + h + 1) * BLOCK)
                        probs = jnp.exp(scores[part] + bias)
                        parts.append(probs.astype(BF16))
                        d_parts.append((probs * d_probs[part]).astype(BF16))
                d_scores = jnp.concatenate(d_parts, axis=0)
                dk_s[p, keys, :] += dot(d_scores, q)
                dv_s[p, keys, :] += dot(jnp.concatenate(parts, axis=0), d_out)
                d_q = t_dot(d_scores, kc[p, keys, 0:128]) * 0.125
                dqkv_s[rows, pl.ds(pl.multiple_of(p * 384, 128), 128)] = d_q.astype(BF16)
                return carry

            lax.fori_loop(0, PAIRS, pair, 0, unroll=2)

        for n in range(1, 7):
            pl.when(n_keys == n)(functools.partial(back, n))

    @pl.when(step >= 2)
    def _():
        even = lax.broadcasted_iota(jnp.int32, (BLOCK, BLOCK), 1) < 64
        for h in range(2):
            block = 2 * (step - 2) + h
            rows = rows_of(block)
            up = pl.ds(pl.multiple_of(block * 256, 256), 128)
            down = pl.ds(pl.multiple_of(block * 256 + 128, 128), 128)
            for p in range(PAIRS):
                for t, source in enumerate((dk_s, dv_s)):
                    both = jnp.where(even, source[p, up, :], source[p, down, :])
                    spot = p * 384 + 128 + t * 128
                    dqkv_s[rows, spot : spot + 128] = both.astype(BF16)
        dqkv_o[...] = dqkv_s[rows_of(2 * (step - 2), 2), :]

    @pl.when(step == blocks // 2 + 1)
    def _():
        for p in range(PAIRS):
            part = t_dot(normed_s[...], dqkv_s[:, p * 384 : (p + 1) * 384]).astype(BF16)
            for half in range(2):
                piece = part[half * 256 : (half + 1) * 256].reshape(16, 16, 384)

                @pl.when(core == half)
                def _():
                    mine_o[:, p] = piece

                @pl.when(core != half)
                def _():
                    sent_o[:, p] = piece


def entry_kernel(blocks, left, x, right, dbr, gain, ln2, weight, d_qkv,
                 grad_o, left_o, right_o, small_o, w_s, x_s, ln_s, grad_s):
    r = pl.program_id(0)
    tiles = blocks // 2

    @pl.when(r == 0)
    def _():
        for p in range(PAIRS):
            for part in range(3):
                spot = part * 512 + p * 128
                to = p * 384 + part * 128
                w_s[:, to : to + 128] = weight[:, spot : spot + 128]
        for t in range(tiles):
            x_s[t * 256 : (t + 1) * 256, :] = two_blocks(left, x, right, t)
        ln_s[0:2, :] = jnp.zeros((2, D), F32)

    rows = pl.ds(pl.multiple_of(r * 256, 256), 256)
    d_n1 = dot_t(d_qkv[...], w_s[...])
    n1, inverse = normalize(x_s[rows, :].astype(F32))
    e = d_n1 * gain[...]
    mean_e = jnp.mean(e, axis=-1, keepdims=True)
    mean_en = jnp.mean(e * n1, axis=-1, keepdims=True)
    grad_s[rows, :] = dbr[...].astype(F32) + (e - mean_e - n1 * mean_en) * inverse
    ln_s[0:1, :] += jnp.sum(d_n1 * n1, axis=0, keepdims=True)
    ln_s[1:2, :] += jnp.sum(d_n1, axis=0, keepdims=True)

    @pl.when(r == tiles - 1)
    def _():
        inner = (blocks - 2) * BLOCK
        grad_o[...] = grad_s[HALO : HALO + inner, :]
        left_o[...] = grad_s[0:HALO, :].astype(BF16)
        right_o[...] = grad_s[HALO + inner :, :].astype(BF16)
        vectors = [ln_s[0:1, :], ln_s[1:2, :], ln2[0:1, :], ln2[1:2, :]]
        small_o[...] = jnp.concatenate(
            [v[:, c * 128 : (c + 1) * 128] for v in vectors for c in range(4)], axis=0
        )


def join_kernel(share, mine, other, out_m, out_o, result):
    wide = share.shape[-1]
    result[:, :, :, 0:wide] = jnp.broadcast_to(share[...][None, None], (4, 4, *share.shape))
    value = mine[...].astype(F32) + other[...].astype(F32)
    result[:, :, :, wide : wide + 384] = value.astype(BF16)
    value = out_m[...].astype(F32) + out_o[...].astype(F32)
    result[:, :, :, wide + 384 : wide + 512] = value.astype(BF16)


def join_call(share, mine, other, out_m, out_o):
    at = lambda s: (s, 0, 0, 0)
    block = (4, 4, 16, share.shape[-1] + 512)
    return pl.pallas_call(
        join_kernel,
        grid=(4,),
        in_specs=[pl.BlockSpec(share.shape, lambda s: (0, 0))]
        + [pl.BlockSpec((4, 4, 16, 384), at)] * 2 + [pl.BlockSpec((4, 4, 16, 128), at)] * 2,
        out_specs=pl.BlockSpec(block, at),
        out_shape=shape_of((16, *block[1:]), BF16),
        compiler_params=params(),
        name="join",
    )(share, mine, other, out_m, out_o)


def whole(shape):
    return pl.BlockSpec(shape, lambda s, scal: (0,) * len(shape))


def shape_of(shape, dtype):
    return jax.ShapeDtypeStruct(shape, dtype)


def params():
    return pltpu.CompilerParams(
        dimension_semantics=("arbitrary",), vmem_limit_bytes=VMEM_LIMIT
    )


def attend_call(scal, left, x, right, seg, gain, shift, weight):
    rows = x.shape[0] + 2 * HALO
    blocks = rows // BLOCK
    at = lambda s, scal: (jnp.maximum(s - 1, 0), 0)
    return pl.pallas_call(
        functools.partial(attend_kernel, blocks),
        grid_spec=pltpu.PrefetchScalarGridSpec(
            num_scalar_prefetch=1,
            grid=(blocks // 2 + 1,),
            in_specs=[
                whole((HALO, D)), whole(x.shape), whole((HALO, D)), whole(seg.shape),
                whole((1, D)), whole((1, D)), whole(weight.shape),
            ],
            out_specs=[
                pl.BlockSpec((2 * BLOCK, D), at),
                pl.BlockSpec((2 * BLOCK, 3 * D), at),
                pl.BlockSpec((2 * BLOCK, D), at),
                pl.BlockSpec((2 * BLOCK, D), at),
            ],
            scratch_shapes=[
                pltpu.VMEM((rows, D), BF16),
                pltpu.VMEM((rows, 3 * D), BF16),
                pltpu.VMEM((PAIRS, blocks * 256, 128), BF16),
                pltpu.VMEM((PAIRS, blocks * 256, 256), BF16),
            ],
        ),
        out_shape=[
            shape_of((rows, D), BF16),
            shape_of((rows, 3 * D), BF16),
            shape_of((rows, D), BF16),
            shape_of((rows, D), BF16),
        ],
        compiler_params=params(),
        cost_estimate=pl.CostEstimate(flops=8 * 10**9, bytes_accessed=25 * 10**6, transcendentals=4 * 10**6),
        name="attend",
    )(scal, left, x, right, seg, gain, shift, weight)


def feed_call(scal, att, left, x, right, cot_l, cot, cot_r, out_w, up_w, down_w, gain, shift):
    rows = att.shape[0]
    blocks = rows // BLOCK
    half = (16, 4, 16, 1024)
    anywhere = pl.BlockSpec(memory_space=pl.ANY)
    return pl.pallas_call(
        functools.partial(feed_kernel, blocks),
        grid_spec=pltpu.PrefetchScalarGridSpec(
            num_scalar_prefetch=1,
            grid=(FF // 512,),
            in_specs=[
                whole((rows, D)),
                whole((HALO, D)), whole(x.shape), whole((HALO, D)),
                whole((HALO, D)), whole(x.shape), whole((HALO, D)),
                whole((D, D)),
                pl.BlockSpec((D, 512), lambda s, scal: (0, s)),
                pl.BlockSpec((512, D), lambda s, scal: (s, 0)),
                whole((1, D)), whole((1, D)),
            ],
            out_specs=[
                anywhere, anywhere, anywhere, whole((rows, D)),
                pl.BlockSpec((rows, 512), lambda s, scal: (0, s)), anywhere, anywhere,
            ],
            scratch_shapes=[
                pltpu.VMEM((rows, D), BF16),
                pltpu.VMEM((rows, 128), F32),
                pltpu.VMEM((rows, D), BF16),
                pltpu.VMEM(half, BF16),
                pltpu.VMEM(half, BF16),
                pltpu.SemaphoreType.DMA((3 + 3 * (FF // 512),)),
                pltpu.VMEM((rows, D), BF16),
                pltpu.VMEM((rows, 512), BF16),
                pltpu.VMEM((FF // 512, rows, 512), BF16),
                pltpu.VMEM((FF // 512, D, 512), BF16),
            ] + [pltpu.VMEM((256, 512), F32)] * 4,
        ),
        out_shape=[
            shape_of((rows, D), BF16),
            shape_of((rows, 128), F32),
            shape_of((rows, D), BF16),
            shape_of((rows, D), BF16),
            shape_of((rows, FF), BF16),
            shape_of(half, BF16),
            shape_of(half, BF16),
        ],
        compiler_params=params(),
        cost_estimate=pl.CostEstimate(flops=16 * 10**9, bytes_accessed=25 * 10**6, transcendentals=3 * 10**6),
        name="feed",
    )(scal, att, left, x, right, cot_l, cot, cot_r, out_w, up_w, down_w, gain, shift)


def middle_call(scal, base, rstd, dn2, cot, att, out_w, gain):
    rows = att.shape[0]
    blocks = rows // BLOCK
    part = (16, 4, 16, 128)
    tile = pl.BlockSpec((256, D), lambda s, scal: (s, 0))
    return pl.pallas_call(
        middle_kernel,
        grid_spec=pltpu.PrefetchScalarGridSpec(
            num_scalar_prefetch=1,
            grid=(rows // 256,),
            in_specs=[
                tile, pl.BlockSpec((256, 128), lambda s, scal: (s, 0)), tile, tile, tile,
                whole((D, D)), whole((1, D)),
            ],
            out_specs=[
                tile, pl.BlockSpec((256, 2 * D), lambda s, scal: (s, 0)),
                whole(part), whole(part), whole((2, D)),
            ],
            scratch_shapes=[pltpu.VMEM((D, D), F32)],
        ),
        out_shape=[
            shape_of((rows, D), BF16), shape_of((rows, 2 * D), BF16),
            shape_of(part, BF16), shape_of(part, BF16), shape_of((2, D), F32),
        ],
        compiler_params=params(),
        cost_estimate=pl.CostEstimate(flops=2 * 10**9, bytes_accessed=15 * 10**6, transcendentals=0),
        name="middle",
    )(scal, base, rstd, dn2, cot, att, out_w, gain)


def back_call(scal, a, lse, seg, qkv, normed):
    rows = qkv.shape[0]
    blocks = rows // BLOCK
    half = (16, PAIRS, 16, 384)
    last = blocks // 2 - 1
    lead = lambda s, scal: (jnp.minimum(s, last), 0)
    now = lambda s, scal: (jnp.clip(s - 1, 0, last), 0)
    done = lambda s, scal: (jnp.maximum(s - 2, 0), 0)
    return pl.pallas_call(
        functools.partial(back_kernel, blocks),
        grid_spec=pltpu.PrefetchScalarGridSpec(
            num_scalar_prefetch=1,
            grid=(blocks // 2 + 2,),
            in_specs=[
                pl.BlockSpec((2 * BLOCK, 2 * D), now), pl.BlockSpec((2 * BLOCK, D), now), whole(seg.shape),
                pl.BlockSpec((2 * BLOCK, 3 * D), lead), pl.BlockSpec((2 * BLOCK, D), lead),
            ],
            out_specs=[pl.BlockSpec((2 * BLOCK, 3 * D), done), whole(half), whole(half)],
            scratch_shapes=[
                pltpu.VMEM((rows, D), BF16),
                pltpu.VMEM((PAIRS, blocks * 256, 256), BF16),
                pltpu.VMEM((PAIRS, blocks * 256, 256), BF16),
                pltpu.VMEM((PAIRS, blocks * 256, 128), F32),
                pltpu.VMEM((PAIRS, blocks * 256, 128), F32),
                pltpu.VMEM((6 * BLOCK, 2 * BLOCK), F32),
                pltpu.VMEM((rows, 3 * D), BF16),
                pltpu.VMEM((rows, D), BF16),
            ],
        ),
        out_shape=[shape_of((rows, 3 * D), BF16), shape_of(half, BF16), shape_of(half, BF16)],
        compiler_params=params(),
        cost_estimate=pl.CostEstimate(flops=12 * 10**9, bytes_accessed=20 * 10**6, transcendentals=4 * 10**6),
        name="back",
    )(scal, a, lse, seg, qkv, normed)


def entry_call(left, x, right, dbr, gain, ln2, weight, d_qkv):
    rows = dbr.shape[0]
    fixed = lambda v: pl.BlockSpec(v.shape, lambda s: (0,) * len(v.shape))
    at = lambda s: (s, 0)
    edge = shape_of((HALO, D), BF16)
    outs = [shape_of(x.shape, F32), edge, edge, shape_of((16, 128), F32)]
    return pl.pallas_call(
        functools.partial(entry_kernel, rows // BLOCK),
        grid=(rows // 256,),
        in_specs=[
            fixed(left), fixed(x), fixed(right), pl.BlockSpec((256, D), at), fixed(gain), fixed(ln2),
            fixed(weight), pl.BlockSpec((256, 3 * D), at),
        ],
        out_specs=[fixed(v) for v in outs],
        out_shape=outs,
        scratch_shapes=[
            pltpu.VMEM((D, 3 * D), BF16), pltpu.VMEM((rows, D), BF16), pltpu.VMEM((8, D), F32),
            pltpu.VMEM((rows, D), F32),
        ],
        compiler_params=params(),
        cost_estimate=pl.CostEstimate(flops=2 * 10**9, bytes_accessed=15 * 10**6, transcendentals=0),
        name="entry",
    )(left, x, right, dbr, gain, ln2, weight, d_qkv)


def other_core(value):
    return lax.ppermute(value, "core", [(0, 1), (1, 0)])


def all_shares(value, groups):
    parts = lax.all_to_all(value, ("rows", "x"), 0, 0, tiled=True)
    return jnp.sum(parts.astype(F32), axis=0).astype(BF16)


def gather_shares(share, groups):
    copies = jnp.broadcast_to(share[None], (groups, *share.shape))
    return lax.all_to_all(copies, ("rows", "x"), 0, 0, tiled=True)


def per_device(
    inputs, qkv_weight, out_weight, up_weight, down_weight, norm1_gain, norm1_shift,
    norm2_gain, norm2_shift, segment_ids, item_steps, gen_rank, out_grad,
):
    x = inputs[0]
    positions = x.shape[0]
    blocks = (positions + 2 * HALO) // BLOCK
    chips = lax.axis_size("rows") * lax.axis_size("x")
    seq_parts = lax.axis_size("x") * lax.axis_size("core")
    seq = ("x", "core")
    to_right = [(i, (i + 1) % seq_parts) for i in range(seq_parts)]
    to_left = [((i + 1) % seq_parts, i) for i in range(seq_parts)]

    place = jnp.stack([lax.axis_index(seq), lax.axis_index("core")]).astype(jnp.int32)
    tie = lax.optimization_barrier
    left = lax.ppermute(x[positions - HALO :], seq, to_right)
    right = lax.ppermute(x[:HALO], seq, to_left)
    scal, seg_rows, cot, send_l, send_r = prepare_call(
        place, segment_ids, item_steps, gen_rank, out_grad[0]
    )
    cot_l = lax.ppermute(send_r, seq, to_right)
    cot_r = lax.ppermute(send_l, seq, to_left)

    gain1, shift1 = norm1_gain.reshape(1, D), norm1_shift.reshape(1, D)
    gain2, shift2 = norm2_gain.reshape(1, D), norm2_shift.reshape(1, D)
    normed1, qkv, att, lse = attend_call(
        scal, left, x, right, seg_rows, gain1, shift1, qkv_weight
    )
    base2, rstd2, cot_w, dn2, act, mine_a, sent_a = feed_call(
        scal, att, left, x, right, cot_l, cot, cot_r, out_weight, up_weight, down_weight, gain2, shift2
    )
    got_a = other_core(sent_a)
    half_a = (mine_a.astype(F32) + got_a.astype(F32)).astype(BF16)
    d_branch, a, mine_o, sent_o, ln2 = middle_call(
        scal, base2, rstd2, dn2, cot_w, att, out_weight, gain2
    )
    a, half_a = tie((a, half_a))
    share_a = all_shares(half_a.reshape(chips, -1, 1024), chips)
    d_qkv, mine_b, sent_b = back_call(scal, a, lse, seg_rows, qkv, normed1)
    share_a, sent_b, sent_o = tie((share_a, sent_b, sent_o))
    joined = join_call(share_a, mine_b, other_core(sent_b), mine_o, other_core(sent_o))
    joined, d_branch, att = tie((joined, d_branch, att))
    got = lax.all_to_all(joined.reshape(chips, -1, 1536), ("rows", "x"), 0, 0, tiled=True)
    grad, grad_l, grad_r, small = entry_call(
        left, x, right, d_branch, gain1, ln2, qkv_weight, d_qkv
    )
    small = small + other_core(small)
    out, out_l, out_r = finish_call(att, left, x, right, act, out_weight, down_weight)
    edge_l = jnp.concatenate([out_l, grad_l], axis=0)
    edge_r = jnp.concatenate([out_r, grad_r], axis=0)
    from_r = lax.ppermute(edge_l, seq, to_left)
    from_l = lax.ppermute(edge_r, seq, to_right)
    got, from_l, from_r, small = tie((got, from_l, from_r, small))
    far_a = other_core(got)
    share_b = jnp.sum(got[:, :, 1024:].astype(F32), axis=0).astype(BF16)
    near_b = gather_shares(jnp.concatenate([share_b, small.astype(BF16)], axis=1), chips)
    feed_shapes, rest_shapes = ((FF, D), (D, FF)), ((D, D), (D, 3 * D))
    grads_a = unpack_call(unpack_feed, feed_shapes, scal, got.reshape(16, 4, 16, 1536))
    grad_down, grad_up = unpack_call(
        unpack_feed, feed_shapes, scal, far_a.reshape(16, 4, 16, 1536), grads_a
    )
    output, input_grad = patch_call(scal, out, grad, seg_rows, from_l, from_r)
    near_b, grad_down, input_grad = tie((near_b, grad_down, input_grad))
    far_b = other_core(near_b)
    *grads_b, small = unpack_call(
        unpack_rest, rest_shapes, scal, near_b.reshape(16, 4, 16, 640), steps=2, small=(16, 128)
    )
    vectors = small.reshape(4, D)
    grad_out, grad_qkv = unpack_call(
        unpack_rest, rest_shapes, scal, far_b.reshape(16, 4, 16, 640), grads_b, steps=2
    )
    return (
        output[None], input_grad[None], grad_qkv, grad_out, grad_up, grad_down,
        vectors[0], vectors[1], vectors[2], vectors[3],
    )


def solution(mesh):
    rows = mesh.devices.shape[0]
    parts = mesh.devices.shape[1]
    split = Mesh(mesh.devices.reshape(rows, parts // 2, 2), ("rows", "x", "core"))
    seq = ("x", "core")
    return jax.shard_map(
        per_device,
        mesh=split,
        in_specs=(
            P("rows", seq, None), P(), P(), P(), P(), P(), P(), P(), P(),
            P("rows", None), P("rows", None), P("rows", seq), P("rows", seq, None),
        ),
        out_specs=(
            P("rows", seq, None), P("rows", seq, None),
            P(), P(), P(), P(), P(), P(), P(), P(),
        ),
        check_vma=False,
    )
```

```python
import functools

import jax
import jax.numpy as jnp
from jax import lax
from jax.experimental import pallas as pl
from jax.experimental.pallas import tpu as pltpu
from jax.sharding import Mesh
from jax.sharding import PartitionSpec as P

D = 512
HEADS = 8
PAIRS = HEADS // 2
FF = 2048
EPS = 1e-05
HALO = 128
BLOCK = 128
BF16 = jnp.bfloat16
F32 = jnp.float32
VMEM_LIMIT = 58 * 1024 * 1024
HIGH, CORE, DROP_L, DROP_R = 16, 32, 33, 34


def dot(a, b):
    return lax.dot_general(a, b, (((1,), (0,)), ((), ())), preferred_element_type=F32)


def dot_t(a, b):
    return lax.dot_general(a, b, (((1,), (1,)), ((), ())), preferred_element_type=F32)


def t_dot(a, b):
    return lax.dot_general(a, b, (((0,), (0,)), ((), ())), preferred_element_type=F32)


def normalize(value):
    center = jnp.mean(value, axis=-1, keepdims=True)
    centred = value - center
    spread = jnp.mean(centred * centred, axis=-1, keepdims=True)
    inverse = lax.rsqrt(spread + EPS)
    return centred * inverse, inverse


def two_blocks(left, middle, right, tile):
    last = 1 + middle.shape[0] // BLOCK
    parts = []
    for block in (2 * tile, 2 * tile + 1):
        if block == 0:
            parts.append(left[...])
        elif block == last:
            parts.append(right[...])
        else:
            parts.append(middle[(block - 1) * BLOCK : block * BLOCK, :])
    return jnp.concatenate(parts, axis=0)


def split_pairs(keys, values, kc, vx, block):
    lane = lax.broadcasted_iota(jnp.int32, (BLOCK, BLOCK), 1)
    even = lane < 64
    zero = jnp.zeros((BLOCK, BLOCK), BF16)
    ones_even = even.astype(F32).astype(BF16)
    ones_odd = (~even).astype(F32).astype(BF16)
    base = block * 256
    for p in range(PAIRS):
        k = keys[:, p * 128 : (p + 1) * 128]
        v = values[:, p * 128 : (p + 1) * 128]
        kc[p, pl.ds(base, 128), 0:128] = jnp.where(even, k, zero)
        kc[p, pl.ds(base + 128, 128), 0:128] = jnp.where(even, zero, k)
        vx[p, pl.ds(base, 128), 0:128] = jnp.where(even, v, zero)
        vx[p, pl.ds(base + 128, 128), 0:128] = jnp.where(even, zero, v)
        vx[p, pl.ds(base, 128), 128:256] = ones_even
        vx[p, pl.ds(base + 128, 128), 128:256] = ones_odd
        if kc.shape[2] == 256:
            minus = jnp.where(lax.rem(lane, 64) < 3, -1.0, 0.0)
            kc[p, pl.ds(base, 128), 128:256] = jnp.where(even, minus, 0.0).astype(BF16)
            kc[p, pl.ds(base + 128, 128), 128:256] = jnp.where(even, 0.0, minus).astype(BF16)


def mask_rows(seg, row, low, n):
    seg_q = column(seg[row].astype(F32))
    return [
        jnp.where(seg_q == jnp.broadcast_to(seg[low + t].astype(F32), (BLOCK, BLOCK)), 0.0, -1e30)
        for t in range(n)
    ]


def column(row):
    return jnp.transpose(jnp.broadcast_to(row, (BLOCK, BLOCK)))


def keep_rows(values, mask):
    return jnp.concatenate(
        [
            jnp.where(mask, values[:, c * 128 : (c + 1) * 128].astype(F32), 0.0).astype(BF16)
            for c in range(D // 128)
        ],
        axis=1,
    )


def prepare_kernel(inner, place, segments, steps, rank, out_grad, scal_o, seg_o, cot_o, left_o, right_o, part_s):
    seq = place[0]
    row_blocks = segments.shape[1] // BLOCK
    blocks = inner + 2
    rows = []
    for b in range(blocks):
        at = seq * inner + b - 1
        if b == 0:
            at = jnp.maximum(at, 0)
        if b == blocks - 1:
            at = jnp.minimum(at, row_blocks - 1)
        row = segments[0:1, pl.ds(pl.multiple_of(at * BLOCK, BLOCK), BLOCK)]
        if b == 0:
            row = jnp.where(seq > 0, row, -1)
        if b == blocks - 1:
            row = jnp.where(seq * inner + inner < row_blocks, row, 1000)
        rows.append(row)
        seg_o[b] = row
    window = jnp.concatenate(rows, axis=0)
    local = window[1 : inner + 1]
    first, last = window[:, 0:1], window[:, BLOCK - 1 : BLOCK]
    below = jnp.zeros(window.shape, F32)
    upto = jnp.zeros(window.shape, F32)
    for row in rows:
        below += (row < first).astype(F32)
        upto += (row <= last).astype(F32)
    part_s[...] = jnp.zeros(part_s.shape, F32)
    part_s[0:blocks, :] = below
    part_s[HIGH : HIGH + blocks, :] = upto
    counts = dot_t(jnp.ones((8, BLOCK), BF16), part_s[...].astype(BF16))[0:1]

    def border(before, after):
        value = before[-1:, BLOCK - 1 : BLOCK]
        across = value == after[0:1, 0:1]
        sizes = [jnp.sum((part == value).astype(F32), axis=(0, 1), keepdims=True) for part in (before, after)]
        return value, across, sizes[0] >= sizes[1]

    value_l, across_l, to_left_l = border(rows[0], local)
    value_r, across_r, to_left_r = border(local, rows[-1])
    drop_l = jnp.where(across_l & to_left_l, value_l, -2)
    drop_r = jnp.where(across_r & jnp.logical_not(to_left_r), value_r, -2)
    lane = lax.broadcasted_iota(jnp.int32, (1, BLOCK), 1)
    at_block = jnp.floor(jnp.where(lane >= HIGH, counts - 1.0, counts) * (1.0 / BLOCK)).astype(jnp.int32)
    at_block = jnp.where(lane == CORE, place[1], at_block)
    at_block = jnp.where(lane == DROP_L, drop_l, at_block)
    scal_o[...] = jnp.where(lane == DROP_R, drop_r, at_block)

    token = jnp.zeros(local.shape, jnp.int32)
    for slot in range(steps.shape[1]):
        token = jnp.where(local == slot, steps[0, slot], token)
    for b in range(inner):
        part = slice(b * BLOCK, (b + 1) * BLOCK)
        keep = rank[0:1, part] >= token[b : b + 1]
        seg = rows[b + 1]
        own = (seg != drop_l) & (seg != drop_r)
        values = out_grad[part, :]
        cot_o[part, :] = keep_rows(values, column((keep & own).astype(F32)) > 0.5)
        if b == 0:
            left_o[...] = keep_rows(values, column((keep & (seg == drop_l)).astype(F32)) > 0.5)
        if b == inner - 1:
            right_o[...] = keep_rows(values, column((keep & (seg == drop_r)).astype(F32)) > 0.5)


def prepare_call(place, segments, steps, rank, out_grad):
    inner = out_grad.shape[0] // BLOCK
    vmem = pl.BlockSpec(memory_space=pltpu.VMEM)
    smem = pl.BlockSpec(memory_space=pltpu.SMEM)
    return pl.pallas_call(
        functools.partial(prepare_kernel, inner),
        in_specs=[smem, vmem, smem, vmem, vmem],
        out_specs=[vmem] * 5,
        out_shape=[
            shape_of((1, BLOCK), jnp.int32),
            shape_of((inner + 2, 1, BLOCK), jnp.int32),
            shape_of(out_grad.shape, BF16),
            shape_of((HALO, D), BF16),
            shape_of((HALO, D), BF16),
        ],
        scratch_shapes=[pltpu.VMEM((BLOCK, BLOCK), F32)],
        compiler_params=pltpu.CompilerParams(vmem_limit_bytes=VMEM_LIMIT),
        cost_estimate=pl.CostEstimate(flops=10**6, bytes_accessed=4 * 10**6, transcendentals=0),
        name="prepare",
    )(place, segments, steps, rank, out_grad)


def patch_kernel(blocks, scal, out, grad, seg, left, right, out_o, grad_o):
    step = pl.program_id(0)
    drop_l, drop_r = scal[0, DROP_L], scal[0, DROP_R]
    row = seg[0]
    drop = jnp.where(step == 0, drop_l, drop_r)
    lost = column((row == drop).astype(F32)) > 0.5
    for c in range(D // 128):
        cols = slice(c * 128, (c + 1) * 128)
        for mine, start, result in ((out, 0, out_o), (grad, HALO, grad_o)):
            part = slice(start, start + HALO)
            other = jnp.where(step == 0, left[part, cols].astype(F32), right[part, cols].astype(F32))
            value = jnp.where(lost, other, mine[:, cols].astype(F32))
            result[:, cols] = value.astype(result.dtype)


def patch_call(scal, out, grad, seg, left, right):
    inner = out.shape[0] // BLOCK
    block = lambda s, scal: (s * (inner - 1), 0)
    return pl.pallas_call(
        functools.partial(patch_kernel, inner + 2),
        grid_spec=pltpu.PrefetchScalarGridSpec(
            num_scalar_prefetch=1,
            grid=(2,),
            in_specs=[
                pl.BlockSpec((BLOCK, D), block),
                pl.BlockSpec((BLOCK, D), block),
                pl.BlockSpec((1, 1, BLOCK), lambda s, scal: (1 + s * (inner - 1), 0, 0)),
                whole((2 * HALO, D)), whole((2 * HALO, D)),
            ],
            out_specs=[pl.BlockSpec((BLOCK, D), block), pl.BlockSpec((BLOCK, D), block)],
        ),
        out_shape=[shape_of(out.shape, out.dtype), shape_of(grad.shape, grad.dtype)],
        input_output_aliases={1: 0, 2: 1},
        compiler_params=params(),
        name="patch",
    )(scal, out, grad, seg, left, right)


def unpack_feed(a, down_o, up_o):
    rows = a.shape[0] * 16
    down_o[...] = a[:, :, :, 0:512].astype(F32).reshape(4 * rows, 512)
    for c in range(4):
        up_o[:, c * 512 : (c + 1) * 512] = a[:, c, :, 512:1024].astype(F32).reshape(rows, 512)


def unpack_rest(a, out_o, qkv_o, *vectors_o):
    rows = a.shape[0] * 16
    for c in range(4):
        value = a[:, c, :, 0:512].astype(F32).reshape(rows, 512)
        for part in range(3):
            spot = part * 512 + c * 128
            qkv_o[:, spot : spot + 128] = value[:, part * 128 : (part + 1) * 128]
        out_o[:, c * 128 : (c + 1) * 128] = value[:, 384:512]
    if vectors_o:
        part = jnp.sum(a[:, :, :, 512:640].astype(F32), axis=(0, 1))
        for v in range(4):
            vectors_o[v][...] = jnp.concatenate([part[4 * v + c : 4 * v + c + 1] for c in range(4)], axis=1)


def unpack_call(body, shapes, scal, value, before=(), steps=4, extra=()):
    def out(s, scal):
        half = scal[0, CORE] if not before else 1 - scal[0, CORE]
        return (half * steps + s, 0)

    def kernel(scal, a, *refs):
        body(a, *refs[len(before) :])

    return pl.pallas_call(
        kernel,
        grid_spec=pltpu.PrefetchScalarGridSpec(
            num_scalar_prefetch=1,
            grid=(steps,),
            in_specs=[pl.BlockSpec((16 // steps, *value.shape[1:]), lambda s, scal: (s, 0, 0, 0))]
            + [pl.BlockSpec(memory_space=pl.ANY)] * len(before),
            out_specs=[pl.BlockSpec((rows // (2 * steps), cols), out) for rows, cols in shapes]
            + [whole(v) for v in extra],
        ),
        out_shape=[shape_of(shape, F32) for shape in (*shapes, *extra)],
        input_output_aliases={2 + k: k for k in range(len(before))},
        compiler_params=params(),
        cost_estimate=pl.CostEstimate(flops=10**6, bytes_accessed=10 * 10**6, transcendentals=0),
        name="unpack",
    )(scal, value, *before)


def attend_kernel(blocks, scal, left, x, right, seg, gain, shift, weight,
                  normed_o, qkv_o, att_o, lse_o, normed_s, qkv_s, kc, vx, sems):
    step = pl.program_id(0)
    tiles = blocks // 2

    def copies(r):
        rows = slice(r * 256, (r + 1) * 256)
        return (
            pltpu.make_async_copy(normed_s.at[rows, :], normed_o.at[rows, :], sems.at[2 * r]),
            pltpu.make_async_copy(qkv_s.at[rows, :], qkv_o.at[rows, :], sems.at[2 * r + 1]),
        )

    @pl.when(step == 0)
    def _():
        for r in range(tiles + 1):
            if r < tiles:
                base, _ = normalize(two_blocks(left, x, right, r).astype(F32))
                normed_s[r * 256 : (r + 1) * 256, :] = (base * gain[...] + shift[...]).astype(BF16)
            if r > 0:
                rows = slice((r - 1) * 256, r * 256)
                qkv = dot(normed_s[rows, :], weight[...]).astype(BF16)
                qkv_s[rows, :] = qkv
                for half in range(2):
                    part = qkv[half * 128 : (half + 1) * 128]
                    split_pairs(part[:, 512:1024], part[:, 1024:1536], kc, vx, 2 * (r - 1) + half)
                for copy in copies(r - 1):
                    copy.start()

    @pl.when(step > 0)
    def _():
        lane = lax.broadcasted_iota(jnp.int32, (BLOCK, BLOCK), 1)
        place = lax.rem(lane, 64)
        for h in range(2):
            i = 2 * (step - 1) + h
            rows = pl.ds(pl.multiple_of(i * BLOCK, BLOCK), BLOCK)
            part = slice(h * BLOCK, (h + 1) * BLOCK)
            low = scal[0, i]
            n_keys = scal[0, HIGH + i] - low + 1
            first = pl.multiple_of(low * 256, 256)

            def attend(n):
                bias = mask_rows(seg, i, low, n)
                def pair(p, carry):
                    cols = pl.ds(pl.multiple_of(p * 128, 128), 128)
                    q = qkv_s[rows, cols] * jnp.asarray(0.125, BF16)
                    scores = dot_t(q, kc[p, pl.ds(first, n * 256), :])
                    tiles_s = [
                        [scores[:, t * 256 + o * 128 : t * 256 + o * 128 + 128] + bias[t] for t in range(n)]
                        for o in range(2)
                    ]
                    highest = [
                        jnp.max(functools.reduce(jnp.maximum, tiles_s[o]), axis=-1, keepdims=True)
                        for o in range(2)
                    ]
                    pieces = []
                    for t in range(n):
                        for o in range(2):
                            pieces.append(jnp.exp(tiles_s[o][t] - highest[o]).astype(BF16))
                    mixed = dot(jnp.concatenate(pieces, axis=1), vx[p, pl.ds(first, n * 256), :])
                    total = mixed[:, 128:256]
                    att_o[part, cols] = (mixed[:, 0:128] * (1.0 / total)).astype(BF16)
                    lse = jnp.where(lane < 64, highest[0], highest[1]) + jnp.log(total)
                    top = lse.astype(BF16).astype(F32)
                    rest = lse - top
                    second = rest.astype(BF16).astype(F32)
                    third = jnp.where(place == 2, rest - second, 0.0)
                    lse_o[part, cols] = jnp.where(
                        place == 0, top, jnp.where(place == 1, second, third)
                    ).astype(BF16)
                    return carry

                lax.fori_loop(0, PAIRS, pair, 0, unroll=PAIRS)

            for n in range(1, 6):
                pl.when(n_keys == n)(functools.partial(attend, n))

    @pl.when(step == tiles)
    def _():
        for r in range(tiles):
            for copy in copies(r):
                copy.wait()


def gelu_both(v):
    c = 0.7978845608028654
    square = v * v
    inner = c + (0.044715 * c) * square
    gate = 0.5 + 0.5 * jnp.tanh(v * inner)
    act = v * gate
    slope = gate + act * ((1.0 - gate) * (6.0 * inner - 4.0 * c))
    return act, slope


def feed_kernel(blocks, scal, att, left, x, right, cot_l, cot, cot_r, out_w, up_w, down_w, gain, shift,
                dbr_o, act_o, ln_o, mine_o, sent_o,
                base_s, rstd_s, cot_s, mine_s, sent_s, sems, n2_s, dpre_s, up_s, *stage_s):
    f = pl.program_id(0)
    steps = FF // 512
    tiles = blocks // 2
    core = scal[0, CORE]

    def down_copy(k, from_s, to_o):
        spot = (slice((k % 2) * 8, (k % 2) * 8 + 8), slice(None), slice(None), slice(0, 512))
        return pltpu.make_async_copy(from_s.at[spot], to_o.at[spot], sems.at[k])

    def up_copies(k):
        spot = (slice(None), slice(k, k + 1), slice(None), slice(512, 1024))
        return [
            pltpu.make_async_copy(mine_s.at[spot], mine_o.at[spot], sems.at[steps + k]),
            pltpu.make_async_copy(sent_s.at[spot], sent_o.at[spot], sems.at[2 * steps + k]),
        ]

    @pl.when(f == 0)
    def _():
        for r in range(tiles):
            rows = slice(r * 256, (r + 1) * 256)
            cot_s[rows, :] = two_blocks(cot_l, cot, cot_r, r)
            mid = two_blocks(left, x, right, r).astype(F32) + dot(att[rows, :], out_w[...])
            base, inverse = normalize(mid)
            base_s[rows, :] = base
            rstd_s[rows, :] = jnp.broadcast_to(inverse, (256, 128))
            n2_s[rows, :] = (base * gain[...] + shift[...]).astype(BF16)

    up_s[f] = up_w[...]
    for r in range(tiles + 1):
        if r < tiles:
            rows = slice(r * 256, (r + 1) * 256)
            stage_s[r % 2][...] = dot(n2_s[rows, :], up_w[...])
            stage_s[2 + r % 2][...] = dot_t(cot_s[rows, :], down_w[...])
        if r > 0:
            rows = slice((r - 1) * 256, r * 256)
            act, slope = gelu_both(stage_s[(r - 1) % 2][...])
            act_o[rows, :] = act.astype(BF16)
            dpre_s[f, rows, :] = (slope * stage_s[2 + (r - 1) % 2][...]).astype(BF16)
    grad_down = t_dot(act_o[...], cot_s[...]).astype(BF16).reshape(8, 4, 16, 512)
    grad_up = t_dot(n2_s[...], dpre_s[f]).astype(BF16).reshape(2, 16, 1, 16, 512)

    for k in range(steps):

        @pl.when((f == k) & (core == k // 2))
        def _():
            mine_s[(k % 2) * 8 : (k % 2) * 8 + 8, :, :, 0:512] = grad_down
            down_copy(k, mine_s, mine_o).start()

        @pl.when((f == k) & (core != k // 2))
        def _():
            sent_s[(k % 2) * 8 : (k % 2) * 8 + 8, :, :, 0:512] = grad_down
            down_copy(k, sent_s, sent_o).start()

    for half in range(2):

        @pl.when(core == half)
        def _():
            mine_s[:, pl.ds(f, 1), :, 512:1024] = grad_up[half]
            sent_s[:, pl.ds(f, 1), :, 512:1024] = grad_up[1 - half]

    for k in range(steps):

        @pl.when(f == k)
        def _():
            for copy in up_copies(k):
                copy.start()

    @pl.when(f == steps - 1)
    def _():
        def turn(r, carry):
            rows = pl.ds(pl.multiple_of(r * 256, 256), 256)
            d_pre = jnp.concatenate([dpre_s[k, rows, :] for k in range(steps)], axis=1)
            up = jnp.concatenate([up_s[k] for k in range(steps)], axis=1)
            d_n2 = dot_t(d_pre, up)
            n2 = base_s[rows, :]
            inverse = jnp.concatenate([rstd_s[rows, :]] * 4, axis=1)
            e = d_n2 * gain[...]
            mean_e = jnp.mean(e, axis=-1, keepdims=True)
            mean_en = jnp.mean(e * n2, axis=-1, keepdims=True)
            d_mid = cot_s[rows, :].astype(F32) + (e - mean_e - n2 * mean_en) * inverse
            dbr_o[rows, :] = d_mid.astype(BF16)
            g, s = carry
            return (
                g + jnp.sum((d_n2 * n2).reshape(32, 8, D), axis=0),
                s + jnp.sum(d_n2.reshape(32, 8, D), axis=0),
            )

        zero = jnp.zeros((8, D), F32)
        g, s = lax.fori_loop(0, tiles, turn, (zero, zero))
        ln_o[0:1, :] = jnp.sum(g, axis=0, keepdims=True)
        ln_o[1:2, :] = jnp.sum(s, axis=0, keepdims=True)
        for k in range(steps):
            pl.when(core == k // 2)(lambda: down_copy(k, mine_s, mine_o).wait())
            pl.when(core != k // 2)(lambda: down_copy(k, sent_s, sent_o).wait())
            for copy in up_copies(k):
                copy.wait()


def finish_kernel(blocks, att, left, x, right, act, out_w, down_w, out_o, left_o, right_o):
    tiles = blocks // 2
    for r in range(tiles):
        rows = slice(r * 256, (r + 1) * 256)
        mid = two_blocks(left, x, right, r).astype(F32) + dot(att[rows, :], out_w[...])
        total = (mid + dot(act[rows, :], down_w[...])).astype(BF16)
        for h in range(2):
            block = 2 * r + h
            part = total[h * BLOCK : (h + 1) * BLOCK]
            if block == 0:
                left_o[...] = part
            elif block == blocks - 1:
                right_o[...] = part
            else:
                out_o[(block - 1) * BLOCK : block * BLOCK, :] = part


def finish_call(att, left, x, right, act, out_w, down_w):
    rows = att.shape[0]
    vmem = pl.BlockSpec(memory_space=pltpu.VMEM)
    edge = shape_of((HALO, D), BF16)
    return pl.pallas_call(
        functools.partial(finish_kernel, rows // BLOCK),
        in_specs=[vmem] * 7,
        out_specs=[vmem] * 3,
        out_shape=[shape_of(x.shape, BF16), edge, edge],
        compiler_params=pltpu.CompilerParams(vmem_limit_bytes=VMEM_LIMIT),
        cost_estimate=pl.CostEstimate(flops=4 * 10**9, bytes_accessed=12 * 10**6, transcendentals=0),
        name="finish",
    )(att, left, x, right, act, out_w, down_w)


def middle_kernel(scal, dbr, att, out_w, d_att_o, mine_o, sent_o):
    core = scal[0, CORE]
    for r in range(dbr.shape[0] // 256):
        rows = slice(r * 256, (r + 1) * 256)
        d_att_o[rows, :] = dot_t(dbr[rows, :], out_w[...]).astype(BF16)
    total = t_dot(att[...], dbr[...]).astype(BF16)
    for half in range(2):
        part = total[half * 256 : (half + 1) * 256].reshape(16, 16, 512)

        @pl.when(core == half)
        def _():
            for c in range(4):
                mine_o[:, c] = part[:, :, c * 128 : (c + 1) * 128]

        @pl.when(core != half)
        def _():
            for c in range(4):
                sent_o[:, c] = part[:, :, c * 128 : (c + 1) * 128]


def back_kernel(blocks, scal, d_att, att, lse, seg, qkv, normed, dqkv_o, mine_o, sent_o,
                q_s, kc, vx, dk_s, dv_s, bias_s, dqkv_s, normed_s):
    step = pl.program_id(0)
    core = scal[0, CORE]

    def rows_of(block, count=1):
        return pl.ds(pl.multiple_of(block * BLOCK, BLOCK), count * BLOCK)

    @pl.when(step < blocks // 2)
    def _():
        rows = rows_of(2 * step, 2)
        q_s[rows, :] = qkv[:, 0:512] * jnp.asarray(0.125, BF16)
        normed_s[rows, :] = normed[...]
        for h in range(2):
            part = slice(h * BLOCK, (h + 1) * BLOCK)
            split_pairs(qkv[part, 512:1024], qkv[part, 1024:1536], kc, vx, 2 * step + h)
        both = pl.ds(pl.multiple_of(step * 512, 512), 512)
        for p in range(PAIRS):
            dk_s[p, both, :] = jnp.zeros((512, 128), F32)
            dv_s[p, both, :] = jnp.zeros((512, 128), F32)

    @pl.when((step >= 1) & (step <= blocks // 2))
    def _():
        i = 2 * (step - 1)
        rows = rows_of(i, 2)
        low = scal[0, i]
        n_keys = scal[0, HIGH + i + 1] - low + 1
        keys_at = pl.multiple_of(low * 256, 256)
        seg_q = [jnp.broadcast_to(seg[i + h].astype(F32), (BLOCK, BLOCK)) for h in range(2)]

        def back(n):
            keys = pl.ds(keys_at, n * 256)
            for t in range(n):
                seg_k = column(seg[low + t].astype(F32))
                for h in range(2):
                    cols = slice(h * BLOCK, (h + 1) * BLOCK)
                    bias_s[t * BLOCK : (t + 1) * BLOCK, cols] = jnp.where(seg_k == seg_q[h], 0.0, -1e30)

            def pair(p, carry):
                cols = pl.ds(pl.multiple_of(p * 128, 128), 128)
                q = q_s[rows, cols]
                d_out = d_att[:, cols]
                minus = -(d_out.astype(F32) * att[:, cols].astype(F32))
                scores = dot_t(kc[p, keys, :], jnp.concatenate([q, lse[:, cols]], axis=1))
                d_probs = dot_t(vx[p, keys, :], jnp.concatenate([d_out, minus.astype(BF16)], axis=1))
                parts, d_parts = [], []
                for t in range(n):
                    bias = bias_s[t * BLOCK : (t + 1) * BLOCK, :]
                    for h in range(2):
                        part = slice((2 * t + h) * BLOCK, (2 * t + h + 1) * BLOCK)
                        probs = jnp.exp(scores[part] + bias)
                        parts.append(probs.astype(BF16))
                        d_parts.append((probs * d_probs[part]).astype(BF16))
                d_scores = jnp.concatenate(d_parts, axis=0)
                dk_s[p, keys, :] += dot(d_scores, q)
                dv_s[p, keys, :] += dot(jnp.concatenate(parts, axis=0), d_out)
                d_q = t_dot(d_scores, kc[p, keys, 0:128]) * 0.125
                dqkv_s[rows, pl.ds(pl.multiple_of(p * 384, 128), 128)] = d_q.astype(BF16)
                return carry

            lax.fori_loop(0, PAIRS, pair, 0, unroll=2)

        for n in range(1, 7):
            pl.when(n_keys == n)(functools.partial(back, n))

    @pl.when(step >= 2)
    def _():
        even = lax.broadcasted_iota(jnp.int32, (BLOCK, BLOCK), 1) < 64
        for h in range(2):
            block = 2 * (step - 2) + h
            rows = rows_of(block)
            up = pl.ds(pl.multiple_of(block * 256, 256), 128)
            down = pl.ds(pl.multiple_of(block * 256 + 128, 128), 128)
            for p in range(PAIRS):
                for t, source in enumerate((dk_s, dv_s)):
                    both = jnp.where(even, source[p, up, :], source[p, down, :])
                    spot = p * 384 + 128 + t * 128
                    dqkv_s[rows, spot : spot + 128] = both.astype(BF16)
        dqkv_o[...] = dqkv_s[rows_of(2 * (step - 2), 2), :]

    @pl.when(step == blocks // 2 + 1)
    def _():
        for p in range(PAIRS):
            part = t_dot(normed_s[...], dqkv_s[:, p * 384 : (p + 1) * 384]).astype(BF16)
            for half in range(2):
                piece = part[half * 256 : (half + 1) * 256].reshape(16, 16, 384)

                @pl.when(core == half)
                def _():
                    mine_o[:, p] = piece

                @pl.when(core != half)
                def _():
                    sent_o[:, p] = piece


def entry_kernel(blocks, left, x, right, dbr, gain, ln2, weight, d_qkv,
                 grad_o, left_o, right_o, small_o, w_s, x_s, ln_s, grad_s):
    r = pl.program_id(0)
    tiles = blocks // 2

    @pl.when(r == 0)
    def _():
        for p in range(PAIRS):
            for part in range(3):
                spot = part * 512 + p * 128
                to = p * 384 + part * 128
                w_s[:, to : to + 128] = weight[:, spot : spot + 128]
        for t in range(tiles):
            x_s[t * 256 : (t + 1) * 256, :] = two_blocks(left, x, right, t)
        ln_s[0:2, :] = jnp.zeros((2, D), F32)

    rows = pl.ds(pl.multiple_of(r * 256, 256), 256)
    d_n1 = dot_t(d_qkv[...], w_s[...])
    n1, inverse = normalize(x_s[rows, :].astype(F32))
    e = d_n1 * gain[...]
    mean_e = jnp.mean(e, axis=-1, keepdims=True)
    mean_en = jnp.mean(e * n1, axis=-1, keepdims=True)
    grad_s[rows, :] = dbr[...].astype(F32) + (e - mean_e - n1 * mean_en) * inverse
    ln_s[0:1, :] += jnp.sum(d_n1 * n1, axis=0, keepdims=True)
    ln_s[1:2, :] += jnp.sum(d_n1, axis=0, keepdims=True)

    @pl.when(r == tiles - 1)
    def _():
        inner = (blocks - 2) * BLOCK
        grad_o[...] = grad_s[HALO : HALO + inner, :]
        left_o[...] = grad_s[0:HALO, :].astype(BF16)
        right_o[...] = grad_s[HALO + inner :, :].astype(BF16)
        vectors = [ln_s[0:1, :], ln_s[1:2, :], ln2[0:1, :], ln2[1:2, :]]
        small_o[...] = jnp.concatenate(
            [v[:, c * 128 : (c + 1) * 128] for v in vectors for c in range(4)], axis=0
        )


def join_kernel(share, mine, other, out_m, out_o, result):
    wide = share.shape[-1]
    result[:, :, :, 0:wide] = jnp.broadcast_to(share[...][None, None], (*result.shape[:2], *share.shape))
    value = mine[...].astype(F32) + other[...].astype(F32)
    result[:, :, :, wide : wide + 384] = value.astype(BF16)
    value = out_m[...].astype(F32) + out_o[...].astype(F32)
    result[:, :, :, wide + 384 : wide + 512] = value.astype(BF16)


def join_call(share, mine, other, out_m, out_o):
    at = lambda s: (s, 0, 0, 0)
    block = (8, 4, 16, share.shape[-1] + 512)
    return pl.pallas_call(
        join_kernel,
        grid=(2,),
        in_specs=[pl.BlockSpec(share.shape, lambda s: (0, 0))]
        + [pl.BlockSpec((8, 4, 16, 384), at)] * 2 + [pl.BlockSpec((8, 4, 16, 128), at)] * 2,
        out_specs=pl.BlockSpec(block, at),
        out_shape=shape_of((16, *block[1:]), BF16),
        compiler_params=params(),
        name="join",
    )(share, mine, other, out_m, out_o)


def whole(shape):
    return pl.BlockSpec(shape, lambda s, scal: (0,) * len(shape))


def shape_of(shape, dtype):
    return jax.ShapeDtypeStruct(shape, dtype)


def params():
    return pltpu.CompilerParams(
        dimension_semantics=("arbitrary",), vmem_limit_bytes=VMEM_LIMIT
    )


def attend_call(scal, left, x, right, seg, gain, shift, weight):
    rows = x.shape[0] + 2 * HALO
    blocks = rows // BLOCK
    at = lambda s, scal: (jnp.maximum(s - 1, 0), 0)
    return pl.pallas_call(
        functools.partial(attend_kernel, blocks),
        grid_spec=pltpu.PrefetchScalarGridSpec(
            num_scalar_prefetch=1,
            grid=(blocks // 2 + 1,),
            in_specs=[
                whole((HALO, D)), whole(x.shape), whole((HALO, D)), whole(seg.shape),
                whole((1, D)), whole((1, D)), whole(weight.shape),
            ],
            out_specs=[
                pl.BlockSpec(memory_space=pl.ANY),
                pl.BlockSpec(memory_space=pl.ANY),
                pl.BlockSpec((2 * BLOCK, D), at),
                pl.BlockSpec((2 * BLOCK, D), at),
            ],
            scratch_shapes=[
                pltpu.VMEM((rows, D), BF16),
                pltpu.VMEM((rows, 3 * D), BF16),
                pltpu.VMEM((PAIRS, blocks * 256, 128), BF16),
                pltpu.VMEM((PAIRS, blocks * 256, 256), BF16),
                pltpu.SemaphoreType.DMA((blocks,)),
            ],
        ),
        out_shape=[
            shape_of((rows, D), BF16),
            shape_of((rows, 3 * D), BF16),
            shape_of((rows, D), BF16),
            shape_of((rows, D), BF16),
        ],
        compiler_params=params(),
        cost_estimate=pl.CostEstimate(flops=8 * 10**9, bytes_accessed=25 * 10**6, transcendentals=4 * 10**6),
        name="attend",
    )(scal, left, x, right, seg, gain, shift, weight)


def feed_call(scal, att, left, x, right, cot_l, cot, cot_r, out_w, up_w, down_w, gain, shift):
    rows = att.shape[0]
    blocks = rows // BLOCK
    half = (16, 4, 16, 1024)
    anywhere = pl.BlockSpec(memory_space=pl.ANY)
    return pl.pallas_call(
        functools.partial(feed_kernel, blocks),
        grid_spec=pltpu.PrefetchScalarGridSpec(
            num_scalar_prefetch=1,
            grid=(FF // 512,),
            in_specs=[
                whole((rows, D)),
                whole((HALO, D)), whole(x.shape), whole((HALO, D)),
                whole((HALO, D)), whole(x.shape), whole((HALO, D)),
                whole((D, D)),
                pl.BlockSpec((D, 512), lambda s, scal: (0, s)),
                pl.BlockSpec((512, D), lambda s, scal: (s, 0)),
                whole((1, D)), whole((1, D)),
            ],
            out_specs=[
                whole((rows, D)), pl.BlockSpec((rows, 512), lambda s, scal: (0, s)), whole((2, D)),
                anywhere, anywhere,
            ],
            scratch_shapes=[
                pltpu.VMEM((rows, D), F32),
                pltpu.VMEM((rows, 128), F32),
                pltpu.VMEM((rows, D), BF16),
                pltpu.VMEM(half, BF16),
                pltpu.VMEM(half, BF16),
                pltpu.SemaphoreType.DMA((3 * (FF // 512),)),
                pltpu.VMEM((rows, D), BF16),
                pltpu.VMEM((FF // 512, rows, 512), BF16),
                pltpu.VMEM((FF // 512, D, 512), BF16),
            ] + [pltpu.VMEM((256, 512), F32)] * 4,
        ),
        out_shape=[
            shape_of((rows, D), BF16),
            shape_of((rows, FF), BF16),
            shape_of((2, D), F32),
            shape_of(half, BF16),
            shape_of(half, BF16),
        ],
        compiler_params=params(),
        cost_estimate=pl.CostEstimate(flops=16 * 10**9, bytes_accessed=25 * 10**6, transcendentals=3 * 10**6),
        name="feed",
    )(scal, att, left, x, right, cot_l, cot, cot_r, out_w, up_w, down_w, gain, shift)


def middle_call(scal, dbr, att, out_w):
    part = (16, 4, 16, 128)
    vmem = pl.BlockSpec(memory_space=pltpu.VMEM)
    return pl.pallas_call(
        middle_kernel,
        in_specs=[pl.BlockSpec(memory_space=pltpu.SMEM)] + [vmem] * 3,
        out_specs=[vmem] * 3,
        out_shape=[shape_of(dbr.shape, BF16), shape_of(part, BF16), shape_of(part, BF16)],
        compiler_params=pltpu.CompilerParams(vmem_limit_bytes=VMEM_LIMIT),
        cost_estimate=pl.CostEstimate(flops=2 * 10**9, bytes_accessed=5 * 10**6, transcendentals=0),
        name="middle",
    )(scal, dbr, att, out_w)


def back_call(scal, d_att, att, lse, seg, qkv, normed):
    rows = qkv.shape[0]
    blocks = rows // BLOCK
    half = (16, PAIRS, 16, 384)
    last = blocks // 2 - 1
    lead = lambda s, scal: (jnp.minimum(s, last), 0)
    now = lambda s, scal: (jnp.clip(s - 1, 0, last), 0)
    done = lambda s, scal: (jnp.maximum(s - 2, 0), 0)
    return pl.pallas_call(
        functools.partial(back_kernel, blocks),
        grid_spec=pltpu.PrefetchScalarGridSpec(
            num_scalar_prefetch=1,
            grid=(blocks // 2 + 2,),
            in_specs=[
                pl.BlockSpec((2 * BLOCK, D), now), pl.BlockSpec((2 * BLOCK, D), now), pl.BlockSpec((2 * BLOCK, D), now),
                whole(seg.shape),
                pl.BlockSpec((2 * BLOCK, 3 * D), lead), pl.BlockSpec((2 * BLOCK, D), lead),
            ],
            out_specs=[pl.BlockSpec((2 * BLOCK, 3 * D), done), whole(half), whole(half)],
            scratch_shapes=[
                pltpu.VMEM((rows, D), BF16),
                pltpu.VMEM((PAIRS, blocks * 256, 256), BF16),
                pltpu.VMEM((PAIRS, blocks * 256, 256), BF16),
                pltpu.VMEM((PAIRS, blocks * 256, 128), F32),
                pltpu.VMEM((PAIRS, blocks * 256, 128), F32),
                pltpu.VMEM((6 * BLOCK, 2 * BLOCK), F32),
                pltpu.VMEM((rows, 3 * D), BF16),
                pltpu.VMEM((rows, D), BF16),
            ],
        ),
        out_shape=[shape_of((rows, 3 * D), BF16), shape_of(half, BF16), shape_of(half, BF16)],
        compiler_params=params(),
        cost_estimate=pl.CostEstimate(flops=12 * 10**9, bytes_accessed=20 * 10**6, transcendentals=4 * 10**6),
        name="back",
    )(scal, d_att, att, lse, seg, qkv, normed)


def entry_call(left, x, right, dbr, gain, ln2, weight, d_qkv):
    rows = dbr.shape[0]
    fixed = lambda v: pl.BlockSpec(v.shape, lambda s: (0,) * len(v.shape))
    at = lambda s: (s, 0)
    edge = shape_of((HALO, D), BF16)
    outs = [shape_of(x.shape, F32), edge, edge, shape_of((16, 128), F32)]
    return pl.pallas_call(
        functools.partial(entry_kernel, rows // BLOCK),
        grid=(rows // 256,),
        in_specs=[
            fixed(left), fixed(x), fixed(right), pl.BlockSpec((256, D), at), fixed(gain), fixed(ln2),
            fixed(weight), pl.BlockSpec((256, 3 * D), at),
        ],
        out_specs=[fixed(v) for v in outs],
        out_shape=outs,
        scratch_shapes=[
            pltpu.VMEM((D, 3 * D), BF16), pltpu.VMEM((rows, D), BF16), pltpu.VMEM((8, D), F32),
            pltpu.VMEM((rows, D), F32),
        ],
        compiler_params=params(),
        cost_estimate=pl.CostEstimate(flops=2 * 10**9, bytes_accessed=15 * 10**6, transcendentals=0),
        name="entry",
    )(left, x, right, dbr, gain, ln2, weight, d_qkv)


def other_core(value):
    return lax.ppermute(value, "core", [(0, 1), (1, 0)])


def all_shares(value, groups):
    parts = lax.all_to_all(value, ("rows", "x"), 0, 0, tiled=True)
    return jnp.sum(parts.astype(F32), axis=0).astype(BF16)


def gather_shares(share, groups):
    copies = jnp.broadcast_to(share[None], (groups, *share.shape))
    return lax.all_to_all(copies, ("rows", "x"), 0, 0, tiled=True)


def per_device(
    inputs, qkv_weight, out_weight, up_weight, down_weight, norm1_gain, norm1_shift,
    norm2_gain, norm2_shift, segment_ids, item_steps, gen_rank, out_grad,
):
    x = inputs[0]
    positions = x.shape[0]
    blocks = (positions + 2 * HALO) // BLOCK
    chips = lax.axis_size("rows") * lax.axis_size("x")
    seq_parts = lax.axis_size("x") * lax.axis_size("core")
    seq = ("x", "core")
    to_right = [(i, (i + 1) % seq_parts) for i in range(seq_parts)]
    to_left = [((i + 1) % seq_parts, i) for i in range(seq_parts)]

    place = jnp.stack([lax.axis_index(seq), lax.axis_index("core")]).astype(jnp.int32)
    tie = lax.optimization_barrier
    left = lax.ppermute(x[positions - HALO :], seq, to_right)
    right = lax.ppermute(x[:HALO], seq, to_left)
    scal, seg_rows, cot, send_l, send_r = prepare_call(
        place, segment_ids, item_steps, gen_rank, out_grad[0]
    )
    cot_l = lax.ppermute(send_r, seq, to_right)
    cot_r = lax.ppermute(send_l, seq, to_left)

    gain1, shift1 = norm1_gain.reshape(1, D), norm1_shift.reshape(1, D)
    gain2, shift2 = norm2_gain.reshape(1, D), norm2_shift.reshape(1, D)
    normed1, qkv, att, lse = attend_call(
        scal, left, x, right, seg_rows, gain1, shift1, qkv_weight
    )
    d_branch, act, ln2, mine_a, sent_a = feed_call(
        scal, att, left, x, right, cot_l, cot, cot_r, out_weight, up_weight, down_weight, gain2, shift2
    )
    got_a = other_core(sent_a)
    half_a = (mine_a.astype(F32) + got_a.astype(F32)).astype(BF16)
    d_att, mine_o, sent_o = middle_call(scal, d_branch, att, out_weight)
    d_att, half_a = tie((d_att, half_a))
    share_a = all_shares(half_a.reshape(chips, -1, 1024), chips)
    d_qkv, mine_b, sent_b = back_call(scal, d_att, att, lse, seg_rows, qkv, normed1)
    joined = join_call(share_a, mine_b, other_core(sent_b), mine_o, other_core(sent_o))
    joined, d_branch, att = tie((joined, d_branch, att))
    got = lax.all_to_all(joined.reshape(chips, -1, 1536), ("rows", "x"), 0, 0, tiled=True)
    grad, grad_l, grad_r, small = entry_call(
        left, x, right, d_branch, gain1, ln2, qkv_weight, d_qkv
    )
    small = small + other_core(small)
    out, out_l, out_r = finish_call(att, left, x, right, act, out_weight, down_weight)
    edge_l = jnp.concatenate([out_l, grad_l], axis=0)
    edge_r = jnp.concatenate([out_r, grad_r], axis=0)
    from_r = lax.ppermute(edge_l, seq, to_left)
    from_l = lax.ppermute(edge_r, seq, to_right)
    got, from_l, from_r, small = tie((got, from_l, from_r, small))
    far_a = other_core(got)
    share_b = jnp.sum(got[:, :, 1024:].astype(F32), axis=0).astype(BF16)
    near_b = gather_shares(jnp.concatenate([share_b, small.astype(BF16)], axis=1), chips)
    feed_shapes, rest_shapes = ((FF, D), (D, FF)), ((D, D), (D, 3 * D))
    grads_a = unpack_call(unpack_feed, feed_shapes, scal, got.reshape(16, 4, 16, 1536))
    grad_down, grad_up = unpack_call(
        unpack_feed, feed_shapes, scal, far_a.reshape(16, 4, 16, 1536), grads_a
    )
    output, input_grad = patch_call(scal, out, grad, seg_rows, from_l, from_r)
    near_b, grad_down, input_grad = tie((near_b, grad_down, input_grad))
    far_b = other_core(near_b)
    *grads_b, v0, v1, v2, v3 = unpack_call(
        unpack_rest, rest_shapes, scal, near_b.reshape(16, 4, 16, 640), steps=1, extra=((1, D),) * 4
    )
    vectors = [v.reshape(D) for v in (v0, v1, v2, v3)]
    grad_out, grad_qkv = unpack_call(
        unpack_rest, rest_shapes, scal, far_b.reshape(16, 4, 16, 640), grads_b, steps=1
    )
    return (
        output[None], input_grad[None], grad_qkv, grad_out, grad_up, grad_down,
        vectors[0], vectors[1], vectors[2], vectors[3],
    )


def solution(mesh):
    rows = mesh.devices.shape[0]
    parts = mesh.devices.shape[1]
    split = Mesh(mesh.devices.reshape(rows, parts // 2, 2), ("rows", "x", "core"))
    seq = ("x", "core")
    return jax.shard_map(
        per_device,
        mesh=split,
        in_specs=(
            P("rows", seq, None), P(), P(), P(), P(), P(), P(), P(), P(),
            P("rows", None), P("rows", None), P("rows", seq), P("rows", seq, None),
        ),
        out_specs=(
            P("rows", seq, None), P("rows", seq, None),
            P(), P(), P(), P(), P(), P(), P(), P(),
        ),
        check_vma=False,
    )
```

```python
import functools

import jax
import jax.numpy as jnp
from jax import lax
from jax.experimental import pallas as pl
from jax.experimental.pallas import tpu as pltpu
from jax.sharding import Mesh
from jax.sharding import PartitionSpec as P

D = 512
HEADS = 8
PAIRS = HEADS // 2
FF = 2048
EPS = 1e-05
HALO = 128
BLOCK = 128
BF16 = jnp.bfloat16
F32 = jnp.float32
MIB = 1024 * 1024
HIGH, CORE, DROP_L, DROP_R = 16, 32, 33, 34


def dot(a, b):
    return lax.dot_general(a, b, (((1,), (0,)), ((), ())), preferred_element_type=F32)


def dot_t(a, b):
    return lax.dot_general(a, b, (((1,), (1,)), ((), ())), preferred_element_type=F32)


def t_dot(a, b):
    return lax.dot_general(a, b, (((0,), (0,)), ((), ())), preferred_element_type=F32)


def normalize(value):
    center = jnp.mean(value, axis=-1, keepdims=True)
    centred = value - center
    spread = jnp.mean(centred * centred, axis=-1, keepdims=True)
    inverse = lax.rsqrt(spread + EPS)
    return centred * inverse, inverse


def two_blocks(left, middle, right, tile):
    last = 1 + middle.shape[0] // BLOCK
    parts = []
    for block in (2 * tile, 2 * tile + 1):
        if block == 0:
            parts.append(left[...])
        elif block == last:
            parts.append(right[...])
        else:
            parts.append(middle[(block - 1) * BLOCK : block * BLOCK, :])
    return jnp.concatenate(parts, axis=0)


def split_pairs(keys, values, kc, vx, block):
    lane = lax.broadcasted_iota(jnp.int32, (BLOCK, BLOCK), 1)
    even = lane < 64
    zero = jnp.zeros((BLOCK, BLOCK), BF16)
    ones_even = even.astype(F32).astype(BF16)
    ones_odd = (~even).astype(F32).astype(BF16)
    base = block * 256
    for p in range(PAIRS):
        k = keys[:, p * 128 : (p + 1) * 128]
        v = values[:, p * 128 : (p + 1) * 128]
        kc[p, pl.ds(base, 128), 0:128] = jnp.where(even, k, zero)
        kc[p, pl.ds(base + 128, 128), 0:128] = jnp.where(even, zero, k)
        vx[p, pl.ds(base, 128), 0:128] = jnp.where(even, v, zero)
        vx[p, pl.ds(base + 128, 128), 0:128] = jnp.where(even, zero, v)
        vx[p, pl.ds(base, 128), 128:256] = ones_even
        vx[p, pl.ds(base + 128, 128), 128:256] = ones_odd
        if kc.shape[2] == 256:
            minus = jnp.where(lax.rem(lane, 64) < 3, -1.0, 0.0)
            kc[p, pl.ds(base, 128), 128:256] = jnp.where(even, minus, 0.0).astype(BF16)
            kc[p, pl.ds(base + 128, 128), 128:256] = jnp.where(even, 0.0, minus).astype(BF16)


def mask_rows(seg, row, low, n):
    seg_q = column(seg[row].astype(F32))
    return [
        jnp.where(seg_q == jnp.broadcast_to(seg[low + t].astype(F32), (BLOCK, BLOCK)), 0.0, -1e30)
        for t in range(n)
    ]


def column(row):
    return jnp.transpose(jnp.broadcast_to(row, (BLOCK, BLOCK)))


def keep_rows(values, mask):
    return jnp.concatenate(
        [
            jnp.where(mask, values[:, c * 128 : (c + 1) * 128].astype(F32), 0.0).astype(BF16)
            for c in range(D // 128)
        ],
        axis=1,
    )


def prepare_kernel(inner, place, segments, steps, rank, out_grad, scal_o, seg_o, cot_o, left_o, right_o, part_s):
    seq = place[0]
    row_blocks = segments.shape[1] // BLOCK
    blocks = inner + 2
    rows = []
    for b in range(blocks):
        at = seq * inner + b - 1
        if b == 0:
            at = jnp.maximum(at, 0)
        if b == blocks - 1:
            at = jnp.minimum(at, row_blocks - 1)
        row = segments[0:1, pl.ds(pl.multiple_of(at * BLOCK, BLOCK), BLOCK)]
        if b == 0:
            row = jnp.where(seq > 0, row, -1)
        if b == blocks - 1:
            row = jnp.where(seq * inner + inner < row_blocks, row, 1000)
        rows.append(row)
        seg_o[b] = row
    window = jnp.concatenate(rows, axis=0)
    local = window[1 : inner + 1]
    first, last = window[:, 0:1], window[:, BLOCK - 1 : BLOCK]
    below = jnp.zeros(window.shape, F32)
    upto = jnp.zeros(window.shape, F32)
    for row in rows:
        below += (row < first).astype(F32)
        upto += (row <= last).astype(F32)
    part_s[...] = jnp.zeros(part_s.shape, F32)
    part_s[0:blocks, :] = below
    part_s[HIGH : HIGH + blocks, :] = upto
    counts = dot_t(jnp.ones((8, BLOCK), BF16), part_s[...].astype(BF16))[0:1]

    def border(before, after):
        value = before[-1:, BLOCK - 1 : BLOCK]
        across = value == after[0:1, 0:1]
        sizes = [jnp.sum((part == value).astype(F32), axis=(0, 1), keepdims=True) for part in (before, after)]
        return value, across, sizes[0] >= sizes[1]

    value_l, across_l, to_left_l = border(rows[0], local)
    value_r, across_r, to_left_r = border(local, rows[-1])
    drop_l = jnp.where(across_l & to_left_l, value_l, -2)
    drop_r = jnp.where(across_r & jnp.logical_not(to_left_r), value_r, -2)
    lane = lax.broadcasted_iota(jnp.int32, (1, BLOCK), 1)
    at_block = jnp.floor(jnp.where(lane >= HIGH, counts - 1.0, counts) * (1.0 / BLOCK)).astype(jnp.int32)
    at_block = jnp.where(lane == CORE, place[1], at_block)
    at_block = jnp.where(lane == DROP_L, drop_l, at_block)
    scal_o[...] = jnp.where(lane == DROP_R, drop_r, at_block)

    token = jnp.zeros(local.shape, jnp.int32)
    for slot in range(steps.shape[1]):
        token = jnp.where(local == slot, steps[0, slot], token)
    for b in range(inner):
        part = slice(b * BLOCK, (b + 1) * BLOCK)
        keep = rank[0:1, part] >= token[b : b + 1]
        seg = rows[b + 1]
        own = (seg != drop_l) & (seg != drop_r)
        values = out_grad[part, :]
        cot_o[part, :] = keep_rows(values, column((keep & own).astype(F32)) > 0.5)
        if b == 0:
            left_o[...] = keep_rows(values, column((keep & (seg == drop_l)).astype(F32)) > 0.5)
        if b == inner - 1:
            right_o[...] = keep_rows(values, column((keep & (seg == drop_r)).astype(F32)) > 0.5)


def prepare_call(place, segments, steps, rank, out_grad):
    inner = out_grad.shape[0] // BLOCK
    vmem = pl.BlockSpec(memory_space=pltpu.VMEM)
    smem = pl.BlockSpec(memory_space=pltpu.SMEM)
    return pl.pallas_call(
        functools.partial(prepare_kernel, inner),
        in_specs=[smem, vmem, smem, vmem, vmem],
        out_specs=[vmem] * 5,
        out_shape=[
            shape_of((1, BLOCK), jnp.int32),
            shape_of((inner + 2, 1, BLOCK), jnp.int32),
            shape_of(out_grad.shape, BF16),
            shape_of((HALO, D), BF16),
            shape_of((HALO, D), BF16),
        ],
        scratch_shapes=[pltpu.VMEM((BLOCK, BLOCK), F32)],
        compiler_params=pltpu.CompilerParams(vmem_limit_bytes=58 * MIB),
        cost_estimate=pl.CostEstimate(flops=10**6, bytes_accessed=4 * 10**6, transcendentals=0),
        name="prepare",
    )(place, segments, steps, rank, out_grad)


def patch_kernel(blocks, scal, out, grad, seg, left, right, out_o, grad_o):
    step = pl.program_id(0)
    drop_l, drop_r = scal[0, DROP_L], scal[0, DROP_R]
    row = seg[0]
    drop = jnp.where(step == 0, drop_l, drop_r)
    lost = column((row == drop).astype(F32)) > 0.5
    for c in range(D // 128):
        cols = slice(c * 128, (c + 1) * 128)
        for mine, start, result in ((out, 0, out_o), (grad, HALO, grad_o)):
            part = slice(start, start + HALO)
            other = jnp.where(step == 0, left[part, cols].astype(F32), right[part, cols].astype(F32))
            value = jnp.where(lost, other, mine[:, cols].astype(F32))
            result[:, cols] = value.astype(result.dtype)


def patch_call(scal, out, grad, seg, left, right):
    inner = out.shape[0] // BLOCK
    block = lambda s, scal: (s * (inner - 1), 0)
    return pl.pallas_call(
        functools.partial(patch_kernel, inner + 2),
        grid_spec=pltpu.PrefetchScalarGridSpec(
            num_scalar_prefetch=1,
            grid=(2,),
            in_specs=[
                pl.BlockSpec((BLOCK, D), block),
                pl.BlockSpec((BLOCK, D), block),
                pl.BlockSpec((1, 1, BLOCK), lambda s, scal: (1 + s * (inner - 1), 0, 0)),
                whole((2 * HALO, D)), whole((2 * HALO, D)),
            ],
            out_specs=[pl.BlockSpec((BLOCK, D), block), pl.BlockSpec((BLOCK, D), block)],
        ),
        out_shape=[shape_of(out.shape, out.dtype), shape_of(grad.shape, grad.dtype)],
        input_output_aliases={1: 0, 2: 1},
        compiler_params=params(),
        name="patch",
    )(scal, out, grad, seg, left, right)


def unpack_feed(a, down_o, up_o):
    rows = a.shape[0] * 16
    down_o[...] = a[:, :, :, 0:512].astype(F32).reshape(4 * rows, 512)
    for c in range(4):
        up_o[:, c * 512 : (c + 1) * 512] = a[:, c, :, 512:1024].astype(F32).reshape(rows, 512)


def rest_kernel(scal, near, far, out_o, qkv_o, *vectors_o):
    step = pl.program_id(0)

    def unpack(a):
        rows = pl.ds(step % 2 * 8, 8)
        for c in range(4):
            value = a[rows, c, :, 0:512].astype(F32).reshape(128, 512)
            for part in range(3):
                spot = part * 512 + c * 128
                qkv_o[:, spot : spot + 128] = value[:, part * 128 : (part + 1) * 128]
            out_o[:, c * 128 : (c + 1) * 128] = value[:, 384:512]

    pl.when(step // 2 == scal[0, CORE])(lambda: unpack(near))
    pl.when(step // 2 != scal[0, CORE])(lambda: unpack(far))

    @pl.when(step == 0)
    def _():
        part = jnp.sum(near[:, :, :, 512:640].astype(F32), axis=(0, 1))
        for v in range(4):
            vectors_o[v][...] = jnp.concatenate([part[4 * v + c : 4 * v + c + 1] for c in range(4)], axis=1)


def rest_call(scal, near, far):
    part = lambda s, scal: (s, 0)
    return pl.pallas_call(
        rest_kernel,
        grid_spec=pltpu.PrefetchScalarGridSpec(
            num_scalar_prefetch=1,
            grid=(4,),
            in_specs=[whole(near.shape), whole(far.shape)],
            out_specs=[pl.BlockSpec((128, D), part), pl.BlockSpec((128, 3 * D), part)] + [whole((1, D))] * 4,
        ),
        out_shape=[shape_of((D, D), F32), shape_of((D, 3 * D), F32)] + [shape_of((1, D), F32)] * 4,
        compiler_params=params(24),
        cost_estimate=pl.CostEstimate(flops=10**6, bytes_accessed=7 * 10**6, transcendentals=0),
        name="rest",
    )(scal, near, far)


def unpack_call(scal, value, before=()):
    steps = 4

    def out(s, scal):
        half = scal[0, CORE] if not before else 1 - scal[0, CORE]
        return (half * steps + s, 0)

    def kernel(scal, a, *refs):
        unpack_feed(a, *refs[len(before) :])

    shapes = ((FF, D), (D, FF))
    return pl.pallas_call(
        kernel,
        grid_spec=pltpu.PrefetchScalarGridSpec(
            num_scalar_prefetch=1,
            grid=(steps,),
            in_specs=[pl.BlockSpec((16 // steps, *value.shape[1:]), lambda s, scal: (s, 0, 0, 0))]
            + [pl.BlockSpec(memory_space=pl.ANY)] * len(before),
            out_specs=[pl.BlockSpec((rows // (2 * steps), cols), out) for rows, cols in shapes],
        ),
        out_shape=[shape_of(shape, F32) for shape in shapes],
        input_output_aliases={2 + k: k for k in range(len(before))},
        compiler_params=params(24),
        cost_estimate=pl.CostEstimate(flops=10**6, bytes_accessed=10 * 10**6, transcendentals=0),
        name="unpack",
    )(scal, value, *before)


def attend_kernel(blocks, scal, left, x, right, seg, gain, shift, weight,
                  normed_o, qkv_o, att_o, lse_o, normed_s, qkv_s, kc, vx, sems):
    step = pl.program_id(0)
    tiles = blocks // 2

    def copies(r):
        rows = slice(r * 256, (r + 1) * 256)
        return (
            pltpu.make_async_copy(normed_s.at[rows, :], normed_o.at[rows, :], sems.at[2 * r]),
            pltpu.make_async_copy(qkv_s.at[rows, :], qkv_o.at[rows, :], sems.at[2 * r + 1]),
        )

    @pl.when(step == 0)
    def _():
        for r in range(tiles + 1):
            if r < tiles:
                base, _ = normalize(two_blocks(left, x, right, r).astype(F32))
                normed_s[r * 256 : (r + 1) * 256, :] = (base * gain[...] + shift[...]).astype(BF16)
            if r > 0:
                rows = slice((r - 1) * 256, r * 256)
                qkv = dot(normed_s[rows, :], weight[...]).astype(BF16)
                qkv_s[rows, :] = qkv
                for half in range(2):
                    part = qkv[half * 128 : (half + 1) * 128]
                    split_pairs(part[:, 512:1024], part[:, 1024:1536], kc, vx, 2 * (r - 1) + half)
                for copy in copies(r - 1):
                    copy.start()

    @pl.when(step > 0)
    def _():
        lane = lax.broadcasted_iota(jnp.int32, (BLOCK, BLOCK), 1)
        place = lax.rem(lane, 64)
        for h in range(2):
            i = 2 * (step - 1) + h
            rows = pl.ds(pl.multiple_of(i * BLOCK, BLOCK), BLOCK)
            part = slice(h * BLOCK, (h + 1) * BLOCK)
            low = scal[0, i]
            n_keys = scal[0, HIGH + i] - low + 1
            first = pl.multiple_of(low * 256, 256)

            def attend(n):
                bias = mask_rows(seg, i, low, n)
                def pair(p, carry):
                    cols = pl.ds(pl.multiple_of(p * 128, 128), 128)
                    q = qkv_s[rows, cols] * jnp.asarray(0.125, BF16)
                    scores = dot_t(q, kc[p, pl.ds(first, n * 256), :])
                    tiles_s = [
                        [scores[:, t * 256 + o * 128 : t * 256 + o * 128 + 128] + bias[t] for t in range(n)]
                        for o in range(2)
                    ]
                    highest = [
                        jnp.max(functools.reduce(jnp.maximum, tiles_s[o]), axis=-1, keepdims=True)
                        for o in range(2)
                    ]
                    pieces = []
                    for t in range(n):
                        for o in range(2):
                            pieces.append(jnp.exp(tiles_s[o][t] - highest[o]).astype(BF16))
                    mixed = dot(jnp.concatenate(pieces, axis=1), vx[p, pl.ds(first, n * 256), :])
                    total = mixed[:, 128:256]
                    att_o[part, cols] = (mixed[:, 0:128] * (1.0 / total)).astype(BF16)
                    lse = jnp.where(lane < 64, highest[0], highest[1]) + jnp.log(total)
                    top = lse.astype(BF16).astype(F32)
                    rest = lse - top
                    second = rest.astype(BF16).astype(F32)
                    third = jnp.where(place == 2, rest - second, 0.0)
                    lse_o[part, cols] = jnp.where(
                        place == 0, top, jnp.where(place == 1, second, third)
                    ).astype(BF16)
                    return carry

                lax.fori_loop(0, PAIRS, pair, 0, unroll=PAIRS)

            for n in range(1, 6):
                pl.when(n_keys == n)(functools.partial(attend, n))

    @pl.when(step == tiles)
    def _():
        for r in range(tiles):
            for copy in copies(r):
                copy.wait()


def gelu_both(v):
    c = 0.7978845608028654
    square = v * v
    inner = c + (0.044715 * c) * square
    gate = 0.5 + 0.5 * jnp.tanh(v * inner)
    act = v * gate
    slope = gate + act * ((1.0 - gate) * (6.0 * inner - 4.0 * c))
    return act, slope


def feed_kernel(blocks, scal, att, left, x, right, cot_l, cot, cot_r, out_w, up_w, down_w, gain, shift,
                dbr_o, act_o, ln_o, mine_o, sent_o,
                base_s, rstd_s, cot_s, mine_s, sent_s, sems, n2_s, dpre_s, up_s, *stage_s):
    f = pl.program_id(0)
    steps = FF // 512
    tiles = blocks // 2
    core = scal[0, CORE]

    def down_copy(k, from_s, to_o):
        spot = (slice((k % 2) * 8, (k % 2) * 8 + 8), slice(None), slice(None), slice(0, 512))
        return pltpu.make_async_copy(from_s.at[spot], to_o.at[spot], sems.at[k])

    def up_copies(k):
        spot = (slice(None), slice(k, k + 1), slice(None), slice(512, 1024))
        return [
            pltpu.make_async_copy(mine_s.at[spot], mine_o.at[spot], sems.at[steps + k]),
            pltpu.make_async_copy(sent_s.at[spot], sent_o.at[spot], sems.at[2 * steps + k]),
        ]

    @pl.when(f == 0)
    def _():
        for r in range(tiles):
            rows = slice(r * 256, (r + 1) * 256)
            cot_s[rows, :] = two_blocks(cot_l, cot, cot_r, r)
            mid = two_blocks(left, x, right, r).astype(F32) + dot(att[rows, :], out_w[...])
            base, inverse = normalize(mid)
            base_s[rows, :] = base
            rstd_s[rows, :] = jnp.broadcast_to(inverse, (256, 128))
            n2_s[rows, :] = (base * gain[...] + shift[...]).astype(BF16)

    up_s[f] = up_w[...]
    for r in range(tiles + 1):
        if r < tiles:
            rows = slice(r * 256, (r + 1) * 256)
            stage_s[r % 2][...] = dot(n2_s[rows, :], up_w[...])
            stage_s[2 + r % 2][...] = dot_t(cot_s[rows, :], down_w[...])
        if r > 0:
            rows = slice((r - 1) * 256, r * 256)
            act, slope = gelu_both(stage_s[(r - 1) % 2][...])
            act_o[rows, :] = act.astype(BF16)
            dpre_s[f, rows, :] = (slope * stage_s[2 + (r - 1) % 2][...]).astype(BF16)
    grad_down = t_dot(act_o[...], cot_s[...]).astype(BF16).reshape(8, 4, 16, 512)
    grad_up = t_dot(n2_s[...], dpre_s[f]).astype(BF16).reshape(2, 16, 1, 16, 512)

    for k in range(steps):

        @pl.when((f == k) & (core == k // 2))
        def _():
            mine_s[(k % 2) * 8 : (k % 2) * 8 + 8, :, :, 0:512] = grad_down
            down_copy(k, mine_s, mine_o).start()

        @pl.when((f == k) & (core != k // 2))
        def _():
            sent_s[(k % 2) * 8 : (k % 2) * 8 + 8, :, :, 0:512] = grad_down
            down_copy(k, sent_s, sent_o).start()

    for half in range(2):

        @pl.when(core == half)
        def _():
            mine_s[:, pl.ds(f, 1), :, 512:1024] = grad_up[half]
            sent_s[:, pl.ds(f, 1), :, 512:1024] = grad_up[1 - half]

    for k in range(steps):

        @pl.when(f == k)
        def _():
            for copy in up_copies(k):
                copy.start()

    @pl.when(f == steps - 1)
    def _():
        def turn(r, carry):
            rows = pl.ds(pl.multiple_of(r * 256, 256), 256)
            d_pre = jnp.concatenate([dpre_s[k, rows, :] for k in range(steps)], axis=1)
            up = jnp.concatenate([up_s[k] for k in range(steps)], axis=1)
            d_n2 = dot_t(d_pre, up)
            n2 = base_s[rows, :]
            inverse = jnp.concatenate([rstd_s[rows, :]] * 4, axis=1)
            e = d_n2 * gain[...]
            mean_e = jnp.mean(e, axis=-1, keepdims=True)
            mean_en = jnp.mean(e * n2, axis=-1, keepdims=True)
            d_mid = cot_s[rows, :].astype(F32) + (e - mean_e - n2 * mean_en) * inverse
            dbr_o[rows, :] = d_mid.astype(BF16)
            g, s = carry
            return (
                g + jnp.sum((d_n2 * n2).reshape(32, 8, D), axis=0),
                s + jnp.sum(d_n2.reshape(32, 8, D), axis=0),
            )

        zero = jnp.zeros((8, D), F32)
        g, s = lax.fori_loop(0, tiles, turn, (zero, zero))
        ln_o[0:1, :] = jnp.sum(g, axis=0, keepdims=True)
        ln_o[1:2, :] = jnp.sum(s, axis=0, keepdims=True)
        for k in range(steps):
            pl.when(core == k // 2)(lambda: down_copy(k, mine_s, mine_o).wait())
            pl.when(core != k // 2)(lambda: down_copy(k, sent_s, sent_o).wait())
            for copy in up_copies(k):
                copy.wait()


def finish_kernel(blocks, att, left, x, right, act, out_w, down_w, out_o, left_o, right_o):
    tiles = blocks // 2
    for r in range(tiles):
        rows = slice(r * 256, (r + 1) * 256)
        mid = two_blocks(left, x, right, r).astype(F32) + dot(att[rows, :], out_w[...])
        total = (mid + dot(act[rows, :], down_w[...])).astype(BF16)
        for h in range(2):
            block = 2 * r + h
            part = total[h * BLOCK : (h + 1) * BLOCK]
            if block == 0:
                left_o[...] = part
            elif block == blocks - 1:
                right_o[...] = part
            else:
                out_o[(block - 1) * BLOCK : block * BLOCK, :] = part


def finish_call(att, left, x, right, act, out_w, down_w):
    rows = att.shape[0]
    vmem = pl.BlockSpec(memory_space=pltpu.VMEM)
    edge = shape_of((HALO, D), BF16)
    return pl.pallas_call(
        functools.partial(finish_kernel, rows // BLOCK),
        in_specs=[vmem] * 7,
        out_specs=[vmem] * 3,
        out_shape=[shape_of(x.shape, BF16), edge, edge],
        compiler_params=pltpu.CompilerParams(vmem_limit_bytes=58 * MIB),
        cost_estimate=pl.CostEstimate(flops=4 * 10**9, bytes_accessed=12 * 10**6, transcendentals=0),
        name="finish",
    )(att, left, x, right, act, out_w, down_w)


def middle_kernel(scal, dbr, att, out_w, d_att_o, mine_o, sent_o):
    core = scal[0, CORE]
    for r in range(dbr.shape[0] // 256):
        rows = slice(r * 256, (r + 1) * 256)
        d_att_o[rows, :] = dot_t(dbr[rows, :], out_w[...]).astype(BF16)
    total = t_dot(att[...], dbr[...]).astype(BF16)
    for half in range(2):
        part = total[half * 256 : (half + 1) * 256].reshape(16, 16, 512)

        @pl.when(core == half)
        def _():
            for c in range(4):
                mine_o[:, c] = part[:, :, c * 128 : (c + 1) * 128]

        @pl.when(core != half)
        def _():
            for c in range(4):
                sent_o[:, c] = part[:, :, c * 128 : (c + 1) * 128]


def back_kernel(blocks, scal, d_att, att, lse, seg, qkv, normed, dqkv_o, mine_o, sent_o,
                q_s, kc, vx, dk_s, dv_s, bias_s, dqkv_s, normed_s):
    step = pl.program_id(0)
    core = scal[0, CORE]

    def rows_of(block, count=1):
        return pl.ds(pl.multiple_of(block * BLOCK, BLOCK), count * BLOCK)

    @pl.when(step < blocks // 2)
    def _():
        rows = rows_of(2 * step, 2)
        q_s[rows, :] = qkv[:, 0:512] * jnp.asarray(0.125, BF16)
        normed_s[rows, :] = normed[...]
        for h in range(2):
            part = slice(h * BLOCK, (h + 1) * BLOCK)
            split_pairs(qkv[part, 512:1024], qkv[part, 1024:1536], kc, vx, 2 * step + h)
        both = pl.ds(pl.multiple_of(step * 512, 512), 512)
        for p in range(PAIRS):
            dk_s[p, both, :] = jnp.zeros((512, 128), F32)
            dv_s[p, both, :] = jnp.zeros((512, 128), F32)

    @pl.when((step >= 1) & (step <= blocks // 2))
    def _():
        i = 2 * (step - 1)
        rows = rows_of(i, 2)
        low = scal[0, i]
        n_keys = scal[0, HIGH + i + 1] - low + 1
        keys_at = pl.multiple_of(low * 256, 256)
        seg_q = [jnp.broadcast_to(seg[i + h].astype(F32), (BLOCK, BLOCK)) for h in range(2)]

        def back(n):
            keys = pl.ds(keys_at, n * 256)
            for t in range(n):
                seg_k = column(seg[low + t].astype(F32))
                for h in range(2):
                    cols = slice(h * BLOCK, (h + 1) * BLOCK)
                    bias_s[t * BLOCK : (t + 1) * BLOCK, cols] = jnp.where(seg_k == seg_q[h], 0.0, -1e30)

            def pair(p, carry):
                cols = pl.ds(pl.multiple_of(p * 128, 128), 128)
                q = q_s[rows, cols]
                d_out = d_att[:, cols]
                minus = -(d_out.astype(F32) * att[:, cols].astype(F32))
                scores = dot_t(kc[p, keys, :], jnp.concatenate([q, lse[:, cols]], axis=1))
                d_probs = dot_t(vx[p, keys, :], jnp.concatenate([d_out, minus.astype(BF16)], axis=1))
                parts, d_parts = [], []
                for t in range(n):
                    bias = bias_s[t * BLOCK : (t + 1) * BLOCK, :]
                    for h in range(2):
                        part = slice((2 * t + h) * BLOCK, (2 * t + h + 1) * BLOCK)
                        probs = jnp.exp(scores[part] + bias)
                        parts.append(probs.astype(BF16))
                        d_parts.append((probs * d_probs[part]).astype(BF16))
                d_scores = jnp.concatenate(d_parts, axis=0)
                dk_s[p, keys, :] += dot(d_scores, q)
                dv_s[p, keys, :] += dot(jnp.concatenate(parts, axis=0), d_out)
                d_q = t_dot(d_scores, kc[p, keys, 0:128]) * 0.125
                dqkv_s[rows, pl.ds(pl.multiple_of(p * 384, 128), 128)] = d_q.astype(BF16)
                return carry

            lax.fori_loop(0, PAIRS, pair, 0, unroll=2)

        for n in range(1, 7):
            pl.when(n_keys == n)(functools.partial(back, n))

    @pl.when(step >= 2)
    def _():
        even = lax.broadcasted_iota(jnp.int32, (BLOCK, BLOCK), 1) < 64
        for h in range(2):
            block = 2 * (step - 2) + h
            rows = rows_of(block)
            up = pl.ds(pl.multiple_of(block * 256, 256), 128)
            down = pl.ds(pl.multiple_of(block * 256 + 128, 128), 128)
            for p in range(PAIRS):
                for t, source in enumerate((dk_s, dv_s)):
                    both = jnp.where(even, source[p, up, :], source[p, down, :])
                    spot = p * 384 + 128 + t * 128
                    dqkv_s[rows, spot : spot + 128] = both.astype(BF16)
        dqkv_o[...] = dqkv_s[rows_of(2 * (step - 2), 2), :]

    @pl.when(step == blocks // 2 + 1)
    def _():
        for p in range(PAIRS):
            part = t_dot(normed_s[...], dqkv_s[:, p * 384 : (p + 1) * 384]).astype(BF16)
            for half in range(2):
                piece = part[half * 256 : (half + 1) * 256].reshape(16, 16, 384)

                @pl.when(core == half)
                def _():
                    mine_o[:, p] = piece

                @pl.when(core != half)
                def _():
                    sent_o[:, p] = piece


def entry_kernel(blocks, left, x, right, dbr, gain, ln2, weight, d_qkv,
                 grad_o, left_o, right_o, small_o, w_s, x_s, ln_s, grad_s):
    r = pl.program_id(0)
    tiles = blocks // 2

    @pl.when(r == 0)
    def _():
        for p in range(PAIRS):
            for part in range(3):
                spot = part * 512 + p * 128
                to = p * 384 + part * 128
                w_s[:, to : to + 128] = weight[:, spot : spot + 128]
        for t in range(tiles):
            x_s[t * 256 : (t + 1) * 256, :] = two_blocks(left, x, right, t)
        ln_s[0:2, :] = jnp.zeros((2, D), F32)

    rows = pl.ds(pl.multiple_of(r * 256, 256), 256)
    d_n1 = dot_t(d_qkv[...], w_s[...])
    n1, inverse = normalize(x_s[rows, :].astype(F32))
    e = d_n1 * gain[...]
    mean_e = jnp.mean(e, axis=-1, keepdims=True)
    mean_en = jnp.mean(e * n1, axis=-1, keepdims=True)
    grad_s[rows, :] = dbr[...].astype(F32) + (e - mean_e - n1 * mean_en) * inverse
    ln_s[0:1, :] += jnp.sum(d_n1 * n1, axis=0, keepdims=True)
    ln_s[1:2, :] += jnp.sum(d_n1, axis=0, keepdims=True)

    @pl.when(r == tiles - 1)
    def _():
        inner = (blocks - 2) * BLOCK
        grad_o[...] = grad_s[HALO : HALO + inner, :]
        left_o[...] = grad_s[0:HALO, :].astype(BF16)
        right_o[...] = grad_s[HALO + inner :, :].astype(BF16)
        vectors = [ln_s[0:1, :], ln_s[1:2, :], ln2[0:1, :], ln2[1:2, :]]
        small_o[...] = jnp.concatenate(
            [v[:, c * 128 : (c + 1) * 128] for v in vectors for c in range(4)], axis=0
        )


def join_kernel(share, mine, other, out_m, out_o, result):
    wide = share.shape[-1]
    result[:, :, :, 0:wide] = jnp.broadcast_to(share[...][None, None], (*result.shape[:2], *share.shape))
    value = mine[...].astype(F32) + other[...].astype(F32)
    result[:, :, :, wide : wide + 384] = value.astype(BF16)
    value = out_m[...].astype(F32) + out_o[...].astype(F32)
    result[:, :, :, wide + 384 : wide + 512] = value.astype(BF16)


def join_call(share, mine, other, out_m, out_o):
    at = lambda s: (s, 0, 0, 0)
    block = (8, 4, 16, share.shape[-1] + 512)
    return pl.pallas_call(
        join_kernel,
        grid=(2,),
        in_specs=[pl.BlockSpec(share.shape, lambda s: (0, 0))]
        + [pl.BlockSpec((8, 4, 16, 384), at)] * 2 + [pl.BlockSpec((8, 4, 16, 128), at)] * 2,
        out_specs=pl.BlockSpec(block, at),
        out_shape=shape_of((16, *block[1:]), BF16),
        compiler_params=params(24),
        name="join",
    )(share, mine, other, out_m, out_o)


def whole(shape):
    return pl.BlockSpec(shape, lambda s, scal: (0,) * len(shape))


def shape_of(shape, dtype):
    return jax.ShapeDtypeStruct(shape, dtype)


def params(mib=58):
    return pltpu.CompilerParams(dimension_semantics=("arbitrary",), vmem_limit_bytes=mib * MIB)


def attend_call(scal, left, x, right, seg, gain, shift, weight):
    rows = x.shape[0] + 2 * HALO
    blocks = rows // BLOCK
    at = lambda s, scal: (jnp.maximum(s - 1, 0), 0)
    return pl.pallas_call(
        functools.partial(attend_kernel, blocks),
        grid_spec=pltpu.PrefetchScalarGridSpec(
            num_scalar_prefetch=1,
            grid=(blocks // 2 + 1,),
            in_specs=[
                whole((HALO, D)), whole(x.shape), whole((HALO, D)), whole(seg.shape),
                whole((1, D)), whole((1, D)), whole(weight.shape),
            ],
            out_specs=[
                pl.BlockSpec(memory_space=pl.ANY),
                pl.BlockSpec(memory_space=pl.ANY),
                pl.BlockSpec((2 * BLOCK, D), at),
                pl.BlockSpec((2 * BLOCK, D), at),
            ],
            scratch_shapes=[
                pltpu.VMEM((rows, D), BF16),
                pltpu.VMEM((rows, 3 * D), BF16),
                pltpu.VMEM((PAIRS, blocks * 256, 128), BF16),
                pltpu.VMEM((PAIRS, blocks * 256, 256), BF16),
                pltpu.SemaphoreType.DMA((blocks,)),
            ],
        ),
        out_shape=[
            shape_of((rows, D), BF16),
            shape_of((rows, 3 * D), BF16),
            shape_of((rows, D), BF16),
            shape_of((rows, D), BF16),
        ],
        compiler_params=params(),
        cost_estimate=pl.CostEstimate(flops=8 * 10**9, bytes_accessed=25 * 10**6, transcendentals=4 * 10**6),
        name="attend",
    )(scal, left, x, right, seg, gain, shift, weight)


def feed_call(scal, att, left, x, right, cot_l, cot, cot_r, out_w, up_w, down_w, gain, shift):
    rows = att.shape[0]
    blocks = rows // BLOCK
    half = (16, 4, 16, 1024)
    anywhere = pl.BlockSpec(memory_space=pl.ANY)
    return pl.pallas_call(
        functools.partial(feed_kernel, blocks),
        grid_spec=pltpu.PrefetchScalarGridSpec(
            num_scalar_prefetch=1,
            grid=(FF // 512,),
            in_specs=[
                whole((rows, D)),
                whole((HALO, D)), whole(x.shape), whole((HALO, D)),
                whole((HALO, D)), whole(x.shape), whole((HALO, D)),
                whole((D, D)),
                pl.BlockSpec((D, 512), lambda s, scal: (0, s)),
                pl.BlockSpec((512, D), lambda s, scal: (s, 0)),
                whole((1, D)), whole((1, D)),
            ],
            out_specs=[
                whole((rows, D)), pl.BlockSpec((rows, 512), lambda s, scal: (0, s)), whole((2, D)),
                anywhere, anywhere,
            ],
            scratch_shapes=[
                pltpu.VMEM((rows, D), F32),
                pltpu.VMEM((rows, 128), F32),
                pltpu.VMEM((rows, D), BF16),
                pltpu.VMEM(half, BF16),
                pltpu.VMEM(half, BF16),
                pltpu.SemaphoreType.DMA((3 * (FF // 512),)),
                pltpu.VMEM((rows, D), BF16),
                pltpu.VMEM((FF // 512, rows, 512), BF16),
                pltpu.VMEM((FF // 512, D, 512), BF16),
            ] + [pltpu.VMEM((256, 512), F32)] * 4,
        ),
        out_shape=[
            shape_of((rows, D), BF16),
            shape_of((rows, FF), BF16),
            shape_of((2, D), F32),
            shape_of(half, BF16),
            shape_of(half, BF16),
        ],
        compiler_params=params(),
        cost_estimate=pl.CostEstimate(flops=16 * 10**9, bytes_accessed=25 * 10**6, transcendentals=3 * 10**6),
        name="feed",
    )(scal, att, left, x, right, cot_l, cot, cot_r, out_w, up_w, down_w, gain, shift)


def middle_call(scal, dbr, att, out_w):
    part = (16, 4, 16, 128)
    vmem = pl.BlockSpec(memory_space=pltpu.VMEM)
    return pl.pallas_call(
        middle_kernel,
        in_specs=[pl.BlockSpec(memory_space=pltpu.SMEM)] + [vmem] * 3,
        out_specs=[vmem] * 3,
        out_shape=[shape_of(dbr.shape, BF16), shape_of(part, BF16), shape_of(part, BF16)],
        compiler_params=pltpu.CompilerParams(vmem_limit_bytes=58 * MIB),
        cost_estimate=pl.CostEstimate(flops=2 * 10**9, bytes_accessed=5 * 10**6, transcendentals=0),
        name="middle",
    )(scal, dbr, att, out_w)


def back_call(scal, d_att, att, lse, seg, qkv, normed):
    rows = qkv.shape[0]
    blocks = rows // BLOCK
    half = (16, PAIRS, 16, 384)
    last = blocks // 2 - 1
    lead = lambda s, scal: (jnp.minimum(s, last), 0)
    now = lambda s, scal: (jnp.clip(s - 1, 0, last), 0)
    done = lambda s, scal: (jnp.maximum(s - 2, 0), 0)
    return pl.pallas_call(
        functools.partial(back_kernel, blocks),
        grid_spec=pltpu.PrefetchScalarGridSpec(
            num_scalar_prefetch=1,
            grid=(blocks // 2 + 2,),
            in_specs=[
                pl.BlockSpec((2 * BLOCK, D), now), pl.BlockSpec((2 * BLOCK, D), now), pl.BlockSpec((2 * BLOCK, D), now),
                whole(seg.shape),
                pl.BlockSpec((2 * BLOCK, 3 * D), lead), pl.BlockSpec((2 * BLOCK, D), lead),
            ],
            out_specs=[pl.BlockSpec((2 * BLOCK, 3 * D), done), whole(half), whole(half)],
            scratch_shapes=[
                pltpu.VMEM((rows, D), BF16),
                pltpu.VMEM((PAIRS, blocks * 256, 256), BF16),
                pltpu.VMEM((PAIRS, blocks * 256, 256), BF16),
                pltpu.VMEM((PAIRS, blocks * 256, 128), F32),
                pltpu.VMEM((PAIRS, blocks * 256, 128), F32),
                pltpu.VMEM((6 * BLOCK, 2 * BLOCK), F32),
                pltpu.VMEM((rows, 3 * D), BF16),
                pltpu.VMEM((rows, D), BF16),
            ],
        ),
        out_shape=[shape_of((rows, 3 * D), BF16), shape_of(half, BF16), shape_of(half, BF16)],
        compiler_params=params(),
        cost_estimate=pl.CostEstimate(flops=12 * 10**9, bytes_accessed=20 * 10**6, transcendentals=4 * 10**6),
        name="back",
    )(scal, d_att, att, lse, seg, qkv, normed)


def entry_call(left, x, right, dbr, gain, ln2, weight, d_qkv):
    rows = dbr.shape[0]
    fixed = lambda v: pl.BlockSpec(v.shape, lambda s: (0,) * len(v.shape))
    at = lambda s: (s, 0)
    edge = shape_of((HALO, D), BF16)
    outs = [shape_of(x.shape, F32), edge, edge, shape_of((16, 128), F32)]
    return pl.pallas_call(
        functools.partial(entry_kernel, rows // BLOCK),
        grid=(rows // 256,),
        in_specs=[
            fixed(left), fixed(x), fixed(right), pl.BlockSpec((256, D), at), fixed(gain), fixed(ln2),
            fixed(weight), pl.BlockSpec((256, 3 * D), at),
        ],
        out_specs=[fixed(v) for v in outs],
        out_shape=outs,
        scratch_shapes=[
            pltpu.VMEM((D, 3 * D), BF16), pltpu.VMEM((rows, D), BF16), pltpu.VMEM((8, D), F32),
            pltpu.VMEM((rows, D), F32),
        ],
        compiler_params=params(),
        cost_estimate=pl.CostEstimate(flops=2 * 10**9, bytes_accessed=15 * 10**6, transcendentals=0),
        name="entry",
    )(left, x, right, dbr, gain, ln2, weight, d_qkv)


def other_core(value):
    return lax.ppermute(value, "core", [(0, 1), (1, 0)])


def all_shares(value, groups):
    parts = lax.all_to_all(value, ("rows", "x"), 0, 0, tiled=True)
    return jnp.sum(parts.astype(F32), axis=0).astype(BF16)


def gather_shares(share, groups):
    copies = jnp.broadcast_to(share[None], (groups, *share.shape))
    return lax.all_to_all(copies, ("rows", "x"), 0, 0, tiled=True)


def per_device(
    inputs, qkv_weight, out_weight, up_weight, down_weight, norm1_gain, norm1_shift,
    norm2_gain, norm2_shift, segment_ids, item_steps, gen_rank, out_grad,
):
    x = inputs[0]
    positions = x.shape[0]
    blocks = (positions + 2 * HALO) // BLOCK
    chips = lax.axis_size("rows") * lax.axis_size("x")
    seq_parts = lax.axis_size("x") * lax.axis_size("core")
    seq = ("x", "core")
    to_right = [(i, (i + 1) % seq_parts) for i in range(seq_parts)]
    to_left = [((i + 1) % seq_parts, i) for i in range(seq_parts)]

    place = jnp.stack([lax.axis_index(seq), lax.axis_index("core")]).astype(jnp.int32)
    tie = lax.optimization_barrier
    left = lax.ppermute(x[positions - HALO :], seq, to_right)
    right = lax.ppermute(x[:HALO], seq, to_left)
    scal, seg_rows, cot, send_l, send_r = prepare_call(
        place, segment_ids, item_steps, gen_rank, out_grad[0]
    )
    cot_l = lax.ppermute(send_r, seq, to_right)
    cot_r = lax.ppermute(send_l, seq, to_left)

    gain1, shift1 = norm1_gain.reshape(1, D), norm1_shift.reshape(1, D)
    gain2, shift2 = norm2_gain.reshape(1, D), norm2_shift.reshape(1, D)
    normed1, qkv, att, lse = attend_call(
        scal, left, x, right, seg_rows, gain1, shift1, qkv_weight
    )
    d_branch, act, ln2, mine_a, sent_a = feed_call(
        scal, att, left, x, right, cot_l, cot, cot_r, out_weight, up_weight, down_weight, gain2, shift2
    )
    got_a = other_core(sent_a)
    half_a = (mine_a.astype(F32) + got_a.astype(F32)).astype(BF16)
    d_att, mine_o, sent_o = middle_call(scal, d_branch, att, out_weight)
    d_att, half_a = tie((d_att, half_a))
    share_a = all_shares(half_a.reshape(chips, -1, 1024), chips)
    d_qkv, mine_b, sent_b = back_call(scal, d_att, att, lse, seg_rows, qkv, normed1)
    joined = join_call(share_a, mine_b, other_core(sent_b), mine_o, other_core(sent_o))
    joined, d_branch, att = tie((joined, d_branch, att))
    got = lax.all_to_all(joined.reshape(chips, -1, 1536), ("rows", "x"), 0, 0, tiled=True)
    grad, grad_l, grad_r, small = entry_call(
        left, x, right, d_branch, gain1, ln2, qkv_weight, d_qkv
    )
    small = small + other_core(small)
    out, out_l, out_r = finish_call(att, left, x, right, act, out_weight, down_weight)
    edge_l = jnp.concatenate([out_l, grad_l], axis=0)
    edge_r = jnp.concatenate([out_r, grad_r], axis=0)
    from_r = lax.ppermute(edge_l, seq, to_left)
    from_l = lax.ppermute(edge_r, seq, to_right)
    got, from_l, from_r, small = tie((got, from_l, from_r, small))
    far_a = other_core(got)
    share_b = jnp.sum(got[:, :, 1024:].astype(F32), axis=0).astype(BF16)
    near_b = gather_shares(jnp.concatenate([share_b, small.astype(BF16)], axis=1), chips)
    grads_a = unpack_call(scal, got.reshape(16, 4, 16, 1536))
    grad_down, grad_up = unpack_call(scal, far_a.reshape(16, 4, 16, 1536), grads_a)
    output, input_grad = patch_call(scal, out, grad, seg_rows, from_l, from_r)
    near_b, grad_down, input_grad = tie((near_b, grad_down, input_grad))
    far_b = other_core(near_b)
    grad_out, grad_qkv, *vectors = rest_call(
        scal, near_b.reshape(16, 4, 16, 640), far_b.reshape(16, 4, 16, 640)
    )
    vectors = [v.reshape(D) for v in vectors]
    return (
        output[None], input_grad[None], grad_qkv, grad_out, grad_up, grad_down,
        vectors[0], vectors[1], vectors[2], vectors[3],
    )


def solution(mesh):
    rows = mesh.devices.shape[0]
    parts = mesh.devices.shape[1]
    split = Mesh(mesh.devices.reshape(rows, parts // 2, 2), ("rows", "x", "core"))
    seq = ("x", "core")
    return jax.shard_map(
        per_device,
        mesh=split,
        in_specs=(
            P("rows", seq, None), P(), P(), P(), P(), P(), P(), P(), P(),
            P("rows", None), P("rows", None), P("rows", seq), P("rows", seq, None),
        ),
        out_specs=(
            P("rows", seq, None), P("rows", seq, None),
            P(), P(), P(), P(), P(), P(), P(), P(),
        ),
        check_vma=False,
    )
```

```python
import functools

import jax
import jax.numpy as jnp
from jax import lax
from jax.experimental import pallas as pl
from jax.experimental.pallas import tpu as pltpu
from jax.sharding import Mesh
from jax.sharding import PartitionSpec as P

D = 512
HEADS = 8
PAIRS = HEADS // 2
FF = 2048
EPS = 1e-05
HALO = 128
BLOCK = 128
BF16 = jnp.bfloat16
F32 = jnp.float32
MIB = 1024 * 1024
HIGH, CORE, DROP_L, DROP_R = 16, 32, 33, 34


def dot(a, b):
    return lax.dot_general(a, b, (((1,), (0,)), ((), ())), preferred_element_type=F32)


def dot_t(a, b):
    return lax.dot_general(a, b, (((1,), (1,)), ((), ())), preferred_element_type=F32)


def t_dot(a, b):
    return lax.dot_general(a, b, (((0,), (0,)), ((), ())), preferred_element_type=F32)


def normalize(value):
    center = jnp.mean(value, axis=-1, keepdims=True)
    centred = value - center
    spread = jnp.mean(centred * centred, axis=-1, keepdims=True)
    inverse = lax.rsqrt(spread + EPS)
    return centred * inverse, inverse


def two_blocks(left, middle, right, tile):
    last = 1 + middle.shape[0] // BLOCK
    parts = []
    for block in (2 * tile, 2 * tile + 1):
        if block == 0:
            parts.append(left[...])
        elif block == last:
            parts.append(right[...])
        else:
            parts.append(middle[(block - 1) * BLOCK : block * BLOCK, :])
    return jnp.concatenate(parts, axis=0)


def split_pairs(keys, values, kc, vx, block):
    lane = lax.broadcasted_iota(jnp.int32, (BLOCK, BLOCK), 1)
    even = lane < 64
    zero = jnp.zeros((BLOCK, BLOCK), BF16)
    ones_even = even.astype(F32).astype(BF16)
    ones_odd = (~even).astype(F32).astype(BF16)
    base = block * 256
    for p in range(PAIRS):
        k = keys[:, p * 128 : (p + 1) * 128]
        v = values[:, p * 128 : (p + 1) * 128]
        kc[p, pl.ds(base, 128), 0:128] = jnp.where(even, k, zero)
        kc[p, pl.ds(base + 128, 128), 0:128] = jnp.where(even, zero, k)
        vx[p, pl.ds(base, 128), 0:128] = jnp.where(even, v, zero)
        vx[p, pl.ds(base + 128, 128), 0:128] = jnp.where(even, zero, v)
        vx[p, pl.ds(base, 128), 128:256] = ones_even
        vx[p, pl.ds(base + 128, 128), 128:256] = ones_odd
        if kc.shape[2] == 256:
            minus = jnp.where(lax.rem(lane, 64) < 3, -1.0, 0.0)
            kc[p, pl.ds(base, 128), 128:256] = jnp.where(even, minus, 0.0).astype(BF16)
            kc[p, pl.ds(base + 128, 128), 128:256] = jnp.where(even, 0.0, minus).astype(BF16)


def mask_rows(seg, row, low, n):
    seg_q = column(seg[row].astype(F32))
    return [
        jnp.where(seg_q == jnp.broadcast_to(seg[low + t].astype(F32), (BLOCK, BLOCK)), 0.0, -1e30)
        for t in range(n)
    ]


def column(row):
    return jnp.transpose(jnp.broadcast_to(row, (BLOCK, BLOCK)))


def keep_rows(values, mask):
    return jnp.concatenate(
        [
            jnp.where(mask, values[:, c * 128 : (c + 1) * 128].astype(F32), 0.0).astype(BF16)
            for c in range(D // 128)
        ],
        axis=1,
    )


def prepare_kernel(inner, place, segments, steps, rank, out_grad, scal_o, seg_o, cot_o, left_o, right_o, part_s):
    seq = place[0]
    row_blocks = segments.shape[1] // BLOCK
    blocks = inner + 2
    rows = []
    for b in range(blocks):
        at = seq * inner + b - 1
        if b == 0:
            at = jnp.maximum(at, 0)
        if b == blocks - 1:
            at = jnp.minimum(at, row_blocks - 1)
        row = segments[0:1, pl.ds(pl.multiple_of(at * BLOCK, BLOCK), BLOCK)]
        if b == 0:
            row = jnp.where(seq > 0, row, -1)
        if b == blocks - 1:
            row = jnp.where(seq * inner + inner < row_blocks, row, 1000)
        rows.append(row)
        seg_o[b] = row
    window = jnp.concatenate(rows, axis=0)
    local = window[1 : inner + 1]
    first, last = window[:, 0:1], window[:, BLOCK - 1 : BLOCK]
    below = jnp.zeros(window.shape, F32)
    upto = jnp.zeros(window.shape, F32)
    for row in rows:
        below += (row < first).astype(F32)
        upto += (row <= last).astype(F32)
    part_s[...] = jnp.zeros(part_s.shape, F32)
    part_s[0:blocks, :] = below
    part_s[HIGH : HIGH + blocks, :] = upto
    counts = dot_t(jnp.ones((8, BLOCK), BF16), part_s[...].astype(BF16))[0:1]

    def border(before, after):
        value = before[-1:, BLOCK - 1 : BLOCK]
        across = value == after[0:1, 0:1]
        sizes = [jnp.sum((part == value).astype(F32), axis=(0, 1), keepdims=True) for part in (before, after)]
        return value, across, sizes[0] >= sizes[1]

    value_l, across_l, to_left_l = border(rows[0], local)
    value_r, across_r, to_left_r = border(local, rows[-1])
    drop_l = jnp.where(across_l & to_left_l, value_l, -2)
    drop_r = jnp.where(across_r & jnp.logical_not(to_left_r), value_r, -2)
    lane = lax.broadcasted_iota(jnp.int32, (1, BLOCK), 1)
    at_block = jnp.floor(jnp.where(lane >= HIGH, counts - 1.0, counts) * (1.0 / BLOCK)).astype(jnp.int32)
    at_block = jnp.where(lane == CORE, place[1], at_block)
    at_block = jnp.where(lane == DROP_L, drop_l, at_block)
    scal_o[...] = jnp.where(lane == DROP_R, drop_r, at_block)

    token = jnp.zeros(local.shape, jnp.int32)
    for slot in range(steps.shape[1]):
        token = jnp.where(local == slot, steps[0, slot], token)
    for b in range(inner):
        part = slice(b * BLOCK, (b + 1) * BLOCK)
        keep = rank[0:1, part] >= token[b : b + 1]
        seg = rows[b + 1]
        own = (seg != drop_l) & (seg != drop_r)
        values = out_grad[part, :]
        cot_o[part, :] = keep_rows(values, column((keep & own).astype(F32)) > 0.5)
        if b == 0:
            left_o[...] = keep_rows(values, column((keep & (seg == drop_l)).astype(F32)) > 0.5)
        if b == inner - 1:
            right_o[...] = keep_rows(values, column((keep & (seg == drop_r)).astype(F32)) > 0.5)


def prepare_call(place, segments, steps, rank, out_grad):
    inner = out_grad.shape[0] // BLOCK
    vmem = pl.BlockSpec(memory_space=pltpu.VMEM)
    smem = pl.BlockSpec(memory_space=pltpu.SMEM)
    return pl.pallas_call(
        functools.partial(prepare_kernel, inner),
        in_specs=[smem, vmem, smem, vmem, vmem],
        out_specs=[vmem] * 5,
        out_shape=[
            shape_of((1, BLOCK), jnp.int32),
            shape_of((inner + 2, 1, BLOCK), jnp.int32),
            shape_of(out_grad.shape, BF16),
            shape_of((HALO, D), BF16),
            shape_of((HALO, D), BF16),
        ],
        scratch_shapes=[pltpu.VMEM((BLOCK, BLOCK), F32)],
        compiler_params=pltpu.CompilerParams(vmem_limit_bytes=58 * MIB),
        cost_estimate=pl.CostEstimate(flops=10**6, bytes_accessed=4 * 10**6, transcendentals=0),
        name="prepare",
    )(place, segments, steps, rank, out_grad)


def patch_kernel(blocks, scal, out, grad, seg, left, right, out_o, grad_o):
    step = pl.program_id(0)
    drop_l, drop_r = scal[0, DROP_L], scal[0, DROP_R]
    row = seg[0]
    drop = jnp.where(step == 0, drop_l, drop_r)
    lost = column((row == drop).astype(F32)) > 0.5
    for c in range(D // 128):
        cols = slice(c * 128, (c + 1) * 128)
        for mine, start, result in ((out, 0, out_o), (grad, HALO, grad_o)):
            part = slice(start, start + HALO)
            other = jnp.where(step == 0, left[part, cols].astype(F32), right[part, cols].astype(F32))
            value = jnp.where(lost, other, mine[:, cols].astype(F32))
            result[:, cols] = value.astype(result.dtype)


def patch_call(scal, out, grad, seg, left, right):
    inner = out.shape[0] // BLOCK
    block = lambda s, scal: (s * (inner - 1), 0)
    return pl.pallas_call(
        functools.partial(patch_kernel, inner + 2),
        grid_spec=pltpu.PrefetchScalarGridSpec(
            num_scalar_prefetch=1,
            grid=(2,),
            in_specs=[
                pl.BlockSpec((BLOCK, D), block),
                pl.BlockSpec((BLOCK, D), block),
                pl.BlockSpec((1, 1, BLOCK), lambda s, scal: (1 + s * (inner - 1), 0, 0)),
                whole((2 * HALO, D)), whole((2 * HALO, D)),
            ],
            out_specs=[pl.BlockSpec((BLOCK, D), block), pl.BlockSpec((BLOCK, D), block)],
        ),
        out_shape=[shape_of(out.shape, out.dtype), shape_of(grad.shape, grad.dtype)],
        input_output_aliases={1: 0, 2: 1},
        compiler_params=params(),
        name="patch",
    )(scal, out, grad, seg, left, right)


def unpack_feed(a, down_o, up_o):
    rows = a.shape[0] * 16
    down_o[...] = a[:, :, :, 0:512].astype(F32).reshape(4 * rows, 512)
    for c in range(4):
        up_o[:, c * 512 : (c + 1) * 512] = a[:, c, :, 512:1024].astype(F32).reshape(rows, 512)


def rest_kernel(first, scal, a, *refs):
    (out_o, qkv_o), vectors_o = refs[first : first + 2], refs[first + 2 :]
    for c in range(4):
        value = a[:, c, :, 0:512].astype(F32).reshape(128, 512)
        for part in range(3):
            spot = part * 512 + c * 128
            qkv_o[:, spot : spot + 128] = value[:, part * 128 : (part + 1) * 128]
        out_o[:, c * 128 : (c + 1) * 128] = value[:, 384:512]
    if vectors_o:
        step = pl.program_id(0)
        part = jnp.sum(a[:, :, :, 512:640].astype(F32), axis=(0, 1))
        for v in range(4):
            row = jnp.concatenate([part[4 * v + c : 4 * v + c + 1] for c in range(4)], axis=1)
            vectors_o[v][...] = jnp.where(step == 0, row, row + vectors_o[v][...])


def rest_call(scal, value, before=()):
    def part(s, scal):
        half = scal[0, CORE] if not before else 1 - scal[0, CORE]
        return (half * 2 + s, 0)

    vectors = [] if before else [(1, D)] * 4
    return pl.pallas_call(
        functools.partial(rest_kernel, len(before)),
        grid_spec=pltpu.PrefetchScalarGridSpec(
            num_scalar_prefetch=1,
            grid=(2,),
            in_specs=[pl.BlockSpec((8, *value.shape[1:]), lambda s, scal: (s, 0, 0, 0))]
            + [pl.BlockSpec(memory_space=pl.ANY)] * len(before),
            out_specs=[pl.BlockSpec((128, D), part), pl.BlockSpec((128, 3 * D), part)]
            + [whole(v) for v in vectors],
        ),
        out_shape=[shape_of(v, F32) for v in ((D, D), (D, 3 * D), *vectors)],
        input_output_aliases={2 + k: k for k in range(len(before))},
        compiler_params=params(24),
        cost_estimate=pl.CostEstimate(flops=10**6, bytes_accessed=4 * 10**6, transcendentals=0),
        name="rest",
    )(scal, value, *before)


def unpack_call(scal, value, before=()):
    steps = 4

    def out(s, scal):
        half = scal[0, CORE] if not before else 1 - scal[0, CORE]
        return (half * steps + s, 0)

    def kernel(scal, a, *refs):
        unpack_feed(a, *refs[len(before) :])

    shapes = ((FF, D), (D, FF))
    return pl.pallas_call(
        kernel,
        grid_spec=pltpu.PrefetchScalarGridSpec(
            num_scalar_prefetch=1,
            grid=(steps,),
            in_specs=[pl.BlockSpec((16 // steps, *value.shape[1:]), lambda s, scal: (s, 0, 0, 0))]
            + [pl.BlockSpec(memory_space=pl.ANY)] * len(before),
            out_specs=[pl.BlockSpec((rows // (2 * steps), cols), out) for rows, cols in shapes],
        ),
        out_shape=[shape_of(shape, F32) for shape in shapes],
        input_output_aliases={2 + k: k for k in range(len(before))},
        compiler_params=params(24),
        cost_estimate=pl.CostEstimate(flops=10**6, bytes_accessed=10 * 10**6, transcendentals=0),
        name="unpack",
    )(scal, value, *before)


def attend_kernel(blocks, scal, left, x, right, seg, gain, shift, weight,
                  normed_o, qkv_o, att_o, lse_o, normed_s, qkv_s, kc, vx, sems):
    step = pl.program_id(0)
    tiles = blocks // 2

    def copies(r):
        rows = slice(r * 256, (r + 1) * 256)
        return (
            pltpu.make_async_copy(normed_s.at[rows, :], normed_o.at[rows, :], sems.at[2 * r]),
            pltpu.make_async_copy(qkv_s.at[rows, :], qkv_o.at[rows, :], sems.at[2 * r + 1]),
        )

    @pl.when(step == 0)
    def _():
        for r in range(tiles + 1):
            if r < tiles:
                base, _ = normalize(two_blocks(left, x, right, r).astype(F32))
                normed_s[r * 256 : (r + 1) * 256, :] = (base * gain[...] + shift[...]).astype(BF16)
            if r > 0:
                rows = slice((r - 1) * 256, r * 256)
                qkv = dot(normed_s[rows, :], weight[...]).astype(BF16)
                qkv_s[rows, :] = qkv
                for half in range(2):
                    part = qkv[half * 128 : (half + 1) * 128]
                    split_pairs(part[:, 512:1024], part[:, 1024:1536], kc, vx, 2 * (r - 1) + half)
                for copy in copies(r - 1):
                    copy.start()

    @pl.when(step > 0)
    def _():
        lane = lax.broadcasted_iota(jnp.int32, (BLOCK, BLOCK), 1)
        place = lax.rem(lane, 64)
        for h in range(2):
            i = 2 * (step - 1) + h
            rows = pl.ds(pl.multiple_of(i * BLOCK, BLOCK), BLOCK)
            part = slice(h * BLOCK, (h + 1) * BLOCK)
            low = scal[0, i]
            n_keys = scal[0, HIGH + i] - low + 1
            first = pl.multiple_of(low * 256, 256)

            def attend(n):
                bias = mask_rows(seg, i, low, n)
                def pair(p, carry):
                    cols = pl.ds(pl.multiple_of(p * 128, 128), 128)
                    q = qkv_s[rows, cols] * jnp.asarray(0.125, BF16)
                    scores = dot_t(q, kc[p, pl.ds(first, n * 256), :])
                    tiles_s = [
                        [scores[:, t * 256 + o * 128 : t * 256 + o * 128 + 128] + bias[t] for t in range(n)]
                        for o in range(2)
                    ]
                    highest = [
                        jnp.max(functools.reduce(jnp.maximum, tiles_s[o]), axis=-1, keepdims=True)
                        for o in range(2)
                    ]
                    pieces = []
                    for t in range(n):
                        for o in range(2):
                            pieces.append(jnp.exp(tiles_s[o][t] - highest[o]).astype(BF16))
                    mixed = dot(jnp.concatenate(pieces, axis=1), vx[p, pl.ds(first, n * 256), :])
                    total = mixed[:, 128:256]
                    att_o[part, cols] = (mixed[:, 0:128] * (1.0 / total)).astype(BF16)
                    lse = jnp.where(lane < 64, highest[0], highest[1]) + jnp.log(total)
                    top = lse.astype(BF16).astype(F32)
                    rest = lse - top
                    second = rest.astype(BF16).astype(F32)
                    third = jnp.where(place == 2, rest - second, 0.0)
                    lse_o[part, cols] = jnp.where(
                        place == 0, top, jnp.where(place == 1, second, third)
                    ).astype(BF16)
                    return carry

                lax.fori_loop(0, PAIRS, pair, 0, unroll=PAIRS)

            for n in range(1, 6):
                pl.when(n_keys == n)(functools.partial(attend, n))

    @pl.when(step == tiles)
    def _():
        for r in range(tiles):
            for copy in copies(r):
                copy.wait()


def gelu_both(v):
    c = 0.7978845608028654
    square = v * v
    inner = c + (0.044715 * c) * square
    gate = 0.5 + 0.5 * jnp.tanh(v * inner)
    act = v * gate
    slope = gate + act * ((1.0 - gate) * (6.0 * inner - 4.0 * c))
    return act, slope


def feed_kernel(blocks, scal, att, left, x, right, cot_l, cot, cot_r, out_w, up_w, down_w, gain, shift,
                dbr_o, act_o, ln_o, mine_o, sent_o,
                base_s, rstd_s, cot_s, mine_s, sent_s, sems, n2_s, dpre_s, up_s, *stage_s):
    f = pl.program_id(0)
    steps = FF // 512
    tiles = blocks // 2
    core = scal[0, CORE]

    def down_copy(k, from_s, to_o):
        spot = (slice((k % 2) * 8, (k % 2) * 8 + 8), slice(None), slice(None), slice(0, 512))
        return pltpu.make_async_copy(from_s.at[spot], to_o.at[spot], sems.at[k])

    def up_copies(k):
        spot = (slice(None), slice(k, k + 1), slice(None), slice(512, 1024))
        return [
            pltpu.make_async_copy(mine_s.at[spot], mine_o.at[spot], sems.at[steps + k]),
            pltpu.make_async_copy(sent_s.at[spot], sent_o.at[spot], sems.at[2 * steps + k]),
        ]

    @pl.when(f == 0)
    def _():
        for r in range(tiles):
            rows = slice(r * 256, (r + 1) * 256)
            cot_s[rows, :] = two_blocks(cot_l, cot, cot_r, r)
            mid = two_blocks(left, x, right, r).astype(F32) + dot(att[rows, :], out_w[...])
            base, inverse = normalize(mid)
            base_s[rows, :] = base
            rstd_s[rows, :] = jnp.broadcast_to(inverse, (256, 128))
            n2_s[rows, :] = (base * gain[...] + shift[...]).astype(BF16)

    up_s[f] = up_w[...]
    for r in range(tiles + 1):
        if r < tiles:
            rows = slice(r * 256, (r + 1) * 256)
            stage_s[r % 2][...] = dot(n2_s[rows, :], up_w[...])
            stage_s[2 + r % 2][...] = dot_t(cot_s[rows, :], down_w[...])
        if r > 0:
            rows = slice((r - 1) * 256, r * 256)
            act, slope = gelu_both(stage_s[(r - 1) % 2][...])
            act_o[rows, :] = act.astype(BF16)
            dpre_s[f, rows, :] = (slope * stage_s[2 + (r - 1) % 2][...]).astype(BF16)
    grad_down = t_dot(act_o[...], cot_s[...]).astype(BF16).reshape(8, 4, 16, 512)
    grad_up = t_dot(n2_s[...], dpre_s[f]).astype(BF16).reshape(2, 16, 1, 16, 512)

    for k in range(steps):

        @pl.when((f == k) & (core == k // 2))
        def _():
            mine_s[(k % 2) * 8 : (k % 2) * 8 + 8, :, :, 0:512] = grad_down
            down_copy(k, mine_s, mine_o).start()

        @pl.when((f == k) & (core != k // 2))
        def _():
            sent_s[(k % 2) * 8 : (k % 2) * 8 + 8, :, :, 0:512] = grad_down
            down_copy(k, sent_s, sent_o).start()

    for half in range(2):

        @pl.when(core == half)
        def _():
            mine_s[:, pl.ds(f, 1), :, 512:1024] = grad_up[half]
            sent_s[:, pl.ds(f, 1), :, 512:1024] = grad_up[1 - half]

    for k in range(steps):

        @pl.when(f == k)
        def _():
            for copy in up_copies(k):
                copy.start()

    @pl.when(f == steps - 1)
    def _():
        def turn(r, carry):
            rows = pl.ds(pl.multiple_of(r * 256, 256), 256)
            d_pre = jnp.concatenate([dpre_s[k, rows, :] for k in range(steps)], axis=1)
            up = jnp.concatenate([up_s[k] for k in range(steps)], axis=1)
            d_n2 = dot_t(d_pre, up)
            n2 = base_s[rows, :]
            inverse = jnp.concatenate([rstd_s[rows, :]] * 4, axis=1)
            e = d_n2 * gain[...]
            mean_e = jnp.mean(e, axis=-1, keepdims=True)
            mean_en = jnp.mean(e * n2, axis=-1, keepdims=True)
            d_mid = cot_s[rows, :].astype(F32) + (e - mean_e - n2 * mean_en) * inverse
            dbr_o[rows, :] = d_mid.astype(BF16)
            g, s = carry
            return (
                g + jnp.sum((d_n2 * n2).reshape(32, 8, D), axis=0),
                s + jnp.sum(d_n2.reshape(32, 8, D), axis=0),
            )

        zero = jnp.zeros((8, D), F32)
        g, s = lax.fori_loop(0, tiles, turn, (zero, zero), unroll=tiles)
        ln_o[0:1, :] = jnp.sum(g, axis=0, keepdims=True)
        ln_o[1:2, :] = jnp.sum(s, axis=0, keepdims=True)
        for k in range(steps):
            pl.when(core == k // 2)(lambda: down_copy(k, mine_s, mine_o).wait())
            pl.when(core != k // 2)(lambda: down_copy(k, sent_s, sent_o).wait())
            for copy in up_copies(k):
                copy.wait()


def finish_kernel(blocks, att, left, x, right, act, out_w, down_w, out_o, left_o, right_o):
    tiles = blocks // 2
    for r in range(tiles):
        rows = slice(r * 256, (r + 1) * 256)
        mid = two_blocks(left, x, right, r).astype(F32) + dot(att[rows, :], out_w[...])
        total = (mid + dot(act[rows, :], down_w[...])).astype(BF16)
        for h in range(2):
            block = 2 * r + h
            part = total[h * BLOCK : (h + 1) * BLOCK]
            if block == 0:
                left_o[...] = part
            elif block == blocks - 1:
                right_o[...] = part
            else:
                out_o[(block - 1) * BLOCK : block * BLOCK, :] = part


def finish_call(att, left, x, right, act, out_w, down_w):
    rows = att.shape[0]
    vmem = pl.BlockSpec(memory_space=pltpu.VMEM)
    edge = shape_of((HALO, D), BF16)
    return pl.pallas_call(
        functools.partial(finish_kernel, rows // BLOCK),
        in_specs=[vmem] * 7,
        out_specs=[vmem] * 3,
        out_shape=[shape_of(x.shape, BF16), edge, edge],
        compiler_params=pltpu.CompilerParams(vmem_limit_bytes=58 * MIB),
        cost_estimate=pl.CostEstimate(flops=4 * 10**9, bytes_accessed=12 * 10**6, transcendentals=0),
        name="finish",
    )(att, left, x, right, act, out_w, down_w)


def middle_kernel(scal, dbr, att, out_w, d_att_o, mine_o, sent_o):
    core = scal[0, CORE]
    for r in range(dbr.shape[0] // 256):
        rows = slice(r * 256, (r + 1) * 256)
        d_att_o[rows, :] = dot_t(dbr[rows, :], out_w[...]).astype(BF16)
    total = t_dot(att[...], dbr[...]).astype(BF16)
    for half in range(2):
        part = total[half * 256 : (half + 1) * 256].reshape(16, 16, 512)

        @pl.when(core == half)
        def _():
            for c in range(4):
                mine_o[:, c] = part[:, :, c * 128 : (c + 1) * 128]

        @pl.when(core != half)
        def _():
            for c in range(4):
                sent_o[:, c] = part[:, :, c * 128 : (c + 1) * 128]


def back_kernel(blocks, scal, d_att, att, lse, seg, qkv, normed, dqkv_o, mine_o, sent_o,
                q_s, kc, vx, dk_s, dv_s, bias_s, dqkv_s, normed_s):
    step = pl.program_id(0)
    core = scal[0, CORE]

    def rows_of(block, count=1):
        return pl.ds(pl.multiple_of(block * BLOCK, BLOCK), count * BLOCK)

    @pl.when(step < blocks // 2)
    def _():
        rows = rows_of(2 * step, 2)
        q_s[rows, :] = qkv[:, 0:512] * jnp.asarray(0.125, BF16)
        normed_s[rows, :] = normed[...]
        for h in range(2):
            part = slice(h * BLOCK, (h + 1) * BLOCK)
            split_pairs(qkv[part, 512:1024], qkv[part, 1024:1536], kc, vx, 2 * step + h)
        both = pl.ds(pl.multiple_of(step * 512, 512), 512)
        for p in range(PAIRS):
            dk_s[p, both, :] = jnp.zeros((512, 128), F32)
            dv_s[p, both, :] = jnp.zeros((512, 128), F32)

    @pl.when((step >= 1) & (step <= blocks // 2))
    def _():
        i = 2 * (step - 1)
        rows = rows_of(i, 2)
        low = scal[0, i]
        n_keys = scal[0, HIGH + i + 1] - low + 1
        keys_at = pl.multiple_of(low * 256, 256)
        seg_q = [jnp.broadcast_to(seg[i + h].astype(F32), (BLOCK, BLOCK)) for h in range(2)]

        def back(n):
            keys = pl.ds(keys_at, n * 256)
            for t in range(n):
                seg_k = column(seg[low + t].astype(F32))
                for h in range(2):
                    cols = slice(h * BLOCK, (h + 1) * BLOCK)
                    bias_s[t * BLOCK : (t + 1) * BLOCK, cols] = jnp.where(seg_k == seg_q[h], 0.0, -1e30)

            def pair(p, carry):
                cols = pl.ds(pl.multiple_of(p * 128, 128), 128)
                q = q_s[rows, cols]
                d_out = d_att[:, cols]
                minus = -(d_out.astype(F32) * att[:, cols].astype(F32))
                scores = dot_t(kc[p, keys, :], jnp.concatenate([q, lse[:, cols]], axis=1))
                d_probs = dot_t(vx[p, keys, :], jnp.concatenate([d_out, minus.astype(BF16)], axis=1))
                parts, d_parts = [], []
                for t in range(n):
                    bias = bias_s[t * BLOCK : (t + 1) * BLOCK, :]
                    for h in range(2):
                        part = slice((2 * t + h) * BLOCK, (2 * t + h + 1) * BLOCK)
                        probs = jnp.exp(scores[part] + bias)
                        parts.append(probs.astype(BF16))
                        d_parts.append((probs * d_probs[part]).astype(BF16))
                d_scores = jnp.concatenate(d_parts, axis=0)
                dk_s[p, keys, :] += dot(d_scores, q)
                dv_s[p, keys, :] += dot(jnp.concatenate(parts, axis=0), d_out)
                d_q = t_dot(d_scores, kc[p, keys, 0:128]) * 0.125
                dqkv_s[rows, pl.ds(pl.multiple_of(p * 384, 128), 128)] = d_q.astype(BF16)
                return carry

            lax.fori_loop(0, PAIRS, pair, 0, unroll=2)

        for n in range(1, 7):
            pl.when(n_keys == n)(functools.partial(back, n))

    @pl.when(step >= 2)
    def _():
        even = lax.broadcasted_iota(jnp.int32, (BLOCK, BLOCK), 1) < 64
        for h in range(2):
            block = 2 * (step - 2) + h
            rows = rows_of(block)
            up = pl.ds(pl.multiple_of(block * 256, 256), 128)
            down = pl.ds(pl.multiple_of(block * 256 + 128, 128), 128)
            for p in range(PAIRS):
                for t, source in enumerate((dk_s, dv_s)):
                    both = jnp.where(even, source[p, up, :], source[p, down, :])
                    spot = p * 384 + 128 + t * 128
                    dqkv_s[rows, spot : spot + 128] = both.astype(BF16)
        dqkv_o[...] = dqkv_s[rows_of(2 * (step - 2), 2), :]

    @pl.when(step == blocks // 2 + 1)
    def _():
        for p in range(PAIRS):
            part = t_dot(normed_s[...], dqkv_s[:, p * 384 : (p + 1) * 384]).astype(BF16)
            for half in range(2):
                piece = part[half * 256 : (half + 1) * 256].reshape(16, 16, 384)

                @pl.when(core == half)
                def _():
                    mine_o[:, p] = piece

                @pl.when(core != half)
                def _():
                    sent_o[:, p] = piece


def entry_kernel(blocks, left, x, right, dbr, gain, ln2, weight, d_qkv,
                 grad_o, left_o, right_o, small_o, w_s, x_s, ln_s, grad_s):
    r = pl.program_id(0)
    tiles = blocks // 2

    @pl.when(r == 0)
    def _():
        for p in range(PAIRS):
            for part in range(3):
                spot = part * 512 + p * 128
                to = p * 384 + part * 128
                w_s[:, to : to + 128] = weight[:, spot : spot + 128]
        for t in range(tiles):
            x_s[t * 256 : (t + 1) * 256, :] = two_blocks(left, x, right, t)
        ln_s[0:2, :] = jnp.zeros((2, D), F32)

    rows = pl.ds(pl.multiple_of(r * 256, 256), 256)
    d_n1 = dot_t(d_qkv[...], w_s[...])
    n1, inverse = normalize(x_s[rows, :].astype(F32))
    e = d_n1 * gain[...]
    mean_e = jnp.mean(e, axis=-1, keepdims=True)
    mean_en = jnp.mean(e * n1, axis=-1, keepdims=True)
    grad_s[rows, :] = dbr[...].astype(F32) + (e - mean_e - n1 * mean_en) * inverse
    ln_s[0:1, :] += jnp.sum(d_n1 * n1, axis=0, keepdims=True)
    ln_s[1:2, :] += jnp.sum(d_n1, axis=0, keepdims=True)

    @pl.when(r == tiles - 1)
    def _():
        inner = (blocks - 2) * BLOCK
        grad_o[...] = grad_s[HALO : HALO + inner, :]
        left_o[...] = grad_s[0:HALO, :].astype(BF16)
        right_o[...] = grad_s[HALO + inner :, :].astype(BF16)
        vectors = [ln_s[0:1, :], ln_s[1:2, :], ln2[0:1, :], ln2[1:2, :]]
        small_o[...] = jnp.concatenate(
            [v[:, c * 128 : (c + 1) * 128] for v in vectors for c in range(4)], axis=0
        )


def join_kernel(share, mine, other, out_m, out_o, result):
    wide = share.shape[-1]
    result[:, :, :, 0:wide] = jnp.broadcast_to(share[...][None, None], (*result.shape[:2], *share.shape))
    value = mine[...].astype(F32) + other[...].astype(F32)
    result[:, :, :, wide : wide + 384] = value.astype(BF16)
    value = out_m[...].astype(F32) + out_o[...].astype(F32)
    result[:, :, :, wide + 384 : wide + 512] = value.astype(BF16)


def join_call(share, mine, other, out_m, out_o):
    at = lambda s: (s, 0, 0, 0)
    block = (8, 4, 16, share.shape[-1] + 512)
    return pl.pallas_call(
        join_kernel,
        grid=(2,),
        in_specs=[pl.BlockSpec(share.shape, lambda s: (0, 0))]
        + [pl.BlockSpec((8, 4, 16, 384), at)] * 2 + [pl.BlockSpec((8, 4, 16, 128), at)] * 2,
        out_specs=pl.BlockSpec(block, at),
        out_shape=shape_of((16, *block[1:]), BF16),
        compiler_params=params(24),
        name="join",
    )(share, mine, other, out_m, out_o)


def whole(shape):
    return pl.BlockSpec(shape, lambda s, scal: (0,) * len(shape))


def shape_of(shape, dtype):
    return jax.ShapeDtypeStruct(shape, dtype)


def params(mib=58):
    return pltpu.CompilerParams(dimension_semantics=("arbitrary",), vmem_limit_bytes=mib * MIB)


def attend_call(scal, left, x, right, seg, gain, shift, weight):
    rows = x.shape[0] + 2 * HALO
    blocks = rows // BLOCK
    at = lambda s, scal: (jnp.maximum(s - 1, 0), 0)
    return pl.pallas_call(
        functools.partial(attend_kernel, blocks),
        grid_spec=pltpu.PrefetchScalarGridSpec(
            num_scalar_prefetch=1,
            grid=(blocks // 2 + 1,),
            in_specs=[
                whole((HALO, D)), whole(x.shape), whole((HALO, D)), whole(seg.shape),
                whole((1, D)), whole((1, D)), whole(weight.shape),
            ],
            out_specs=[
                pl.BlockSpec(memory_space=pl.ANY),
                pl.BlockSpec(memory_space=pl.ANY),
                pl.BlockSpec((2 * BLOCK, D), at),
                pl.BlockSpec((2 * BLOCK, D), at),
            ],
            scratch_shapes=[
                pltpu.VMEM((rows, D), BF16),
                pltpu.VMEM((rows, 3 * D), BF16),
                pltpu.VMEM((PAIRS, blocks * 256, 128), BF16),
                pltpu.VMEM((PAIRS, blocks * 256, 256), BF16),
                pltpu.SemaphoreType.DMA((blocks,)),
            ],
        ),
        out_shape=[
            shape_of((rows, D), BF16),
            shape_of((rows, 3 * D), BF16),
            shape_of((rows, D), BF16),
            shape_of((rows, D), BF16),
        ],
        compiler_params=params(),
        cost_estimate=pl.CostEstimate(flops=8 * 10**9, bytes_accessed=25 * 10**6, transcendentals=4 * 10**6),
        name="attend",
    )(scal, left, x, right, seg, gain, shift, weight)


def feed_call(scal, att, left, x, right, cot_l, cot, cot_r, out_w, up_w, down_w, gain, shift):
    rows = att.shape[0]
    blocks = rows // BLOCK
    half = (16, 4, 16, 1024)
    anywhere = pl.BlockSpec(memory_space=pl.ANY)
    return pl.pallas_call(
        functools.partial(feed_kernel, blocks),
        grid_spec=pltpu.PrefetchScalarGridSpec(
            num_scalar_prefetch=1,
            grid=(FF // 512,),
            in_specs=[
                whole((rows, D)),
                whole((HALO, D)), whole(x.shape), whole((HALO, D)),
                whole((HALO, D)), whole(x.shape), whole((HALO, D)),
                whole((D, D)),
                pl.BlockSpec((D, 512), lambda s, scal: (0, s)),
                pl.BlockSpec((512, D), lambda s, scal: (s, 0)),
                whole((1, D)), whole((1, D)),
            ],
            out_specs=[
                whole((rows, D)), pl.BlockSpec((rows, 512), lambda s, scal: (0, s)), whole((2, D)),
                anywhere, anywhere,
            ],
            scratch_shapes=[
                pltpu.VMEM((rows, D), F32),
                pltpu.VMEM((rows, 128), F32),
                pltpu.VMEM((rows, D), BF16),
                pltpu.VMEM(half, BF16),
                pltpu.VMEM(half, BF16),
                pltpu.SemaphoreType.DMA((3 * (FF // 512),)),
                pltpu.VMEM((rows, D), BF16),
                pltpu.VMEM((FF // 512, rows, 512), BF16),
                pltpu.VMEM((FF // 512, D, 512), BF16),
            ] + [pltpu.VMEM((256, 512), F32)] * 4,
        ),
        out_shape=[
            shape_of((rows, D), BF16),
            shape_of((rows, FF), BF16),
            shape_of((2, D), F32),
            shape_of(half, BF16),
            shape_of(half, BF16),
        ],
        compiler_params=params(),
        cost_estimate=pl.CostEstimate(flops=16 * 10**9, bytes_accessed=25 * 10**6, transcendentals=3 * 10**6),
        name="feed",
    )(scal, att, left, x, right, cot_l, cot, cot_r, out_w, up_w, down_w, gain, shift)


def middle_call(scal, dbr, att, out_w):
    part = (16, 4, 16, 128)
    vmem = pl.BlockSpec(memory_space=pltpu.VMEM)
    return pl.pallas_call(
        middle_kernel,
        in_specs=[pl.BlockSpec(memory_space=pltpu.SMEM)] + [vmem] * 3,
        out_specs=[vmem] * 3,
        out_shape=[shape_of(dbr.shape, BF16), shape_of(part, BF16), shape_of(part, BF16)],
        compiler_params=pltpu.CompilerParams(vmem_limit_bytes=58 * MIB),
        cost_estimate=pl.CostEstimate(flops=2 * 10**9, bytes_accessed=5 * 10**6, transcendentals=0),
        name="middle",
    )(scal, dbr, att, out_w)


def back_call(scal, d_att, att, lse, seg, qkv, normed):
    rows = qkv.shape[0]
    blocks = rows // BLOCK
    half = (16, PAIRS, 16, 384)
    last = blocks // 2 - 1
    lead = lambda s, scal: (jnp.minimum(s, last), 0)
    now = lambda s, scal: (jnp.clip(s - 1, 0, last), 0)
    done = lambda s, scal: (jnp.maximum(s - 2, 0), 0)
    return pl.pallas_call(
        functools.partial(back_kernel, blocks),
        grid_spec=pltpu.PrefetchScalarGridSpec(
            num_scalar_prefetch=1,
            grid=(blocks // 2 + 2,),
            in_specs=[
                pl.BlockSpec((2 * BLOCK, D), now), pl.BlockSpec((2 * BLOCK, D), now), pl.BlockSpec((2 * BLOCK, D), now),
                whole(seg.shape),
                pl.BlockSpec((2 * BLOCK, 3 * D), lead), pl.BlockSpec((2 * BLOCK, D), lead),
            ],
            out_specs=[pl.BlockSpec((2 * BLOCK, 3 * D), done), whole(half), whole(half)],
            scratch_shapes=[
                pltpu.VMEM((rows, D), BF16),
                pltpu.VMEM((PAIRS, blocks * 256, 256), BF16),
                pltpu.VMEM((PAIRS, blocks * 256, 256), BF16),
                pltpu.VMEM((PAIRS, blocks * 256, 128), F32),
                pltpu.VMEM((PAIRS, blocks * 256, 128), F32),
                pltpu.VMEM((6 * BLOCK, 2 * BLOCK), F32),
                pltpu.VMEM((rows, 3 * D), BF16),
                pltpu.VMEM((rows, D), BF16),
            ],
        ),
        out_shape=[shape_of((rows, 3 * D), BF16), shape_of(half, BF16), shape_of(half, BF16)],
        compiler_params=params(),
        cost_estimate=pl.CostEstimate(flops=12 * 10**9, bytes_accessed=20 * 10**6, transcendentals=4 * 10**6),
        name="back",
    )(scal, d_att, att, lse, seg, qkv, normed)


def entry_call(left, x, right, dbr, gain, ln2, weight, d_qkv):
    rows = dbr.shape[0]
    fixed = lambda v: pl.BlockSpec(v.shape, lambda s: (0,) * len(v.shape))
    at = lambda s: (s, 0)
    edge = shape_of((HALO, D), BF16)
    outs = [shape_of(x.shape, F32), edge, edge, shape_of((16, 128), F32)]
    return pl.pallas_call(
        functools.partial(entry_kernel, rows // BLOCK),
        grid=(rows // 256,),
        in_specs=[
            fixed(left), fixed(x), fixed(right), pl.BlockSpec((256, D), at), fixed(gain), fixed(ln2),
            fixed(weight), pl.BlockSpec((256, 3 * D), at),
        ],
        out_specs=[fixed(v) for v in outs],
        out_shape=outs,
        scratch_shapes=[
            pltpu.VMEM((D, 3 * D), BF16), pltpu.VMEM((rows, D), BF16), pltpu.VMEM((8, D), F32),
            pltpu.VMEM((rows, D), F32),
        ],
        compiler_params=params(),
        cost_estimate=pl.CostEstimate(flops=2 * 10**9, bytes_accessed=15 * 10**6, transcendentals=0),
        name="entry",
    )(left, x, right, dbr, gain, ln2, weight, d_qkv)


def other_core(value):
    return lax.ppermute(value, "core", [(0, 1), (1, 0)])


def all_shares(value, groups):
    parts = lax.all_to_all(value, ("rows", "x"), 0, 0, tiled=True)
    return jnp.sum(parts.astype(F32), axis=0).astype(BF16)


def gather_shares(share, groups):
    copies = jnp.broadcast_to(share[None], (groups, *share.shape))
    return lax.all_to_all(copies, ("rows", "x"), 0, 0, tiled=True)


def per_device(
    inputs, qkv_weight, out_weight, up_weight, down_weight, norm1_gain, norm1_shift,
    norm2_gain, norm2_shift, segment_ids, item_steps, gen_rank, out_grad,
):
    x = inputs[0]
    positions = x.shape[0]
    blocks = (positions + 2 * HALO) // BLOCK
    chips = lax.axis_size("rows") * lax.axis_size("x")
    seq_parts = lax.axis_size("x") * lax.axis_size("core")
    seq = ("x", "core")
    to_right = [(i, (i + 1) % seq_parts) for i in range(seq_parts)]
    to_left = [((i + 1) % seq_parts, i) for i in range(seq_parts)]

    place = jnp.stack([lax.axis_index(seq), lax.axis_index("core")]).astype(jnp.int32)
    tie = lax.optimization_barrier
    left = lax.ppermute(x[positions - HALO :], seq, to_right)
    right = lax.ppermute(x[:HALO], seq, to_left)
    scal, seg_rows, cot, send_l, send_r = prepare_call(
        place, segment_ids, item_steps, gen_rank, out_grad[0]
    )
    cot_l = lax.ppermute(send_r, seq, to_right)
    cot_r = lax.ppermute(send_l, seq, to_left)

    gain1, shift1 = norm1_gain.reshape(1, D), norm1_shift.reshape(1, D)
    gain2, shift2 = norm2_gain.reshape(1, D), norm2_shift.reshape(1, D)
    normed1, qkv, att, lse = attend_call(
        scal, left, x, right, seg_rows, gain1, shift1, qkv_weight
    )
    d_branch, act, ln2, mine_a, sent_a = feed_call(
        scal, att, left, x, right, cot_l, cot, cot_r, out_weight, up_weight, down_weight, gain2, shift2
    )
    got_a = other_core(sent_a)
    half_a = (mine_a.astype(F32) + got_a.astype(F32)).astype(BF16)
    d_att, mine_o, sent_o = middle_call(scal, d_branch, att, out_weight)
    d_att, half_a = tie((d_att, half_a))
    share_a = all_shares(half_a.reshape(chips, -1, 1024), chips)
    d_qkv, mine_b, sent_b = back_call(scal, d_att, att, lse, seg_rows, qkv, normed1)
    joined = join_call(share_a, mine_b, other_core(sent_b), mine_o, other_core(sent_o))
    joined, d_branch, att = tie((joined, d_branch, att))
    got = lax.all_to_all(joined.reshape(chips, -1, 1536), ("rows", "x"), 0, 0, tiled=True)
    grad, grad_l, grad_r, small = entry_call(
        left, x, right, d_branch, gain1, ln2, qkv_weight, d_qkv
    )
    small = small + other_core(small)
    out, out_l, out_r = finish_call(att, left, x, right, act, out_weight, down_weight)
    edge_l = jnp.concatenate([out_l, grad_l], axis=0)
    edge_r = jnp.concatenate([out_r, grad_r], axis=0)
    from_r = lax.ppermute(edge_l, seq, to_left)
    from_l = lax.ppermute(edge_r, seq, to_right)
    got, from_l, from_r, small = tie((got, from_l, from_r, small))
    far_a = other_core(got)
    share_b = jnp.sum(got[:, :, 1024:].astype(F32), axis=0).astype(BF16)
    near_b = gather_shares(jnp.concatenate([share_b, small.astype(BF16)], axis=1), chips)
    grads_a = unpack_call(scal, got.reshape(16, 4, 16, 1536))
    grad_down, grad_up = unpack_call(scal, far_a.reshape(16, 4, 16, 1536), grads_a)
    output, input_grad = patch_call(scal, out, grad, seg_rows, from_l, from_r)
    near_b, grad_down, input_grad = tie((near_b, grad_down, input_grad))
    far_b = other_core(near_b)
    *grads_b, v0, v1, v2, v3 = rest_call(scal, near_b.reshape(16, 4, 16, 640))
    grad_out, grad_qkv = rest_call(scal, far_b.reshape(16, 4, 16, 640), grads_b)
    vectors = (v0, v1, v2, v3)
    vectors = [v.reshape(D) for v in vectors]
    return (
        output[None], input_grad[None], grad_qkv, grad_out, grad_up, grad_down,
        vectors[0], vectors[1], vectors[2], vectors[3],
    )


def solution(mesh):
    rows = mesh.devices.shape[0]
    parts = mesh.devices.shape[1]
    split = Mesh(mesh.devices.reshape(rows, parts // 2, 2), ("rows", "x", "core"))
    seq = ("x", "core")
    return jax.shard_map(
        per_device,
        mesh=split,
        in_specs=(
            P("rows", seq, None), P(), P(), P(), P(), P(), P(), P(), P(),
            P("rows", None), P("rows", None), P("rows", seq), P("rows", seq, None),
        ),
        out_specs=(
            P("rows", seq, None), P("rows", seq, None),
            P(), P(), P(), P(), P(), P(), P(), P(),
        ),
        check_vma=False,
    )
```

```python
import functools

import jax
import jax.numpy as jnp
from jax import lax
from jax.experimental import pallas as pl
from jax.experimental.pallas import tpu as pltpu
from jax.sharding import Mesh
from jax.sharding import PartitionSpec as P

D = 512
HEADS = 8
PAIRS = HEADS // 2
FF = 2048
EPS = 1e-05
HALO = 128
BLOCK = 128
BF16 = jnp.bfloat16
F32 = jnp.float32
MIB = 1024 * 1024
HIGH, CORE, DROP_L, DROP_R = 16, 32, 33, 34


def dot(a, b):
    return lax.dot_general(a, b, (((1,), (0,)), ((), ())), preferred_element_type=F32)


def dot_t(a, b):
    return lax.dot_general(a, b, (((1,), (1,)), ((), ())), preferred_element_type=F32)


def t_dot(a, b):
    return lax.dot_general(a, b, (((0,), (0,)), ((), ())), preferred_element_type=F32)


def normalize(value):
    center = jnp.mean(value, axis=-1, keepdims=True)
    centred = value - center
    spread = jnp.mean(centred * centred, axis=-1, keepdims=True)
    inverse = lax.rsqrt(spread + EPS)
    return centred * inverse, inverse


def two_blocks(left, middle, right, tile):
    last = 1 + middle.shape[0] // BLOCK
    parts = []
    for block in (2 * tile, 2 * tile + 1):
        if block == 0:
            parts.append(left[...])
        elif block == last:
            parts.append(right[...])
        else:
            parts.append(middle[(block - 1) * BLOCK : block * BLOCK, :])
    return jnp.concatenate(parts, axis=0)


def split_pairs(keys, values, kc, vx, block):
    lane = lax.broadcasted_iota(jnp.int32, (BLOCK, BLOCK), 1)
    even = lane < 64
    zero = jnp.zeros((BLOCK, BLOCK), BF16)
    ones_even = even.astype(F32).astype(BF16)
    ones_odd = (~even).astype(F32).astype(BF16)
    base = block * 256
    for p in range(PAIRS):
        k = keys[:, p * 128 : (p + 1) * 128]
        v = values[:, p * 128 : (p + 1) * 128]
        kc[p, pl.ds(base, 128), 0:128] = jnp.where(even, k, zero)
        kc[p, pl.ds(base + 128, 128), 0:128] = jnp.where(even, zero, k)
        vx[p, pl.ds(base, 128), 0:128] = jnp.where(even, v, zero)
        vx[p, pl.ds(base + 128, 128), 0:128] = jnp.where(even, zero, v)
        vx[p, pl.ds(base, 128), 128:256] = ones_even
        vx[p, pl.ds(base + 128, 128), 128:256] = ones_odd
        if kc.shape[2] == 256:
            minus = jnp.where(lax.rem(lane, 64) < 3, -1.0, 0.0)
            kc[p, pl.ds(base, 128), 128:256] = jnp.where(even, minus, 0.0).astype(BF16)
            kc[p, pl.ds(base + 128, 128), 128:256] = jnp.where(even, 0.0, minus).astype(BF16)


def mask_rows(seg, row, low, n):
    seg_q = column(seg[row].astype(F32))
    return [
        jnp.where(seg_q == jnp.broadcast_to(seg[low + t].astype(F32), (BLOCK, BLOCK)), 0.0, -1e30)
        for t in range(n)
    ]


def column(row):
    return jnp.transpose(jnp.broadcast_to(row, (BLOCK, BLOCK)))


def keep_rows(values, mask):
    return jnp.concatenate(
        [
            jnp.where(mask, values[:, c * 128 : (c + 1) * 128].astype(F32), 0.0).astype(BF16)
            for c in range(D // 128)
        ],
        axis=1,
    )


def prepare_kernel(inner, place, segments, steps, rank, out_grad, scal_o, seg_o, cot_o, left_o, right_o, part_s):
    seq = place[0]
    row_blocks = segments.shape[1] // BLOCK
    blocks = inner + 2
    rows = []
    for b in range(blocks):
        at = seq * inner + b - 1
        if b == 0:
            at = jnp.maximum(at, 0)
        if b == blocks - 1:
            at = jnp.minimum(at, row_blocks - 1)
        row = segments[0:1, pl.ds(pl.multiple_of(at * BLOCK, BLOCK), BLOCK)]
        if b == 0:
            row = jnp.where(seq > 0, row, -1)
        if b == blocks - 1:
            row = jnp.where(seq * inner + inner < row_blocks, row, 1000)
        rows.append(row)
        seg_o[b] = row
    window = jnp.concatenate(rows, axis=0)
    local = window[1 : inner + 1]
    first, last = window[:, 0:1], window[:, BLOCK - 1 : BLOCK]
    below = jnp.zeros(window.shape, F32)
    upto = jnp.zeros(window.shape, F32)
    for row in rows:
        below += (row < first).astype(F32)
        upto += (row <= last).astype(F32)
    part_s[...] = jnp.zeros(part_s.shape, F32)
    part_s[0:blocks, :] = below
    part_s[HIGH : HIGH + blocks, :] = upto
    counts = dot_t(jnp.ones((8, BLOCK), BF16), part_s[...].astype(BF16))[0:1]

    def border(before, after):
        value = before[-1:, BLOCK - 1 : BLOCK]
        across = value == after[0:1, 0:1]
        sizes = [jnp.sum((part == value).astype(F32), axis=(0, 1), keepdims=True) for part in (before, after)]
        return value, across, sizes[0] >= sizes[1]

    value_l, across_l, to_left_l = border(rows[0], local)
    value_r, across_r, to_left_r = border(local, rows[-1])
    drop_l = jnp.where(across_l & to_left_l, value_l, -2)
    drop_r = jnp.where(across_r & jnp.logical_not(to_left_r), value_r, -2)
    lane = lax.broadcasted_iota(jnp.int32, (1, BLOCK), 1)
    at_block = jnp.floor(jnp.where(lane >= HIGH, counts - 1.0, counts) * (1.0 / BLOCK)).astype(jnp.int32)
    at_block = jnp.where(lane == CORE, place[1], at_block)
    at_block = jnp.where(lane == DROP_L, drop_l, at_block)
    scal_o[...] = jnp.where(lane == DROP_R, drop_r, at_block)

    token = jnp.zeros(local.shape, jnp.int32)
    for slot in range(steps.shape[1]):
        token = jnp.where(local == slot, steps[0, slot], token)
    for b in range(inner):
        part = slice(b * BLOCK, (b + 1) * BLOCK)
        keep = rank[0:1, part] >= token[b : b + 1]
        seg = rows[b + 1]
        own = (seg != drop_l) & (seg != drop_r)
        values = out_grad[part, :]
        cot_o[part, :] = keep_rows(values, column((keep & own).astype(F32)) > 0.5)
        if b == 0:
            left_o[...] = keep_rows(values, column((keep & (seg == drop_l)).astype(F32)) > 0.5)
        if b == inner - 1:
            right_o[...] = keep_rows(values, column((keep & (seg == drop_r)).astype(F32)) > 0.5)


def prepare_call(place, segments, steps, rank, out_grad):
    inner = out_grad.shape[0] // BLOCK
    vmem = pl.BlockSpec(memory_space=pltpu.VMEM)
    smem = pl.BlockSpec(memory_space=pltpu.SMEM)
    return pl.pallas_call(
        functools.partial(prepare_kernel, inner),
        in_specs=[smem, vmem, smem, vmem, vmem],
        out_specs=[vmem] * 5,
        out_shape=[
            shape_of((1, BLOCK), jnp.int32),
            shape_of((inner + 2, 1, BLOCK), jnp.int32),
            shape_of(out_grad.shape, BF16),
            shape_of((HALO, D), BF16),
            shape_of((HALO, D), BF16),
        ],
        scratch_shapes=[pltpu.VMEM((BLOCK, BLOCK), F32)],
        compiler_params=pltpu.CompilerParams(vmem_limit_bytes=58 * MIB),
        cost_estimate=pl.CostEstimate(flops=10**6, bytes_accessed=4 * 10**6, transcendentals=0),
        name="prepare",
    )(place, segments, steps, rank, out_grad)


def patch_kernel(blocks, scal, out, grad, seg, left, right, out_o, grad_o):
    step = pl.program_id(0)
    drop_l, drop_r = scal[0, DROP_L], scal[0, DROP_R]
    row = seg[0]
    drop = jnp.where(step == 0, drop_l, drop_r)
    lost = column((row == drop).astype(F32)) > 0.5
    for c in range(D // 128):
        cols = slice(c * 128, (c + 1) * 128)
        for mine, start, result in ((out, 0, out_o), (grad, HALO, grad_o)):
            part = slice(start, start + HALO)
            other = jnp.where(step == 0, left[part, cols].astype(F32), right[part, cols].astype(F32))
            value = jnp.where(lost, other, mine[:, cols].astype(F32))
            result[:, cols] = value.astype(result.dtype)


def patch_call(scal, out, grad, seg, left, right):
    inner = out.shape[0] // BLOCK
    block = lambda s, scal: (s * (inner - 1), 0)
    return pl.pallas_call(
        functools.partial(patch_kernel, inner + 2),
        grid_spec=pltpu.PrefetchScalarGridSpec(
            num_scalar_prefetch=1,
            grid=(2,),
            in_specs=[
                pl.BlockSpec((BLOCK, D), block),
                pl.BlockSpec((BLOCK, D), block),
                pl.BlockSpec((1, 1, BLOCK), lambda s, scal: (1 + s * (inner - 1), 0, 0)),
                whole((2 * HALO, D)), whole((2 * HALO, D)),
            ],
            out_specs=[pl.BlockSpec((BLOCK, D), block), pl.BlockSpec((BLOCK, D), block)],
        ),
        out_shape=[shape_of(out.shape, out.dtype), shape_of(grad.shape, grad.dtype)],
        input_output_aliases={1: 0, 2: 1},
        compiler_params=params(),
        name="patch",
    )(scal, out, grad, seg, left, right)


def unpack_feed(a, down_o, up_o):
    rows = a.shape[0] * 16
    down_o[...] = a[:, :, :, 0:512].astype(F32).reshape(4 * rows, 512)
    for c in range(4):
        up_o[:, c * 512 : (c + 1) * 512] = a[:, c, :, 512:1024].astype(F32).reshape(rows, 512)


def rest_kernel(first, scal, a, *refs):
    (out_o, qkv_o), vectors_o = refs[first : first + 2], refs[first + 2 :]
    for c in range(4):
        value = a[:, c, :, 0:512].astype(F32).reshape(128, 512)
        for part in range(3):
            spot = part * 512 + c * 128
            qkv_o[:, spot : spot + 128] = value[:, part * 128 : (part + 1) * 128]
        out_o[:, c * 128 : (c + 1) * 128] = value[:, 384:512]
    if vectors_o:
        step = pl.program_id(0)
        part = jnp.sum(a[:, :, :, 512:640].astype(F32), axis=(0, 1))
        for v in range(4):
            row = jnp.concatenate([part[4 * v + c : 4 * v + c + 1] for c in range(4)], axis=1)
            vectors_o[v][...] = jnp.where(step == 0, row, row + vectors_o[v][...])


def rest_call(scal, value, before=()):
    def part(s, scal):
        half = scal[0, CORE] if not before else 1 - scal[0, CORE]
        return (half * 2 + s, 0)

    vectors = [] if before else [(1, D)] * 4
    return pl.pallas_call(
        functools.partial(rest_kernel, len(before)),
        grid_spec=pltpu.PrefetchScalarGridSpec(
            num_scalar_prefetch=1,
            grid=(2,),
            in_specs=[pl.BlockSpec((8, *value.shape[1:]), lambda s, scal: (s, 0, 0, 0))]
            + [pl.BlockSpec(memory_space=pl.ANY)] * len(before),
            out_specs=[pl.BlockSpec((128, D), part), pl.BlockSpec((128, 3 * D), part)]
            + [whole(v) for v in vectors],
        ),
        out_shape=[shape_of(v, F32) for v in ((D, D), (D, 3 * D), *vectors)],
        input_output_aliases={2 + k: k for k in range(len(before))},
        compiler_params=params(24),
        cost_estimate=pl.CostEstimate(flops=10**6, bytes_accessed=4 * 10**6, transcendentals=0),
        name="rest",
    )(scal, value, *before)


def unpack_call(scal, value, before=()):
    steps = 4

    def out(s, scal):
        half = scal[0, CORE] if not before else 1 - scal[0, CORE]
        return (half * steps + s, 0)

    def kernel(scal, a, *refs):
        unpack_feed(a, *refs[len(before) :])

    shapes = ((FF, D), (D, FF))
    return pl.pallas_call(
        kernel,
        grid_spec=pltpu.PrefetchScalarGridSpec(
            num_scalar_prefetch=1,
            grid=(steps,),
            in_specs=[pl.BlockSpec((16 // steps, *value.shape[1:]), lambda s, scal: (s, 0, 0, 0))]
            + [pl.BlockSpec(memory_space=pl.ANY)] * len(before),
            out_specs=[pl.BlockSpec((rows // (2 * steps), cols), out) for rows, cols in shapes],
        ),
        out_shape=[shape_of(shape, F32) for shape in shapes],
        input_output_aliases={2 + k: k for k in range(len(before))},
        compiler_params=params(24),
        cost_estimate=pl.CostEstimate(flops=10**6, bytes_accessed=10 * 10**6, transcendentals=0),
        name="unpack",
    )(scal, value, *before)


def attend_kernel(blocks, scal, left, x, right, seg, gain, shift, weight,
                  normed_o, qkv_o, att_o, lse_o, normed_s, qkv_s, kc, vx, sems):
    step = pl.program_id(0)
    tiles = blocks // 2

    def copies(r):
        rows = slice(r * 256, (r + 1) * 256)
        return (
            pltpu.make_async_copy(normed_s.at[rows, :], normed_o.at[rows, :], sems.at[2 * r]),
            pltpu.make_async_copy(qkv_s.at[rows, :], qkv_o.at[rows, :], sems.at[2 * r + 1]),
        )

    @pl.when(step == 0)
    def _():
        for r in range(tiles + 1):
            if r < tiles:
                base, _ = normalize(two_blocks(left, x, right, r).astype(F32))
                normed_s[r * 256 : (r + 1) * 256, :] = (base * gain[...] + shift[...]).astype(BF16)
            if r > 0:
                rows = slice((r - 1) * 256, r * 256)
                qkv = dot(normed_s[rows, :], weight[...]).astype(BF16)
                qkv_s[rows, :] = qkv
                for half in range(2):
                    part = qkv[half * 128 : (half + 1) * 128]
                    split_pairs(part[:, 512:1024], part[:, 1024:1536], kc, vx, 2 * (r - 1) + half)
                for copy in copies(r - 1):
                    copy.start()

    @pl.when(step > 0)
    def _():
        lane = lax.broadcasted_iota(jnp.int32, (BLOCK, BLOCK), 1)
        place = lax.rem(lane, 64)
        for h in range(2):
            i = 2 * (step - 1) + h
            rows = pl.ds(pl.multiple_of(i * BLOCK, BLOCK), BLOCK)
            part = slice(h * BLOCK, (h + 1) * BLOCK)
            low = scal[0, i]
            n_keys = scal[0, HIGH + i] - low + 1
            first = pl.multiple_of(low * 256, 256)

            def attend(n):
                bias = mask_rows(seg, i, low, n)
                def pair(p, carry):
                    cols = pl.ds(pl.multiple_of(p * 128, 128), 128)
                    q = qkv_s[rows, cols] * jnp.asarray(0.125, BF16)
                    scores = dot_t(q, kc[p, pl.ds(first, n * 256), :])
                    tiles_s = [
                        [scores[:, t * 256 + o * 128 : t * 256 + o * 128 + 128] + bias[t] for t in range(n)]
                        for o in range(2)
                    ]
                    highest = [
                        jnp.max(functools.reduce(jnp.maximum, tiles_s[o]), axis=-1, keepdims=True)
                        for o in range(2)
                    ]
                    pieces = []
                    for t in range(n):
                        for o in range(2):
                            pieces.append(jnp.exp(tiles_s[o][t] - highest[o]).astype(BF16))
                    mixed = dot(jnp.concatenate(pieces, axis=1), vx[p, pl.ds(first, n * 256), :])
                    total = mixed[:, 128:256]
                    att_o[part, cols] = (mixed[:, 0:128] * (1.0 / total)).astype(BF16)
                    lse = jnp.where(lane < 64, highest[0], highest[1]) + jnp.log(total)
                    top = lse.astype(BF16).astype(F32)
                    rest = lse - top
                    second = rest.astype(BF16).astype(F32)
                    third = jnp.where(place == 2, rest - second, 0.0)
                    lse_o[part, cols] = jnp.where(
                        place == 0, top, jnp.where(place == 1, second, third)
                    ).astype(BF16)
                    return carry

                lax.fori_loop(0, PAIRS, pair, 0, unroll=PAIRS)

            for n in range(1, 6):
                pl.when(n_keys == n)(functools.partial(attend, n))

    @pl.when(step == tiles)
    def _():
        for r in range(tiles):
            for copy in copies(r):
                copy.wait()


def gelu_both(v):
    c = 0.7978845608028654
    square = v * v
    inner = c + (0.044715 * c) * square
    gate = 0.5 + 0.5 * jnp.tanh(v * inner)
    act = v * gate
    slope = gate + act * ((1.0 - gate) * (6.0 * inner - 4.0 * c))
    return act, slope


def feed_kernel(blocks, scal, att, left, x, right, cot_l, cot, cot_r, out_w, up_w, down_w, gain, shift,
                dbr_o, act_o, ln_o, mine_o, sent_o,
                base_s, rstd_s, cot_s, mine_s, sent_s, sems, n2_s, dpre_s, up_s, *stage_s):
    f = pl.program_id(0)
    steps = FF // 512
    tiles = blocks // 2
    core = scal[0, CORE]

    def down_copy(k, from_s, to_o):
        spot = (slice((k % 2) * 8, (k % 2) * 8 + 8), slice(None), slice(None), slice(0, 512))
        return pltpu.make_async_copy(from_s.at[spot], to_o.at[spot], sems.at[k])

    def up_copies(k):
        spot = (slice(None), slice(k, k + 1), slice(None), slice(512, 1024))
        return [
            pltpu.make_async_copy(mine_s.at[spot], mine_o.at[spot], sems.at[steps + k]),
            pltpu.make_async_copy(sent_s.at[spot], sent_o.at[spot], sems.at[2 * steps + k]),
        ]

    @pl.when(f == 0)
    def _():
        for r in range(tiles):
            rows = slice(r * 256, (r + 1) * 256)
            cot_s[rows, :] = two_blocks(cot_l, cot, cot_r, r)
            mid = two_blocks(left, x, right, r).astype(F32) + dot(att[rows, :], out_w[...])
            base, inverse = normalize(mid)
            base_s[rows, :] = base
            rstd_s[rows, :] = jnp.broadcast_to(inverse, (256, 128))
            n2_s[rows, :] = (base * gain[...] + shift[...]).astype(BF16)

    up_s[f] = up_w[...]
    for r in range(tiles + 1):
        if r < tiles:
            rows = slice(r * 256, (r + 1) * 256)
            stage_s[r % 2][...] = dot(n2_s[rows, :], up_w[...])
            stage_s[2 + r % 2][...] = dot_t(cot_s[rows, :], down_w[...])
        if r > 0:
            rows = slice((r - 1) * 256, r * 256)
            act, slope = gelu_both(stage_s[(r - 1) % 2][...])
            act_o[rows, :] = act.astype(BF16)
            dpre_s[f, rows, :] = (slope * stage_s[2 + (r - 1) % 2][...]).astype(BF16)
    grad_down = t_dot(act_o[...], cot_s[...]).astype(BF16).reshape(8, 4, 16, 512)
    grad_up = t_dot(n2_s[...], dpre_s[f]).astype(BF16).reshape(2, 16, 1, 16, 512)

    for k in range(steps):

        @pl.when((f == k) & (core == k // 2))
        def _():
            mine_s[(k % 2) * 8 : (k % 2) * 8 + 8, :, :, 0:512] = grad_down
            down_copy(k, mine_s, mine_o).start()

        @pl.when((f == k) & (core != k // 2))
        def _():
            sent_s[(k % 2) * 8 : (k % 2) * 8 + 8, :, :, 0:512] = grad_down
            down_copy(k, sent_s, sent_o).start()

    for half in range(2):

        @pl.when(core == half)
        def _():
            mine_s[:, pl.ds(f, 1), :, 512:1024] = grad_up[half]
            sent_s[:, pl.ds(f, 1), :, 512:1024] = grad_up[1 - half]

    for k in range(steps):

        @pl.when(f == k)
        def _():
            for copy in up_copies(k):
                copy.start()

    @pl.when(f == steps - 1)
    def _():
        def turn(r, carry):
            rows = pl.ds(pl.multiple_of(r * 256, 256), 256)
            d_pre = jnp.concatenate([dpre_s[k, rows, :] for k in range(steps)], axis=1)
            up = jnp.concatenate([up_s[k] for k in range(steps)], axis=1)
            d_n2 = dot_t(d_pre, up)
            n2 = base_s[rows, :]
            inverse = jnp.concatenate([rstd_s[rows, :]] * 4, axis=1)
            e = d_n2 * gain[...]
            mean_e = jnp.mean(e, axis=-1, keepdims=True)
            mean_en = jnp.mean(e * n2, axis=-1, keepdims=True)
            d_mid = cot_s[rows, :].astype(F32) + (e - mean_e - n2 * mean_en) * inverse
            dbr_o[rows, :] = d_mid.astype(BF16)
            g, s = carry
            return (
                g + jnp.sum((d_n2 * n2).reshape(32, 8, D), axis=0),
                s + jnp.sum(d_n2.reshape(32, 8, D), axis=0),
            )

        zero = jnp.zeros((8, D), F32)
        g, s = lax.fori_loop(0, tiles, turn, (zero, zero), unroll=tiles)
        ln_o[0:1, :] = jnp.sum(g, axis=0, keepdims=True)
        ln_o[1:2, :] = jnp.sum(s, axis=0, keepdims=True)
        for k in range(steps):
            pl.when(core == k // 2)(lambda: down_copy(k, mine_s, mine_o).wait())
            pl.when(core != k // 2)(lambda: down_copy(k, sent_s, sent_o).wait())
            for copy in up_copies(k):
                copy.wait()


def finish_kernel(blocks, att, left, x, right, act, out_w, down_w, out_o, left_o, right_o):
    tiles = blocks // 2
    for r in range(tiles):
        rows = slice(r * 256, (r + 1) * 256)
        mid = two_blocks(left, x, right, r).astype(F32) + dot(att[rows, :], out_w[...])
        total = (mid + dot(act[rows, :], down_w[...])).astype(BF16)
        for h in range(2):
            block = 2 * r + h
            part = total[h * BLOCK : (h + 1) * BLOCK]
            if block == 0:
                left_o[...] = part
            elif block == blocks - 1:
                right_o[...] = part
            else:
                out_o[(block - 1) * BLOCK : block * BLOCK, :] = part


def finish_call(att, left, x, right, act, out_w, down_w):
    rows = att.shape[0]
    vmem = pl.BlockSpec(memory_space=pltpu.VMEM)
    edge = shape_of((HALO, D), BF16)
    return pl.pallas_call(
        functools.partial(finish_kernel, rows // BLOCK),
        in_specs=[vmem] * 7,
        out_specs=[vmem] * 3,
        out_shape=[shape_of(x.shape, BF16), edge, edge],
        compiler_params=pltpu.CompilerParams(vmem_limit_bytes=58 * MIB),
        cost_estimate=pl.CostEstimate(flops=4 * 10**9, bytes_accessed=12 * 10**6, transcendentals=0),
        name="finish",
    )(att, left, x, right, act, out_w, down_w)


def middle_kernel(scal, dbr, att, out_w, d_att_o, mine_o, sent_o):
    core = scal[0, CORE]
    for r in range(dbr.shape[0] // 256):
        rows = slice(r * 256, (r + 1) * 256)
        d_att_o[rows, :] = dot_t(dbr[rows, :], out_w[...]).astype(BF16)
    total = t_dot(att[...], dbr[...]).astype(BF16)
    for half in range(2):
        part = total[half * 256 : (half + 1) * 256].reshape(16, 16, 512)

        @pl.when(core == half)
        def _():
            for c in range(4):
                mine_o[:, c] = part[:, :, c * 128 : (c + 1) * 128]

        @pl.when(core != half)
        def _():
            for c in range(4):
                sent_o[:, c] = part[:, :, c * 128 : (c + 1) * 128]


def back_kernel(blocks, scal, d_att, att, lse, seg, qkv, normed, dqkv_o, mine_o, sent_o,
                q_s, kc, vx, dk_s, dv_s, bias_s, dqkv_s, normed_s):
    step = pl.program_id(0)
    core = scal[0, CORE]

    def rows_of(block, count=1):
        return pl.ds(pl.multiple_of(block * BLOCK, BLOCK), count * BLOCK)

    @pl.when(step < blocks // 2)
    def _():
        rows = rows_of(2 * step, 2)
        q_s[rows, :] = qkv[:, 0:512] * jnp.asarray(0.125, BF16)
        normed_s[rows, :] = normed[...]
        for h in range(2):
            part = slice(h * BLOCK, (h + 1) * BLOCK)
            split_pairs(qkv[part, 512:1024], qkv[part, 1024:1536], kc, vx, 2 * step + h)
        both = pl.ds(pl.multiple_of(step * 512, 512), 512)
        for p in range(PAIRS):
            dk_s[p, both, :] = jnp.zeros((512, 128), F32)
            dv_s[p, both, :] = jnp.zeros((512, 128), F32)

    @pl.when((step >= 1) & (step <= blocks // 2))
    def _():
        i = 2 * (step - 1)
        rows = rows_of(i, 2)
        low = scal[0, i]
        n_keys = scal[0, HIGH + i + 1] - low + 1
        keys_at = pl.multiple_of(low * 256, 256)
        seg_q = [jnp.broadcast_to(seg[i + h].astype(F32), (BLOCK, BLOCK)) for h in range(2)]

        def back(n):
            keys = pl.ds(keys_at, n * 256)
            for t in range(n):
                seg_k = column(seg[low + t].astype(F32))
                for h in range(2):
                    cols = slice(h * BLOCK, (h + 1) * BLOCK)
                    bias_s[t * BLOCK : (t + 1) * BLOCK, cols] = jnp.where(seg_k == seg_q[h], 0.0, -1e30)

            def pair(p, carry):
                cols = pl.ds(pl.multiple_of(p * 128, 128), 128)
                q = q_s[rows, cols]
                d_out = d_att[:, cols]
                minus = -(d_out.astype(F32) * att[:, cols].astype(F32))
                scores = dot_t(kc[p, keys, :], jnp.concatenate([q, lse[:, cols]], axis=1))
                d_probs = dot_t(vx[p, keys, :], jnp.concatenate([d_out, minus.astype(BF16)], axis=1))
                parts, d_parts = [], []
                for t in range(n):
                    bias = bias_s[t * BLOCK : (t + 1) * BLOCK, :]
                    for h in range(2):
                        part = slice((2 * t + h) * BLOCK, (2 * t + h + 1) * BLOCK)
                        probs = jnp.exp(scores[part] + bias)
                        parts.append(probs.astype(BF16))
                        d_parts.append((probs * d_probs[part]).astype(BF16))
                d_scores = jnp.concatenate(d_parts, axis=0)
                dk_s[p, keys, :] += dot(d_scores, q)
                dv_s[p, keys, :] += dot(jnp.concatenate(parts, axis=0), d_out)
                d_q = t_dot(d_scores, kc[p, keys, 0:128]) * 0.125
                dqkv_s[rows, pl.ds(pl.multiple_of(p * 384, 128), 128)] = d_q.astype(BF16)
                return carry

            lax.fori_loop(0, PAIRS, pair, 0, unroll=2)

        for n in range(1, 7):
            pl.when(n_keys == n)(functools.partial(back, n))

    @pl.when(step >= 2)
    def _():
        even = lax.broadcasted_iota(jnp.int32, (BLOCK, BLOCK), 1) < 64
        for h in range(2):
            block = 2 * (step - 2) + h
            rows = rows_of(block)
            up = pl.ds(pl.multiple_of(block * 256, 256), 128)
            down = pl.ds(pl.multiple_of(block * 256 + 128, 128), 128)
            for p in range(PAIRS):
                for t, source in enumerate((dk_s, dv_s)):
                    both = jnp.where(even, source[p, up, :], source[p, down, :])
                    spot = p * 384 + 128 + t * 128
                    dqkv_s[rows, spot : spot + 128] = both.astype(BF16)
        dqkv_o[...] = dqkv_s[rows_of(2 * (step - 2), 2), :]

    @pl.when(step == blocks // 2 + 1)
    def _():
        for p in range(PAIRS):
            part = t_dot(normed_s[...], dqkv_s[:, p * 384 : (p + 1) * 384]).astype(BF16)
            for half in range(2):
                piece = part[half * 256 : (half + 1) * 256].reshape(16, 16, 384)

                @pl.when(core == half)
                def _():
                    mine_o[:, p] = piece

                @pl.when(core != half)
                def _():
                    sent_o[:, p] = piece


def entry_kernel(blocks, left, x, right, dbr, gain, ln2, weight, d_qkv,
                 grad_o, left_o, right_o, small_o, w_s, x_s, ln_s, grad_s):
    r = pl.program_id(0)
    tiles = blocks // 2

    @pl.when(r == 0)
    def _():
        for p in range(PAIRS):
            for part in range(3):
                spot = part * 512 + p * 128
                to = p * 384 + part * 128
                w_s[:, to : to + 128] = weight[:, spot : spot + 128]
        for t in range(tiles):
            x_s[t * 256 : (t + 1) * 256, :] = two_blocks(left, x, right, t)
        ln_s[0:2, :] = jnp.zeros((2, D), F32)

    rows = pl.ds(pl.multiple_of(r * 256, 256), 256)
    d_n1 = dot_t(d_qkv[...], w_s[...])
    n1, inverse = normalize(x_s[rows, :].astype(F32))
    e = d_n1 * gain[...]
    mean_e = jnp.mean(e, axis=-1, keepdims=True)
    mean_en = jnp.mean(e * n1, axis=-1, keepdims=True)
    grad_s[rows, :] = dbr[...].astype(F32) + (e - mean_e - n1 * mean_en) * inverse
    ln_s[0:1, :] += jnp.sum(d_n1 * n1, axis=0, keepdims=True)
    ln_s[1:2, :] += jnp.sum(d_n1, axis=0, keepdims=True)

    @pl.when(r == tiles - 1)
    def _():
        inner = (blocks - 2) * BLOCK
        grad_o[...] = grad_s[HALO : HALO + inner, :]
        left_o[...] = grad_s[0:HALO, :].astype(BF16)
        right_o[...] = grad_s[HALO + inner :, :].astype(BF16)
        vectors = [ln_s[0:1, :], ln_s[1:2, :], ln2[0:1, :], ln2[1:2, :]]
        small_o[...] = jnp.concatenate(
            [v[:, c * 128 : (c + 1) * 128] for v in vectors for c in range(4)], axis=0
        )


def join_kernel(share, mine, other, out_m, out_o, result):
    wide = share.shape[-1]
    result[:, :, :, 0:wide] = jnp.broadcast_to(share[...][None, None], (*result.shape[:2], *share.shape))
    value = mine[...].astype(F32) + other[...].astype(F32)
    result[:, :, :, wide : wide + 384] = value.astype(BF16)
    value = out_m[...].astype(F32) + out_o[...].astype(F32)
    result[:, :, :, wide + 384 : wide + 512] = value.astype(BF16)


def join_call(share, mine, other, out_m, out_o):
    at = lambda s: (s, 0, 0, 0)
    block = (8, 4, 16, share.shape[-1] + 512)
    return pl.pallas_call(
        join_kernel,
        grid=(2,),
        in_specs=[pl.BlockSpec(share.shape, lambda s: (0, 0))]
        + [pl.BlockSpec((8, 4, 16, 384), at)] * 2 + [pl.BlockSpec((8, 4, 16, 128), at)] * 2,
        out_specs=pl.BlockSpec(block, at),
        out_shape=shape_of((16, *block[1:]), BF16),
        compiler_params=params(24),
        name="join",
    )(share, mine, other, out_m, out_o)


def whole(shape):
    return pl.BlockSpec(shape, lambda s, scal: (0,) * len(shape))


def shape_of(shape, dtype):
    return jax.ShapeDtypeStruct(shape, dtype)


def params(mib=58):
    return pltpu.CompilerParams(dimension_semantics=("arbitrary",), vmem_limit_bytes=mib * MIB)


def attend_call(scal, left, x, right, seg, gain, shift, weight):
    rows = x.shape[0] + 2 * HALO
    blocks = rows // BLOCK
    at = lambda s, scal: (jnp.maximum(s - 1, 0), 0)
    return pl.pallas_call(
        functools.partial(attend_kernel, blocks),
        grid_spec=pltpu.PrefetchScalarGridSpec(
            num_scalar_prefetch=1,
            grid=(blocks // 2 + 1,),
            in_specs=[
                whole((HALO, D)), whole(x.shape), whole((HALO, D)), whole(seg.shape),
                whole((1, D)), whole((1, D)), whole(weight.shape),
            ],
            out_specs=[
                pl.BlockSpec(memory_space=pl.ANY),
                pl.BlockSpec(memory_space=pl.ANY),
                pl.BlockSpec((2 * BLOCK, D), at),
                pl.BlockSpec((2 * BLOCK, D), at),
            ],
            scratch_shapes=[
                pltpu.VMEM((rows, D), BF16),
                pltpu.VMEM((rows, 3 * D), BF16),
                pltpu.VMEM((PAIRS, blocks * 256, 128), BF16),
                pltpu.VMEM((PAIRS, blocks * 256, 256), BF16),
                pltpu.SemaphoreType.DMA((blocks,)),
            ],
        ),
        out_shape=[
            shape_of((rows, D), BF16),
            shape_of((rows, 3 * D), BF16),
            shape_of((rows, D), BF16),
            shape_of((rows, D), BF16),
        ],
        compiler_params=params(),
        cost_estimate=pl.CostEstimate(flops=8 * 10**9, bytes_accessed=25 * 10**6, transcendentals=4 * 10**6),
        name="attend",
    )(scal, left, x, right, seg, gain, shift, weight)


def feed_call(scal, att, left, x, right, cot_l, cot, cot_r, out_w, up_w, down_w, gain, shift):
    rows = att.shape[0]
    blocks = rows // BLOCK
    half = (16, 4, 16, 1024)
    anywhere = pl.BlockSpec(memory_space=pl.ANY)
    return pl.pallas_call(
        functools.partial(feed_kernel, blocks),
        grid_spec=pltpu.PrefetchScalarGridSpec(
            num_scalar_prefetch=1,
            grid=(FF // 512,),
            in_specs=[
                whole((rows, D)),
                whole((HALO, D)), whole(x.shape), whole((HALO, D)),
                whole((HALO, D)), whole(x.shape), whole((HALO, D)),
                whole((D, D)),
                pl.BlockSpec((D, 512), lambda s, scal: (0, s)),
                pl.BlockSpec((512, D), lambda s, scal: (s, 0)),
                whole((1, D)), whole((1, D)),
            ],
            out_specs=[
                whole((rows, D)), pl.BlockSpec((rows, 512), lambda s, scal: (0, s)), whole((2, D)),
                anywhere, anywhere,
            ],
            scratch_shapes=[
                pltpu.VMEM((rows, D), F32),
                pltpu.VMEM((rows, 128), F32),
                pltpu.VMEM((rows, D), BF16),
                pltpu.VMEM(half, BF16),
                pltpu.VMEM(half, BF16),
                pltpu.SemaphoreType.DMA((3 * (FF // 512),)),
                pltpu.VMEM((rows, D), BF16),
                pltpu.VMEM((FF // 512, rows, 512), BF16),
                pltpu.VMEM((FF // 512, D, 512), BF16),
            ] + [pltpu.VMEM((256, 512), F32)] * 4,
        ),
        out_shape=[
            shape_of((rows, D), BF16),
            shape_of((rows, FF), BF16),
            shape_of((2, D), F32),
            shape_of(half, BF16),
            shape_of(half, BF16),
        ],
        compiler_params=params(),
        cost_estimate=pl.CostEstimate(flops=16 * 10**9, bytes_accessed=25 * 10**6, transcendentals=3 * 10**6),
        name="feed",
    )(scal, att, left, x, right, cot_l, cot, cot_r, out_w, up_w, down_w, gain, shift)


def middle_call(scal, dbr, att, out_w):
    part = (16, 4, 16, 128)
    vmem = pl.BlockSpec(memory_space=pltpu.VMEM)
    return pl.pallas_call(
        middle_kernel,
        in_specs=[pl.BlockSpec(memory_space=pltpu.SMEM)] + [vmem] * 3,
        out_specs=[vmem] * 3,
        out_shape=[shape_of(dbr.shape, BF16), shape_of(part, BF16), shape_of(part, BF16)],
        compiler_params=pltpu.CompilerParams(vmem_limit_bytes=24 * MIB),
        cost_estimate=pl.CostEstimate(flops=2 * 10**9, bytes_accessed=5 * 10**6, transcendentals=0),
        name="middle",
    )(scal, dbr, att, out_w)


def back_call(scal, d_att, att, lse, seg, qkv, normed):
    rows = qkv.shape[0]
    blocks = rows // BLOCK
    half = (16, PAIRS, 16, 384)
    last = blocks // 2 - 1
    lead = lambda s, scal: (jnp.minimum(s, last), 0)
    now = lambda s, scal: (jnp.clip(s - 1, 0, last), 0)
    done = lambda s, scal: (jnp.maximum(s - 2, 0), 0)
    return pl.pallas_call(
        functools.partial(back_kernel, blocks),
        grid_spec=pltpu.PrefetchScalarGridSpec(
            num_scalar_prefetch=1,
            grid=(blocks // 2 + 2,),
            in_specs=[
                pl.BlockSpec((2 * BLOCK, D), now), pl.BlockSpec((2 * BLOCK, D), now), pl.BlockSpec((2 * BLOCK, D), now),
                whole(seg.shape),
                pl.BlockSpec((2 * BLOCK, 3 * D), lead), pl.BlockSpec((2 * BLOCK, D), lead),
            ],
            out_specs=[pl.BlockSpec((2 * BLOCK, 3 * D), done), whole(half), whole(half)],
            scratch_shapes=[
                pltpu.VMEM((rows, D), BF16),
                pltpu.VMEM((PAIRS, blocks * 256, 256), BF16),
                pltpu.VMEM((PAIRS, blocks * 256, 256), BF16),
                pltpu.VMEM((PAIRS, blocks * 256, 128), F32),
                pltpu.VMEM((PAIRS, blocks * 256, 128), F32),
                pltpu.VMEM((6 * BLOCK, 2 * BLOCK), F32),
                pltpu.VMEM((rows, 3 * D), BF16),
                pltpu.VMEM((rows, D), BF16),
            ],
        ),
        out_shape=[shape_of((rows, 3 * D), BF16), shape_of(half, BF16), shape_of(half, BF16)],
        compiler_params=params(),
        cost_estimate=pl.CostEstimate(flops=12 * 10**9, bytes_accessed=20 * 10**6, transcendentals=4 * 10**6),
        name="back",
    )(scal, d_att, att, lse, seg, qkv, normed)


def entry_call(left, x, right, dbr, gain, ln2, weight, d_qkv):
    rows = dbr.shape[0]
    fixed = lambda v: pl.BlockSpec(v.shape, lambda s: (0,) * len(v.shape))
    at = lambda s: (s, 0)
    edge = shape_of((HALO, D), BF16)
    outs = [shape_of(x.shape, F32), edge, edge, shape_of((16, 128), F32)]
    return pl.pallas_call(
        functools.partial(entry_kernel, rows // BLOCK),
        grid=(rows // 256,),
        in_specs=[
            fixed(left), fixed(x), fixed(right), pl.BlockSpec((256, D), at), fixed(gain), fixed(ln2),
            fixed(weight), pl.BlockSpec((256, 3 * D), at),
        ],
        out_specs=[fixed(v) for v in outs],
        out_shape=outs,
        scratch_shapes=[
            pltpu.VMEM((D, 3 * D), BF16), pltpu.VMEM((rows, D), BF16), pltpu.VMEM((8, D), F32),
            pltpu.VMEM((rows, D), F32),
        ],
        compiler_params=params(),
        cost_estimate=pl.CostEstimate(flops=2 * 10**9, bytes_accessed=15 * 10**6, transcendentals=0),
        name="entry",
    )(left, x, right, dbr, gain, ln2, weight, d_qkv)


def other_core(value):
    return lax.ppermute(value, "core", [(0, 1), (1, 0)])


def all_shares(value, groups):
    parts = lax.all_to_all(value, ("rows", "x"), 0, 0, tiled=True)
    return jnp.sum(parts.astype(F32), axis=0).astype(BF16)


def gather_shares(share, groups):
    copies = jnp.broadcast_to(share[None], (groups, *share.shape))
    return lax.all_to_all(copies, ("rows", "x"), 0, 0, tiled=True)


def per_device(
    inputs, qkv_weight, out_weight, up_weight, down_weight, norm1_gain, norm1_shift,
    norm2_gain, norm2_shift, segment_ids, item_steps, gen_rank, out_grad,
):
    x = inputs[0]
    positions = x.shape[0]
    blocks = (positions + 2 * HALO) // BLOCK
    chips = lax.axis_size("rows") * lax.axis_size("x")
    seq_parts = lax.axis_size("x") * lax.axis_size("core")
    seq = ("x", "core")
    to_right = [(i, (i + 1) % seq_parts) for i in range(seq_parts)]
    to_left = [((i + 1) % seq_parts, i) for i in range(seq_parts)]

    place = jnp.stack([lax.axis_index(seq), lax.axis_index("core")]).astype(jnp.int32)
    tie = lax.optimization_barrier
    left = lax.ppermute(x[positions - HALO :], seq, to_right)
    right = lax.ppermute(x[:HALO], seq, to_left)
    scal, seg_rows, cot, send_l, send_r = prepare_call(
        place, segment_ids, item_steps, gen_rank, out_grad[0]
    )
    cot_l = lax.ppermute(send_r, seq, to_right)
    cot_r = lax.ppermute(send_l, seq, to_left)

    gain1, shift1 = norm1_gain.reshape(1, D), norm1_shift.reshape(1, D)
    gain2, shift2 = norm2_gain.reshape(1, D), norm2_shift.reshape(1, D)
    normed1, qkv, att, lse = attend_call(
        scal, left, x, right, seg_rows, gain1, shift1, qkv_weight
    )
    d_branch, act, ln2, mine_a, sent_a = feed_call(
        scal, att, left, x, right, cot_l, cot, cot_r, out_weight, up_weight, down_weight, gain2, shift2
    )
    got_a = other_core(sent_a)
    half_a = (mine_a.astype(F32) + got_a.astype(F32)).astype(BF16)
    d_att, mine_o, sent_o = middle_call(scal, d_branch, att, out_weight)
    d_att, half_a = tie((d_att, half_a))
    share_a = all_shares(half_a.reshape(chips, -1, 1024), chips)
    d_qkv, mine_b, sent_b = back_call(scal, d_att, att, lse, seg_rows, qkv, normed1)
    joined = join_call(share_a, mine_b, other_core(sent_b), mine_o, other_core(sent_o))
    joined, d_branch, att = tie((joined, d_branch, att))
    got = lax.all_to_all(joined.reshape(chips, -1, 1536), ("rows", "x"), 0, 0, tiled=True)
    grad, grad_l, grad_r, small = entry_call(
        left, x, right, d_branch, gain1, ln2, qkv_weight, d_qkv
    )
    small = small + other_core(small)
    out, out_l, out_r = finish_call(att, left, x, right, act, out_weight, down_weight)
    edge_l = jnp.concatenate([out_l, grad_l], axis=0)
    edge_r = jnp.concatenate([out_r, grad_r], axis=0)
    from_r = lax.ppermute(edge_l, seq, to_left)
    from_l = lax.ppermute(edge_r, seq, to_right)
    got, from_l, from_r, small = tie((got, from_l, from_r, small))
    far_a = other_core(got)
    share_b = jnp.sum(got[:, :, 1024:].astype(F32), axis=0).astype(BF16)
    near_b = gather_shares(jnp.concatenate([share_b, small.astype(BF16)], axis=1), chips)
    grads_a = unpack_call(scal, got.reshape(16, 4, 16, 1536))
    grad_down, grad_up = unpack_call(scal, far_a.reshape(16, 4, 16, 1536), grads_a)
    output, input_grad = patch_call(scal, out, grad, seg_rows, from_l, from_r)
    near_b, grad_down, input_grad = tie((near_b, grad_down, input_grad))
    far_b = other_core(near_b)
    *grads_b, v0, v1, v2, v3 = rest_call(scal, near_b.reshape(16, 4, 16, 640))
    grad_out, grad_qkv = rest_call(scal, far_b.reshape(16, 4, 16, 640), grads_b)
    vectors = (v0, v1, v2, v3)
    vectors = [v.reshape(D) for v in vectors]
    return (
        output[None], input_grad[None], grad_qkv, grad_out, grad_up, grad_down,
        vectors[0], vectors[1], vectors[2], vectors[3],
    )


def solution(mesh):
    rows = mesh.devices.shape[0]
    parts = mesh.devices.shape[1]
    split = Mesh(mesh.devices.reshape(rows, parts // 2, 2), ("rows", "x", "core"))
    seq = ("x", "core")
    return jax.shard_map(
        per_device,
        mesh=split,
        in_specs=(
            P("rows", seq, None), P(), P(), P(), P(), P(), P(), P(), P(),
            P("rows", None), P("rows", None), P("rows", seq), P("rows", seq, None),
        ),
        out_specs=(
            P("rows", seq, None), P("rows", seq, None),
            P(), P(), P(), P(), P(), P(), P(), P(),
        ),
        check_vma=False,
    )
```
